32 devices in a mesh: seq: 8 (over z, x), head: 4 (over y, core).
Axes of the slice: x: 2, y: 2, z: 4, core: 2. Of those that a mesh axis runs over, the one named last changes fastest.
Arguments:
- block_in: bfloat16 [4096, 1024], P('seq'), may hold values from -6 to 6
- seq_start: int32 [10], replicated, may hold values from 0 to 4095, as said below
- attn_gain: float32 [1024], replicated, may hold values from 0.5 to 1.5
- q_weight: bfloat16 [1024, 1024], P(None, 'head'), may hold values from -0.1875 to 0.1875
- k_weight: bfloat16 [1024, 2048], P(None, 'head'), may hold values from -0.1875 to 0.1875
- v_weight: bfloat16 [1024, 2048], P(None, 'head'), may hold values from -0.1875 to 0.1875
- conv_q: float32 [4, 1024], P(None, 'head'), may hold values from -3 to 3
- conv_k: float32 [4, 2048], P(None, 'head'), may hold values from -3 to 3
- conv_v: float32 [4, 2048], P(None, 'head'), may hold values from -3 to 3
- beta_weight: bfloat16 [1024, 16], P(None, 'head'), may hold values from -0.1875 to 0.1875
- decay_weight: bfloat16 [1024, 8], P(None, 'head'), may hold values from -0.1875 to 0.1875
- a_log: float32 [8], P('head'), may hold values from -10 to -3.5
- dt_bias: float32 [8], P('head'), may hold values from -2 to 1
- outgate_weight: bfloat16 [1024, 1024], P(None, 'head'), may hold values from -0.1875 to 0.1875
- o_gain: float32 [128], replicated, may hold values from 0.5 to 1.5
- out_weight: bfloat16 [1024, 1024], P('head'), may hold values from -0.3125 to 0.3125
- mlp_gain: float32 [1024], replicated, may hold values from 0.5 to 1.5
- gate_weight: bfloat16 [1024, 2816], P(None, 'head'), may hold values from -0.1875 to 0.1875
- up_weight: bfloat16 [1024, 2816], P(None, 'head'), may hold values from -0.1875 to 0.1875
- down_weight: bfloat16 [2816, 1024], P('head'), may hold values from -0.1875 to 0.1875
- out_grad: bfloat16 [4096, 1024], P('seq'), may hold values from -6 to 6
Outputs:
- output: bfloat16 [4096, 1024], P('seq')
- grad_input: bfloat16 [4096, 1024], P('seq')
- grad_attn_gain: float32 [1024], replicated
- grad_q_weight: float32 [1024, 1024], P(None, 'head')
- grad_k_weight: float32 [1024, 2048], P(None, 'head')
- grad_v_weight: float32 [1024, 2048], P(None, 'head')
- grad_conv_q: float32 [4, 1024], P(None, 'head')
- grad_conv_k: float32 [4, 2048], P(None, 'head')
- grad_conv_v: float32 [4, 2048], P(None, 'head')
- grad_beta_weight: float32 [1024, 16], P(None, 'head')
- grad_decay_weight: float32 [1024, 8], P(None, 'head')
- grad_a_log: float32 [8], P('head')
- grad_dt_bias: float32 [8], P('head')
- grad_outgate_weight: float32 [1024, 1024], P(None, 'head')
- grad_o_gain: float32 [128], replicated
- grad_out_weight: float32 [1024, 1024], P('head')
- grad_mlp_gain: float32 [1024], replicated
- grad_gate_weight: float32 [1024, 2816], P(None, 'head')
- grad_up_weight: float32 [1024, 2816], P(None, 'head')
- grad_down_weight: float32 [2816, 1024], P('head')
The draws below stay inside these ranges and needn't reach their ends.
Inputs may be any that keep to these rules, and one draw needn't show every extreme that they name: seq_start holds the first token of each packed sequence in increasing order, the first being 0; two sequences have about 4096 // 4 tokens and eight about 4096 // 16, in an order drawn from the seed, each boundary moved by fewer than 64 tokens; every entry after the first is odd.
All inputs are finite; a program needn't handle non-finite values.
Results may differ from the reference program's by a relative error of at most 0.018.
The reference program's roundings to bfloat16 on the way count: a program that leaves them out, or rounds other values in their place, can miss the bound.
Values may be sent and summed in bfloat16 or wider, within the bound.
No kernel may reach another device: no remote copies, remote signals or barrier semaphores. Data moves between devices by JAX's collectives and lax.ppermute only.
A program may use at most 192 MiB of HBM per device.

```python
import jax
import jax.numpy as jnp
from jax import lax

D = 1024
HEADS = 8
HEAD_DIM = 128
FF = 2816
NH = 2
CONV = 4
GROUP = 64
NSEQ = 10
TOKENS = 4096
KDIM = 1024


def draw_seq_start(key, part):
    key = jax.random.fold_in(key, 11)
    order_key, jitter_key = jax.random.split(key)
    order = jax.random.permutation(order_key, NSEQ)
    lengths = jnp.where(order < 2, TOKENS // 4, TOKENS // 16).astype(jnp.int32)
    bounds = jnp.cumsum(lengths)[:NSEQ - 1]
    spread = TOKENS // 64
    jitter = 2 * jax.random.randint(jitter_key, (NSEQ - 1,), -(spread // 2), spread // 2) + 1
    starts = jnp.concatenate([jnp.zeros((1,), jnp.int32), (bounds + jitter).astype(jnp.int32)])
    return starts.astype(jnp.int32)


def levels(rng, extent, pieces, smallest, largest):
    loudness, own = 1.0, jax.random.fold_in(rng, 6)
    for position, parts in pieces:
        steps = jnp.exp(jax.random.uniform(jax.random.fold_in(own, position), (parts,), jnp.float32, smallest / len(pieces), largest / len(pieces)))
        loudness = loudness * jnp.repeat(steps, extent[position] // parts).reshape([-1 if axis == position else 1 for axis in range(len(extent))])
    return loudness


def scatter_about(key, dims, scale, limit, pieces=(), held_as=jnp.bfloat16):
    values = jax.random.normal(key, dims, jnp.float32) * scale
    if len(pieces) > 0:
        values = levels(key, dims, pieces, -0.22, 0.18) * values
    return jnp.clip(values, min=-limit, max=limit).astype(held_as)


def setup_inputs(seed: int = 0) -> dict:
    key_list = jax.random.split(jax.random.key(seed), 22)
    block_in = scatter_about(key_list[0], (TOKENS, D), 1.0, 6.0, ((0, 8),))
    seq_start = draw_seq_start(jax.random.fold_in(key_list[21], 71), 0)
    attn_gain = jnp.clip(1.0 + 0.1 * jax.random.normal(key_list[2], (D,), jnp.float32), 0.5, 1.5)
    q_weight = scatter_about(key_list[3], (D, KDIM), D ** -0.5, 0.1875, ((1, 4),))
    k_weight = scatter_about(key_list[4], (D, NH * KDIM), D ** -0.5, 0.1875, ((1, 4),))
    v_weight = scatter_about(key_list[5], (D, NH * KDIM), D ** -0.5, 0.1875, ((1, 4),))
    conv_q = scatter_about(key_list[6], (CONV, KDIM), 0.5, 3.0, ((1, 4),), jnp.float32)
    conv_k = scatter_about(key_list[7], (CONV, NH * KDIM), 0.5, 3.0, ((1, 4),), jnp.float32)
    conv_v = scatter_about(key_list[8], (CONV, NH * KDIM), 0.5, 3.0, ((1, 4),), jnp.float32)
    beta_weight = scatter_about(key_list[9], (D, HEADS * NH), D ** -0.5, 0.1875, ((1, 4),))
    decay_weight = scatter_about(key_list[10], (D, HEADS), D ** -0.5, 0.1875, ((1, 4),))
    a_log = jnp.clip(-10.0 + 6.5 * jax.random.uniform(key_list[11], (HEADS,), jnp.float32) ** levels(key_list[11], (HEADS,), ((0, 4),), -0.2, 0.2), -10.0, -3.5)
    dt_bias = jnp.clip(-2.0 + 3.0 * jax.random.uniform(key_list[12], (HEADS,), jnp.float32) ** levels(key_list[12], (HEADS,), ((0, 4),), -0.2, 0.2), -2.0, 1.0)
    outgate_weight = scatter_about(key_list[13], (D, KDIM), D ** -0.5, 0.1875, ((1, 4),))
    o_gain = jnp.clip(1.0 + 0.1 * jax.random.normal(key_list[14], (HEAD_DIM,), jnp.float32), 0.5, 1.5)
    out_weight = scatter_about(key_list[15], (KDIM, D), (KDIM // 3) ** -0.5, 0.3125, ((0, 4),))
    mlp_gain = jnp.clip(1.0 + 0.1 * jax.random.normal(key_list[16], (D,), jnp.float32), 0.5, 1.5)
    gate_weight = scatter_about(key_list[17], (D, FF), D ** -0.5, 0.1875, ((1, 4),))
    up_weight = scatter_about(key_list[18], (D, FF), D ** -0.5, 0.1875, ((1, 4),))
    down_weight = scatter_about(key_list[19], (FF, D), (FF // 3) ** -0.5, 0.1875, ((0, 4),))
    out_grad = scatter_about(key_list[20], (TOKENS, D), 1.0, 6.0, ((0, 8),))
    return {"block_in": block_in, "seq_start": seq_start, "attn_gain": attn_gain, "q_weight": q_weight, "k_weight": k_weight, "v_weight": v_weight, "conv_q": conv_q, "conv_k": conv_k, "conv_v": conv_v, "beta_weight": beta_weight, "decay_weight": decay_weight, "a_log": a_log, "dt_bias": dt_bias, "outgate_weight": outgate_weight, "o_gain": o_gain, "out_weight": out_weight, "mlp_gain": mlp_gain, "gate_weight": gate_weight, "up_weight": up_weight, "down_weight": down_weight, "out_grad": out_grad}


HIGH_ACCURACY = lax.Precision.HIGHEST
EPSILON = 1e-06

@jax.custom_vjp
def low(v):
    return lax.optimization_barrier(v.astype(jnp.bfloat16)).astype(jnp.float32)

@jax.custom_vjp
def low_back(v):
    return v

def low_keep(v):
    return (low(v), None)

def low_pass(kept, grad):
    return (grad,)

def back_keep(v):
    return (v, None)

def back_low(kept, grad):
    return (low(grad),)
low.defvjp(low_keep, low_pass)
low_back.defvjp(back_keep, back_low)

def matmul_high(left, right):
    return jnp.matmul(left, right, precision=HIGH_ACCURACY)

def rms_norm(values, gain):
    return values * lax.rsqrt(lax.optimization_barrier(jnp.mean(values * values, axis=-1, keepdims=True)) + EPSILON) * gain

def unit_rows(values):
    return values * lax.rsqrt(lax.optimization_barrier(jnp.sum(values * values, axis=-1, keepdims=True)) + EPSILON)

def short_conv(projected, kernel, documents):
    count = projected.shape[0]
    width = kernel.shape[0]
    total = jnp.zeros(projected.shape, jnp.float32)
    for j in range(width):
        lag = width - 1 - j
        moved = jnp.concatenate([jnp.zeros((lag, projected.shape[1]), jnp.float32), projected[:count - lag]], 0)
        moved_docs = jnp.concatenate([jnp.full((lag,), -1, jnp.int32), documents[:count - lag]], 0)
        total = total + kernel[j] * moved * (moved_docs == documents).astype(jnp.float32)[:, None]
    return jax.nn.silu(total)

def delta_product(queries, keys, values, betas, logdec, resets):
    count = queries.shape[0]
    keep = jnp.exp(logdec) * (1.0 - resets[:, None])

    def token(recurrent_state, item):
        query_vector, key_set, value_set, beta_set, factor = item
        recurrent_state = recurrent_state * factor[:, None, None]
        for s in range(NH):
            single_key_row = key_set[:, s]
            initial_estimate = jnp.einsum('jq,jqy->jy', single_key_row, recurrent_state, precision=HIGH_ACCURACY)
            recurrent_state = recurrent_state + beta_set[:, s][:, None, None] * single_key_row[:, :, None] * (value_set[:, s] - initial_estimate)[:, None, :]
        return (recurrent_state, jnp.einsum('jq,jqy->jy', query_vector, recurrent_state, precision=HIGH_ACCURACY))

    @jax.checkpoint
    def block(recurrent_state, items):
        return lax.scan(token, recurrent_state, items)
    blocked = tuple((a.reshape((count // GROUP, GROUP) + a.shape[1:]) for a in (queries, keys, values, betas, keep)))
    initial = jnp.zeros((HEADS, HEAD_DIM, HEAD_DIM), jnp.float32)
    _, outputs = lax.scan(block, initial, blocked)
    return outputs.reshape(count, HEADS, HEAD_DIM)

def reference(block_in, seq_start, attn_gain, q_weight, k_weight, v_weight, conv_q, conv_k, conv_v, beta_weight, decay_weight, a_log, dt_bias, outgate_weight, o_gain, out_weight, mlp_gain, gate_weight, up_weight, down_weight, out_grad):
    count = block_in.shape[0]
    positions = jnp.arange(count, dtype=jnp.int32)
    documents = lax.optimization_barrier(jnp.sum((seq_start[None, :] <= positions[:, None]).astype(jnp.int32), axis=1)) - 1
    resets = jnp.any(seq_start[None, :] == positions[:, None], axis=1).astype(jnp.float32)

    def forward(x_in, attn_gain, q_weight, k_weight, v_weight, conv_q, conv_k, conv_v, beta_weight, decay_weight, a_log, dt_bias, outgate_weight, o_gain, out_weight, mlp_gain, gate_weight, up_weight, down_weight):
        normed = low(rms_norm(x_in, attn_gain))
        proj_q = low(low_back(matmul_high(normed, q_weight)))
        proj_k = low(low_back(matmul_high(normed, k_weight)))
        proj_v = low(low_back(matmul_high(normed, v_weight)))
        act_q = short_conv(proj_q, conv_q, documents).reshape(count, HEADS, HEAD_DIM)
        act_k = short_conv(proj_k, conv_k, documents).reshape(count, HEADS, NH, HEAD_DIM)
        act_v = short_conv(proj_v, conv_v, documents).reshape(count, HEADS, NH, HEAD_DIM)
        queries = low(unit_rows(act_q) * HEAD_DIM ** (-0.5))
        keys = low(unit_rows(act_k))
        values = low(act_v)
        betas = jax.nn.sigmoid(low_back(matmul_high(normed, beta_weight))).reshape(count, HEADS, NH)
        logdec = -jnp.exp(a_log) * jax.nn.softplus(low_back(matmul_high(normed, decay_weight)) + dt_bias)
        outgate = low_back(matmul_high(normed, outgate_weight)).reshape(count, HEADS, HEAD_DIM)
        mixed = delta_product(queries, keys, values, betas, logdec, resets)
        gated = rms_norm(mixed, o_gain) * jax.nn.silu(outgate)
        branch = low(gated.reshape(count, HEADS * HEAD_DIM))
        hidden = x_in + low_back(matmul_high(branch, out_weight))
        normed_mlp = low(rms_norm(hidden, mlp_gain))
        gate = low_back(matmul_high(normed_mlp, gate_weight))
        up = low_back(matmul_high(normed_mlp, up_weight))
        inner = low(jax.nn.silu(gate) * up)
        return hidden + low_back(matmul_high(inner, down_weight))
    primals = (block_in, attn_gain, q_weight, k_weight, v_weight, conv_q, conv_k, conv_v, beta_weight, decay_weight, a_log, dt_bias, outgate_weight, o_gain, out_weight, mlp_gain, gate_weight, up_weight, down_weight)
    primals = tuple((a.astype(jnp.float32) for a in primals))
    result, pull = jax.vjp(forward, *primals)
    gradients = pull(out_grad.astype(jnp.float32))
    return (result.astype(jnp.bfloat16), gradients[0].astype(jnp.bfloat16), gradients[1], gradients[2], gradients[3], gradients[4], gradients[5], gradients[6], gradients[7], gradients[8], gradients[9], gradients[10], gradients[11], gradients[12], gradients[13], gradients[14], gradients[15], gradients[16], gradients[17], gradients[18])
```

```python
import functools
import jax
import jax.numpy as jnp
from jax import lax
from jax.experimental import pallas as pl
from jax.experimental.pallas import tpu as pltpu
from jax.sharding import PartitionSpec as P

NH = 2
GROUP = 64
LANES = 128
EPSILON = 1e-06
BF = jnp.bfloat16
F32 = jnp.float32
VMEM = pltpu.VMEM
VMEM_LIMIT = 60 * 1024 * 1024


def mm(left, right):
    return jnp.dot(left.astype(BF), right.astype(BF), preferred_element_type=F32)


def mm_nt(left, right):
    return lax.dot_general(
        left.astype(BF), right.astype(BF), (((1,), (1,)), ((), ())), preferred_element_type=F32
    )


def mm_tn(left, right):
    return lax.dot_general(
        left.astype(BF), right.astype(BF), (((0,), (0,)), ((), ())), preferred_element_type=F32
    )


def mm_exact(left, right):
    return jnp.dot(left, right, preferred_element_type=F32, precision=lax.Precision.HIGHEST)


def sigmoid(values):
    return 1.0 / (1.0 + jnp.exp(-values))


def softplus(values):
    return jnp.maximum(values, 0.0) + jnp.log1p(jnp.exp(-jnp.abs(values)))


def documents_at(starts, positions):
    total = jnp.zeros(positions.shape, jnp.int32)
    for k in range(starts.shape[0]):
        total = total + (starts[k] <= positions).astype(jnp.int32)
    return total


def sub_order(index):
    return NH * (index % GROUP) + index // GROUP


def order_pair():
    rows = sub_order(lax.broadcasted_iota(jnp.int32, (LANES, LANES), 0))
    cols = sub_order(lax.broadcasted_iota(jnp.int32, (LANES, LANES), 1))
    return rows, cols


def gate_columns(small, log_rate, bias, heads):
    lane = lax.broadcasted_iota(jnp.int32, (1, LANES), 1)
    rate = jnp.zeros((1, LANES), F32)
    shift = jnp.zeros((1, LANES), F32)
    for h in range(heads):
        at = lane == NH * heads + h
        rate = jnp.where(at, -jnp.exp(jnp.full((1, LANES), log_rate[h], F32)), rate)
        shift = jnp.where(at, bias[h], shift)
    return sigmoid(small), rate * softplus(small + shift), small + shift, rate


def chunk_decays(rows, cols_ref, row_ref, doc_ref, c, h, heads, doc_before):
    cum_col = cols_ref[rows, NH * heads + h : NH * heads + h + 1]
    doc_col = doc_ref[rows, 0:1]
    packed = row_ref[c]
    cum_row = packed[NH * heads + h : NH * heads + h + 1, :]
    doc_row = packed[NH * heads + heads : NH * heads + heads + 1, :]
    token_row = lax.broadcasted_iota(jnp.int32, (GROUP, LANES), 1) % GROUP
    token_col = lax.broadcasted_iota(jnp.int32, (GROUP, LANES), 0)
    seen = (token_col >= token_row) & (doc_col == doc_row)
    pair = jnp.where(seen, jnp.exp(jnp.where(seen, cum_col - cum_row, 0.0)), 0.0)
    start = jnp.where(doc_col == doc_before, jnp.exp(cum_col), 0.0)
    cum_last = cum_col[GROUP - 1 :, :]
    doc_last = doc_col[GROUP - 1 :, :]
    to_end = jnp.where(doc_col == doc_last, jnp.exp(cum_last - cum_col), 0.0)
    return pair, start, to_end


def two(array):
    return jnp.concatenate([array, array], axis=0)


def beta_pair(rows, cols_ref, row_ref, c, h):
    lane = lax.broadcasted_iota(jnp.int32, (1, LANES), 1)
    packed = row_ref[c]
    row = jnp.where(lane < GROUP, packed[NH * h : NH * h + 1, :], packed[NH * h + 1 : NH * h + 2, :])
    col = jnp.concatenate(
        [cols_ref[rows, NH * h : NH * h + 1], cols_ref[rows, NH * h + 1 : NH * h + 2]], axis=0
    )
    return row, col


def prep_kernel(
    heads, starts, log_rate, bias, proj, halo, conv_q, conv_k, conv_v, small,
    out_aug, state_aug, wy_k, wy_v, inverse, step_p, query_map, keys, queries, conv_total, cols, doc, row,
    final_state, final_map,
    ext, vals, score_map, step_b, masks,
):
    tokens = proj.shape[0]
    chunks = tokens // GROUP
    first = lax.axis_index("seq") * tokens
    lead = 8
    lower_r = lax.broadcasted_iota(jnp.int32, (LANES, LANES), 0)
    lower_c = lax.broadcasted_iota(jnp.int32, (LANES, LANES), 1)
    lower = ((lower_r >= lower_c) & (lower_r // GROUP == lower_c // GROUP)).astype(F32)
    lane = lax.broadcasted_iota(jnp.int32, (LANES, LANES), 1)
    per = LANES // GROUP
    for block in range(tokens // LANES):
        at = pl.ds(block * LANES, LANES)
        betas, logdec, _, _ = gate_columns(small[at, :], log_rate, bias, heads)
        cum = mm_exact(lower, logdec)
        where = lax.broadcasted_iota(jnp.int32, (LANES, LANES), 0) + (first + block * LANES)
        document = documents_at(starts, where).astype(F32)
        packed = jnp.where(lane < NH * heads, betas, jnp.where(lane < NH * heads + heads, cum, document))
        cols[at, :] = packed
        doc[at, :] = document
        turned = packed.T
        for part in range(per):
            piece = turned[0:8, part * GROUP : (part + 1) * GROUP]
            row[block * per + part] = jnp.concatenate([piece] * NH, axis=1)
    order_r, order_c = order_pair()
    level = 0
    width = 1
    while width < LANES:
        inside = (order_r // (2 * width) == order_c // (2 * width)) & (order_r // width > order_c // width)
        masks[level] = inside.astype(F32)
        level += 1
        width *= 2
    ext[0:lead, :] = halo[16 - lead : 16, :].astype(F32)
    ext[lead:, :] = proj[...].astype(F32)
    width_q = heads * LANES
    width_k = NH * heads * LANES
    taps = conv_q.shape[0]

    def conv_chunk(c, _):
        base = pl.multiple_of(c * GROUP, GROUP)
        rows = pl.ds(base, GROUP)
        position = lax.broadcasted_iota(jnp.int32, (GROUP, LANES), 0) + (first + base)
        document = doc[rows, :]
        kept = [
            (documents_at(starts, position - lag).astype(F32) == document).astype(F32) for lag in range(1, taps)
        ]
        for group in range((width_q + 2 * width_k) // LANES):
            at = slice(group * LANES, (group + 1) * LANES)
            if group * LANES < width_q:
                kernel, shift = conv_q, 0
            elif group * LANES < width_q + width_k:
                kernel, shift = conv_k, width_q
            else:
                kernel, shift = conv_v, width_q + width_k
            cut = slice(at.start - shift, at.stop - shift)
            window = ext[pl.ds(base, GROUP + lead), at]
            total = kernel[taps - 1 : taps, cut] * window[lead:, :]
            for lag in range(1, taps):
                total += kernel[taps - 1 - lag : taps - lag, cut] * window[lead - lag : lead - lag + GROUP, :] * kept[lag - 1]
            conv_total[rows, at] = total
            active = total * sigmoid(total)
            if group * LANES < width_q:
                unit = active * lax.rsqrt(jnp.sum(active * active, axis=1, keepdims=True) + EPSILON)
                queries[group, c] = (unit * LANES ** (-0.5)).astype(BF)
            elif group * LANES < width_q + width_k:
                piece = group - width_q // LANES
                unit = active * lax.rsqrt(jnp.sum(active * active, axis=1, keepdims=True) + EPSILON)
                keys[piece // NH, c, (piece % NH) * GROUP : (piece % NH + 1) * GROUP] = unit.astype(BF)
            else:
                piece = group - (width_q + width_k) // LANES
                vals[piece // NH, c, (piece % NH) * GROUP : (piece % NH + 1) * GROUP] = active.astype(BF)
        return 0

    lax.fori_loop(0, chunks, conv_chunk, 0)

    strict = order_r > order_c
    eye = (lower_r == lower_c).astype(F32)
    together = 2

    def part_chunks(step, _):
        jobs = []
        for k in range(together):
            c = step * together + k
            rows = pl.ds(pl.multiple_of(c * GROUP, GROUP), GROUP)
            before = documents_at(starts, jnp.full((1, 1), first + c * GROUP - 1, jnp.int32)).astype(F32)
            for h in range(heads):
                pair, start, to_end = chunk_decays(rows, cols, row, doc, c, h, heads, before)
                beta_row, beta_col = beta_pair(rows, cols, row, c, h)
                key = keys[h, c]
                query = queries[h, c]
                grams = mm_nt(jnp.concatenate([key, query], axis=0), key)
                system = jnp.where(strict, grams[:LANES] * two(pair), 0.0) * beta_row
                scores = grams[LANES:] * pair * beta_row
                jobs.append((c, h, start, to_end, beta_col, key, query, system, scores))
        inverses = [eye - job[7] * masks[0] for job in jobs]
        for n in range(1, level):
            halves = [mm(job[7] * masks[n], inv) for job, inv in zip(jobs, inverses)]
            inverses = [inv - mm(inv, half) for inv, half in zip(inverses, halves)]
        for job, inv in zip(jobs, inverses):
            c, h, start, to_end, beta_col, key, query, system, scores = job
            low_inv = inv.astype(BF)
            inverse[h, c] = low_inv
            key_f = key.astype(F32)
            both = mm(low_inv, jnp.concatenate([(two(start) * key_f).astype(BF), vals[h, c]], axis=1)).astype(BF)
            wy_k[h, c] = both[:, :LANES]
            wy_v[h, c] = both[:, LANES:]
            carried = (beta_col * two(to_end) * key_f).astype(BF)
            ahead = mm_tn(carried, both)
            step_p[h, c] = ahead[:, :LANES].astype(BF)
            step_b[h, c] = ahead[:, LANES:]
            scored = mm(scores, both)
            query_map[h, c] = (start * query.astype(F32) - scored[:, :LANES]).astype(BF)
            score_map[h, c] = scored[:, LANES:]
        return 0

    lax.fori_loop(0, chunks // together, part_chunks, 0)

    zero = jnp.zeros((LANES, LANES), F32)

    def advance(c, carry):
        rows = pl.ds(pl.multiple_of(c * GROUP, GROUP), GROUP)
        before = documents_at(starts, jnp.full((1, 1), first + c * GROUP - 1, jnp.int32)).astype(F32)
        new = []
        for h in range(heads):
            state = carry[h]
            low_state = state.astype(BF)
            state_aug[h, c] = low_state
            last = cols[rows, NH * heads + h : NH * heads + h + 1][GROUP - 1 :, :]
            whole = jnp.where(doc[rows, 0:1][GROUP - 1 :, :] == before, jnp.exp(last), 0.0)
            new.append(
                whole * state - mm(step_p[h, c], low_state) + jnp.concatenate([step_b[h, c], zero], axis=1)
            )
            mapped = mm(query_map[h, c], low_state)
            out_aug[h, rows, :] = jnp.concatenate([mapped[:, :LANES] + score_map[h, c], mapped[:, LANES:]], axis=1)
        return tuple(new)

    begin = jnp.concatenate([zero, eye], axis=1)
    end = lax.fori_loop(0, chunks, advance, (begin,) * heads)
    for h in range(heads):
        final_state[h] = end[h][:, :LANES].astype(final_state.dtype)
        final_map[h] = end[h][:, LANES:].astype(final_map.dtype)


def specs(count, space=None):
    return [pl.BlockSpec(memory_space=space or pltpu.VMEM)] * count


def mixer_prep(starts, log_rate, bias, proj, halo, conv_q, conv_k, conv_v, small):
    tokens, width = proj.shape
    heads = log_rate.shape[0]
    chunks = tokens // GROUP
    square = (heads, chunks, LANES, LANES)
    shape = jax.ShapeDtypeStruct
    outs = [
        shape((heads, tokens, 2 * LANES), F32),
        shape((heads, chunks, LANES, 2 * LANES), BF),
        shape(square, BF),
        shape(square, BF),
        shape(square, BF),
        shape(square, BF),
        shape((heads, chunks, GROUP, LANES), BF),
        shape(square, BF),
        shape((heads, chunks, GROUP, LANES), BF),
        shape((tokens, width), F32),
        shape((tokens, LANES), F32),
        shape((tokens, LANES), F32),
        shape((chunks, 8, LANES), F32),
        shape((heads, LANES, LANES), BF),
        shape((heads, LANES, LANES), BF),
    ]
    return pl.pallas_call(
        functools.partial(prep_kernel, heads),
        out_shape=outs,
        in_specs=specs(3, pltpu.SMEM) + specs(6),
        out_specs=specs(len(outs)),
        scratch_shapes=[
            VMEM((tokens + 8, width), F32),
            VMEM(square, BF),
            VMEM((heads, chunks, GROUP, LANES), F32),
            VMEM(square, F32),
            VMEM((8, LANES, LANES), F32),
        ],
        compiler_params=pltpu.CompilerParams(vmem_limit_bytes=VMEM_LIMIT),
        cost_estimate=pl.CostEstimate(flops=4_000_000_000, bytes_accessed=16_000_000, transcendentals=2_000_000),
        name="mixer_prep",
    )(starts, log_rate, bias, proj, halo, conv_q, conv_k, conv_v, small)


def attend_kernel(heads, reach, out_aug, outgate, o_gain, out_weight, *rest):
    before = rest[:reach]
    mixed, branch, partial, state_in = rest[reach:]
    gain = o_gain[...]
    for h in range(heads):
        at = slice(h * LANES, (h + 1) * LANES)
        state = before[reach - 1][0, h].astype(F32)
        for r in range(reach - 2, -1, -1):
            state = mm(before[r][1, h], state) + before[r][0, h].astype(F32)
        state_in[h] = state
        mix = out_aug[h, :, :LANES] + mm(out_aug[h, :, LANES:], state)
        mixed[:, at] = mix
        gate = outgate[:, at]
        normed = mix * lax.rsqrt(jnp.mean(mix * mix, axis=1, keepdims=True) + EPSILON)
        branch[:, at] = (normed * gain * (gate * sigmoid(gate))).astype(BF)
    partial[...] = mm(branch[...], out_weight[...]).astype(partial.dtype)


def attend(out_aug, outgate, o_gain, out_weight, before, dtype=F32):
    heads, tokens, _ = out_aug.shape
    shape = jax.ShapeDtypeStruct
    reach = len(before)
    outs = [
        shape((tokens, heads * LANES), F32),
        shape((tokens, heads * LANES), BF),
        shape((tokens, out_weight.shape[1]), dtype),
        shape((heads, LANES, LANES), F32),
    ]
    return pl.pallas_call(
        functools.partial(attend_kernel, heads, reach),
        out_shape=outs,
        in_specs=specs(4 + reach),
        out_specs=specs(len(outs)),
        compiler_params=pltpu.CompilerParams(vmem_limit_bytes=VMEM_LIMIT),
        name="attend",
    )(out_aug, outgate, o_gain.reshape(1, -1), out_weight, *before)


def attend_back_kernel(heads, grad, out_weight, mixed, outgate, o_gain, out_aug, d_mixed, d_outgate, d_gain, carry):
    gain = o_gain[...]
    d_branch = mm_nt(grad[...], out_weight[...])
    gain_sum = jnp.zeros((1, LANES), F32)
    for h in range(heads):
        at = slice(h * LANES, (h + 1) * LANES)
        mix = mixed[:, at]
        gate = outgate[:, at]
        grad_h = d_branch[:, at]
        scale = lax.rsqrt(jnp.mean(mix * mix, axis=1, keepdims=True) + EPSILON)
        normed = mix * scale
        sg = sigmoid(gate)
        through = grad_h * (gate * sg)
        gain_sum += jnp.sum(through * normed, axis=0, keepdims=True)
        d_normed = through * gain
        d_mix = scale * (d_normed - normed * jnp.mean(d_normed * normed, axis=1, keepdims=True))
        d_mixed[:, at] = d_mix.astype(BF)
        d_outgate[:, at] = (grad_h * normed * gain * (sg * (1.0 + gate * (1.0 - sg)))).astype(BF)
        carry[h] = mm_tn(out_aug[h, :, LANES:], d_mix).astype(carry.dtype)
    d_gain[...] = gain_sum


def attend_back(grad, out_weight, mixed, outgate, o_gain, out_aug):
    heads, tokens, _ = out_aug.shape
    shape = jax.ShapeDtypeStruct
    outs = [
        shape((tokens, heads * LANES), BF),
        shape((tokens, heads * LANES), BF),
        shape((1, LANES), F32),
        shape((heads, LANES, LANES), BF),
    ]
    return pl.pallas_call(
        functools.partial(attend_back_kernel, heads),
        out_shape=outs,
        in_specs=specs(6),
        out_specs=specs(len(outs)),
        compiler_params=pltpu.CompilerParams(vmem_limit_bytes=VMEM_LIMIT),
        name="attend_back",
    )(grad, out_weight, mixed, outgate, o_gain.reshape(1, -1), out_aug)


def back_kernel(
    heads, reach, starts, log_rate, bias, proj, halo, conv_q, conv_k, conv_v, small,
    state_aug, wy_k, wy_v, inverse, step_p, query_map, keys, queries, conv_total, cols, doc, row,
    state_in, d_mixed, *rest,
):
    after = rest[:reach]
    later = rest[reach : 2 * reach - 1]
    (
        d_proj, tail, lead_rows, d_small, d_taps, d_scalars,
        ext, state_grads, d_query, d_key, d_value, col_grads, row_grads, d_total,
    ) = rest[2 * reach - 1 :]
    tokens = proj.shape[0]
    chunks = tokens // GROUP
    first = lax.axis_index("seq") * tokens
    lead = 8
    lane = lax.broadcasted_iota(jnp.int32, (GROUP, LANES), 1)

    def document_before(c):
        return documents_at(starts, jnp.full((1, 1), first + c * GROUP - 1, jnp.int32)).astype(F32)

    def whole_decay(c, h):
        at = pl.ds(pl.multiple_of(c * GROUP, GROUP) + GROUP - 8, 8)
        last = cols[at, NH * heads + h : NH * heads + h + 1][7:8, :]
        return jnp.where(doc[at, 0:1][7:8, :] == document_before(c), jnp.exp(last), 0.0)

    begin = []
    for h in range(heads):
        state = after[reach - 1][h].astype(F32)
        for r in range(reach - 2, -1, -1):
            state = mm_tn(later[r][h], state) + after[r][h].astype(F32)
        begin.append(state)

    def retreat(step, carry):
        c = chunks - 1 - step
        rows = pl.ds(pl.multiple_of(c * GROUP, GROUP), GROUP)
        new = []
        for h in range(heads):
            low_state = carry[h].astype(BF)
            state_grads[h, c] = low_state
            new.append(
                whole_decay(c, h) * carry[h]
                - mm_tn(step_p[h, c], low_state)
                + mm_tn(query_map[h, c], d_mixed[rows, h * LANES : (h + 1) * LANES])
            )
        return tuple(new)

    lax.fori_loop(0, chunks, retreat, tuple(begin))

    order_r, order_c = order_pair()
    strict = order_r > order_c
    together = 2
    last_token = lax.broadcasted_iota(jnp.int32, (GROUP, 1), 0) == GROUP - 1

    def chunk_back(step, _):
        for k in range(together):
            c = step * together + k
            rows = pl.ds(pl.multiple_of(c * GROUP, GROUP), GROUP)
            before = document_before(c)
            col_acc = jnp.zeros((GROUP, LANES), F32)
            row_acc = []
            row_beta = []
            for h in range(heads):
                pair, start, to_end = chunk_decays(rows, cols, row, doc, c, h, heads, before)
                beta_row, beta_col = beta_pair(rows, cols, row, c, h)
                key = keys[h, c]
                query = queries[h, c]
                key_f = key.astype(F32)
                query_f = query.astype(F32)
                d_out = d_mixed[rows, h * LANES : (h + 1) * LANES]
                d_state = state_grads[h, c]
                both = state_aug[h, c]
                state = both[:, :LANES].astype(F32) + mm(both[:, LANES:], state_in[h])
                low_state = state.astype(BF)
                fresh = wy_v[h, c].astype(F32) - mm(wy_k[h, c], low_state)
                grams = mm_nt(jnp.concatenate([key, query], axis=0), key)
                pair2 = two(pair)
                system = jnp.where(strict, grams[:LANES] * pair2, 0.0)
                scores = grams[LANES:] * pair
                key_end = two(to_end) * key_f
                key_start = two(start) * key_f
                d_wide = mm_tn(scores, d_out) + mm(key_end, d_state)
                solved = mm_tn(inverse[h, c], beta_col * d_wide)
                d_value[h, c] = solved
                low_fresh = fresh.astype(BF)
                crossed = mm_nt(
                    jnp.concatenate([solved.astype(BF), d_out], axis=0),
                    jnp.concatenate([low_fresh, low_state], axis=0),
                )
                pairs = jnp.where(strict, crossed[:LANES, :LANES], 0.0)
                solved_state = crossed[:LANES, LANES:]
                out_state = crossed[LANES:, LANES:]
                fresh_grad = mm_nt(beta_col * fresh, d_state)
                system_pairs = system * pairs
                decayed = -(system_pairs * beta_row)
                gram_grad = -(pairs * pair2 * beta_row)
                score_grad = crossed[LANES:, :LANES] * beta_row
                query_key = score_grad * pair
                score_decay = score_grad * scores
                stacked = jnp.concatenate([gram_grad, query_key], axis=0).astype(BF)
                direct = mm(stacked, key)
                turned = mm_tn(stacked, jnp.concatenate([key, query], axis=0))
                d_key[h, c] = direct[:LANES] + turned - two(start) * solved_state + two(to_end) * fresh_grad
                d_query[h, c] = direct[LANES:] + start * out_state
                ending = key_end * fresh_grad
                parts = decayed - key_start * solved_state - ending
                parts = parts[:GROUP] + parts[GROUP:] + score_decay + (start * query_f) * out_state
                at_end = jnp.sum(ending, keepdims=True) + whole_decay(c, h) * jnp.sum(
                    state * d_state.astype(F32), keepdims=True
                )
                decay_col = jnp.sum(parts, axis=1, keepdims=True) + jnp.where(last_token, at_end, 0.0)
                beta_sum = jnp.sum(d_wide * fresh, axis=1, keepdims=True)
                col_acc = jnp.where(lane == NH * heads + h, decay_col, col_acc)
                for s in range(NH):
                    col_acc = jnp.where(lane == NH * h + s, beta_sum[s * GROUP : (s + 1) * GROUP], col_acc)
                beta_row_sum = jnp.sum(system_pairs, axis=0, keepdims=True)
                row_beta.append(-beta_row_sum)
                row_acc.append(beta_row * beta_row_sum - jnp.sum(score_decay, axis=0, keepdims=True))
            col_grads[rows, :] = col_acc
            row_grads[c] = jnp.concatenate(
                row_acc + row_beta + [jnp.zeros((8 - 2 * heads, LANES), F32)], axis=0
            )
        return 0

    lax.fori_loop(0, chunks // together, chunk_back, 0)

    lower_r = lax.broadcasted_iota(jnp.int32, (LANES, LANES), 0)
    lower_c = lax.broadcasted_iota(jnp.int32, (LANES, LANES), 1)
    upper = ((lower_r <= lower_c) & (lower_r // GROUP == lower_c // GROUP)).astype(F32)
    per = LANES // GROUP
    scalar_decay = jnp.zeros((1, LANES), F32)
    scalar_rate = jnp.zeros((1, LANES), F32)
    wide = lax.broadcasted_iota(jnp.int32, (LANES, LANES), 1)
    for block in range(tokens // LANES):
        at = pl.ds(block * LANES, LANES)
        pieces = []
        for part in range(per):
            c = block * per + part
            turned = jnp.concatenate([row_grads[c], jnp.zeros((LANES - 8, LANES), F32)], axis=0).T
            piece = jnp.zeros((GROUP, LANES), F32)
            for h in range(heads):
                decay_col = turned[:GROUP, h : h + 1] + turned[GROUP:, h : h + 1]
                piece = jnp.where(lane == NH * heads + h, decay_col, piece)
                for s in range(NH):
                    beta_col = turned[s * GROUP : (s + 1) * GROUP, heads + h : heads + h + 1]
                    piece = jnp.where(lane == NH * h + s, beta_col, piece)
            pieces.append(piece)
        grads = col_grads[at, :] + jnp.concatenate(pieces, axis=0)
        d_logdec = mm_exact(upper, grads)
        betas, logdec, argument, rate = gate_columns(small[at, :], log_rate, bias, heads)
        d_argument = d_logdec * rate * sigmoid(argument)
        scalar_rate += jnp.sum(d_logdec * logdec, axis=0, keepdims=True)
        scalar_decay += jnp.sum(d_argument, axis=0, keepdims=True)
        d_small[at, :] = jnp.where(
            wide < NH * heads,
            grads * betas * (1.0 - betas),
            jnp.where(wide < NH * heads + heads, d_argument, 0.0),
        ).astype(BF)
    d_scalars[...] = jnp.concatenate([scalar_rate, scalar_decay, jnp.zeros((6, LANES), F32)], axis=0)

    ext[0:lead, :] = halo[16 - lead : 16, :].astype(F32)
    ext[lead:, :] = proj[...].astype(F32)
    width_q = heads * LANES
    width_k = NH * heads * LANES
    width = width_q + 2 * width_k
    taps = conv_q.shape[0]
    d_taps[...] = jnp.zeros(d_taps.shape, F32)
    d_total[tokens:, :] = jnp.zeros((8, width), F32)

    def kernel_of(group):
        if group * LANES < width_q:
            return conv_q, slice(group * LANES, (group + 1) * LANES)
        if group * LANES < width_q + width_k:
            return conv_k, slice(group * LANES - width_q, (group + 1) * LANES - width_q)
        return conv_v, slice(group * LANES - width_q - width_k, (group + 1) * LANES - width_q - width_k)

    def active_back(c, _):
        base = pl.multiple_of(c * GROUP, GROUP)
        rows = pl.ds(base, GROUP)
        position = lax.broadcasted_iota(jnp.int32, (GROUP, LANES), 0) + (first + base)
        document = doc[rows, :]
        kept = [
            (documents_at(starts, position - lag).astype(F32) == document).astype(F32) for lag in range(1, taps)
        ]
        for group in range(width // LANES):
            at = slice(group * LANES, (group + 1) * LANES)
            total = conv_total[rows, at]
            sg = sigmoid(total)
            if group * LANES < width_q + width_k:
                active = total * sg
                scale = lax.rsqrt(jnp.sum(active * active, axis=1, keepdims=True) + EPSILON)
                unit = active * scale
                if group * LANES < width_q:
                    grad = d_query[group, c] * LANES ** (-0.5)
                else:
                    piece = group - width_q // LANES
                    grad = d_key[piece // NH, c, (piece % NH) * GROUP : (piece % NH + 1) * GROUP]
                grad = scale * (grad - unit * jnp.sum(unit * grad, axis=1, keepdims=True))
            else:
                piece = group - (width_q + width_k) // LANES
                grad = d_value[piece // NH, c, (piece % NH) * GROUP : (piece % NH + 1) * GROUP]
            grad = grad * (sg * (1.0 + total * (1.0 - sg)))
            d_total[rows, at] = grad
            window = ext[pl.ds(base, GROUP + lead), at]
            sums = []
            for j in range(taps):
                lag = taps - 1 - j
                term = grad * window[lead - lag : lead - lag + GROUP, :]
                if lag > 0:
                    term = term * kept[lag - 1]
                sums.append(jnp.sum(term, axis=0, keepdims=True))
            d_taps[0:taps, at] += jnp.concatenate(sums, axis=0)
        return 0

    lax.fori_loop(0, chunks, active_back, 0)
    lead_rows[...] = d_total[0:8, :]

    def conv_back(c, _):
        base = pl.multiple_of(c * GROUP, GROUP)
        rows = pl.ds(base, GROUP)
        position = lax.broadcasted_iota(jnp.int32, (GROUP, LANES), 0) + (first + base)
        document = doc[rows, :]
        kept = [
            (documents_at(starts, position + lag).astype(F32) == document).astype(F32) for lag in range(1, taps)
        ]
        for group in range(width // LANES):
            at = slice(group * LANES, (group + 1) * LANES)
            kernel, cut = kernel_of(group)
            window = d_total[pl.ds(base, GROUP + lead), at]
            grad = kernel[taps - 1 : taps, cut] * window[:GROUP]
            for lag in range(1, taps):
                grad += kernel[taps - 1 - lag : taps - lag, cut] * kept[lag - 1] * window[lag : lag + GROUP]
            d_proj[rows, at] = grad.astype(BF)
            tail[:, at] = grad[GROUP - 8 :]
        return 0

    lax.fori_loop(0, chunks, conv_back, 0)


def mixer_back(starts, log_rate, bias, proj, halo, conv_q, conv_k, conv_v, small, saved, state_in, d_mixed, after, later):
    tokens, width = proj.shape
    heads = log_rate.shape[0]
    chunks = tokens // GROUP
    reach = len(after)
    square = (heads, chunks, LANES, LANES)
    shape = jax.ShapeDtypeStruct
    outs = [
        shape((tokens, width), BF),
        shape((8, width), F32),
        shape((8, width), F32),
        shape((tokens, LANES), BF),
        shape((8, width), F32),
        shape((8, LANES), F32),
    ]
    operands = [starts, log_rate, bias, proj, halo, conv_q, conv_k, conv_v, small, *saved, state_in, d_mixed, *after, *later]
    return pl.pallas_call(
        functools.partial(back_kernel, heads, reach),
        out_shape=outs,
        in_specs=specs(3, pltpu.SMEM) + specs(len(operands) - 3),
        out_specs=specs(len(outs)),
        scratch_shapes=[
            VMEM((tokens + 8, width), F32),
            VMEM(square, BF),
            VMEM((heads, chunks, GROUP, LANES), F32),
            VMEM(square, F32),
            VMEM(square, F32),
            VMEM((tokens, LANES), F32),
            VMEM((chunks, 8, LANES), F32),
            VMEM((tokens + 8, width), F32),
        ],
        compiler_params=pltpu.CompilerParams(vmem_limit_bytes=VMEM_LIMIT),
        cost_estimate=pl.CostEstimate(flops=8_000_000_000, bytes_accessed=20_000_000, transcendentals=2_000_000),
        name="mixer_back",
    )(*operands)


def shifted(value, axis, steps):
    count = lax.axis_size(axis)
    leading, last = max(0, -steps), min(count, count - steps)
    return lax.ppermute(value, axis, [(source, source + steps) for source in range(leading, last)])


def swapped(value, axis, bit):
    return lax.ppermute(value, axis, [(s, s ^ bit) for s in range(lax.axis_size(axis))])


def head_sum(part):
    count = lax.axis_size("head")
    low = lax.axis_index("head") % 2
    half = part.shape[0] // 2
    keep = lax.dynamic_slice_in_dim(part, low * half, half, 0)
    give = lax.dynamic_slice_in_dim(part, (1 - low) * half, half, 0)
    total = keep.astype(F32) + swapped(give, "head", 1).astype(F32)
    bit = 2
    while bit < count:
        sent = total.astype(BF)
        total = sent.astype(F32) + swapped(sent, "head", bit).astype(F32)
        bit *= 2
    return total


def both_halves(mine):
    low = lax.axis_index("head") % 2
    other = swapped(mine, "head", 1)
    return jnp.concatenate([jnp.where(low == 0, mine, other), jnp.where(low == 0, other, mine)], axis=0)


def dot_plain(left, right):
    return jnp.dot(left, right, preferred_element_type=F32)


def dot_rows(left, right):
    return lax.dot_general(left, right, (((1,), (1,)), ((), ())), preferred_element_type=F32)


def dot_cols(left, right):
    return lax.dot_general(left, right, (((0,), (0,)), ((), ())), preferred_element_type=F32)


def rms_norm(values, gain):
    return values * lax.rsqrt(jnp.mean(values * values, axis=-1, keepdims=True) + EPSILON) * gain


def reach_of(tokens, count):
    whole = tokens * count
    longest = whole // 4 + 2 * (whole // 64 - 1)
    return max(1, min(count - 1, -(-(longest - 1) // tokens)))


def local(
    block_in, seq_start, attn_gain, q_weight, k_weight, v_weight, conv_q, conv_k, conv_v,
    beta_weight, decay_weight, a_log, dt_bias, outgate_weight, o_gain, out_weight,
    mlp_gain, gate_weight, up_weight, down_weight, out_grad,
):
    tokens = block_in.shape[0]
    heads = a_log.shape[0]
    width_q = q_weight.shape[1]
    width_k = k_weight.shape[1]
    width = width_q + 2 * width_k
    betas = beta_weight.shape[1]
    reach = reach_of(tokens, lax.axis_size("seq"))
    x_float = block_in.astype(F32)
    normed_float, attn_norm_back = jax.vjp(rms_norm, x_float, attn_gain)
    normed = normed_float.astype(BF)
    mix_weight = jnp.concatenate([q_weight, k_weight, v_weight], axis=1)
    small_weight = jnp.concatenate(
        [beta_weight, decay_weight, jnp.zeros((beta_weight.shape[0], LANES - betas - heads), BF)], axis=1
    )
    projected = dot_plain(normed, mix_weight).astype(BF)
    small = dot_plain(normed, small_weight)
    outgate = dot_plain(normed, outgate_weight)
    halo = shifted(projected[tokens - 16 :], "seq", 1)
    mixer_args = (seq_start, a_log, dt_bias, projected, halo, conv_q, conv_k, conv_v, small)
    prepared = mixer_prep(*mixer_args)
    out_aug, saved, final_state, final_map = prepared[0], prepared[1:13], prepared[13], prepared[14]
    pair = jnp.stack([final_state, final_map])
    before = [shifted(pair, "seq", r) for r in range(1, reach)] + [shifted(final_state[None], "seq", reach)]
    later = [shifted(final_map, "seq", -r) for r in range(1, reach)]
    mixed, branch, partial, state_in = attend(out_aug, outgate, o_gain, out_weight, before)
    attention_out = both_halves(head_sum(partial))
    hidden = x_float + attention_out
    normed_mlp_float, mlp_norm_back = jax.vjp(rms_norm, hidden, mlp_gain)
    normed_mlp = normed_mlp_float.astype(BF)
    gate = dot_plain(normed_mlp, gate_weight)
    up = dot_plain(normed_mlp, up_weight)

    def swiglu(gate, up):
        return jax.nn.silu(gate) * up

    inner_float, swiglu_back = jax.vjp(swiglu, gate, up)
    inner = inner_float.astype(BF)
    grad_inner = dot_rows(out_grad, down_weight)
    grad_gate, grad_up = swiglu_back(grad_inner)
    grad_gate = grad_gate.astype(BF)
    grad_up = grad_up.astype(BF)
    part_mlp = dot_rows(grad_gate, gate_weight) + dot_rows(grad_up, up_weight)
    grad_normed_mlp = both_halves(head_sum(part_mlp))
    grad_hidden_norm, grad_mlp_gain = mlp_norm_back(grad_normed_mlp)
    grad_hidden = out_grad.astype(F32) + grad_hidden_norm
    attention_gradient = grad_hidden.astype(BF)
    grad_mixed, grad_outgate, grad_o_part, carry = attend_back(
        attention_gradient, out_weight, mixed, outgate, o_gain, out_aug
    )
    after = [shifted(carry, "seq", -r) for r in range(1, reach + 1)]
    feed_out = both_halves(head_sum(dot_plain(inner, down_weight)))
    output = (hidden + feed_out).astype(BF)
    early = lax.psum(
        (
            dot_cols(branch, attention_gradient).astype(BF),
            dot_cols(normed_mlp, grad_gate).astype(BF),
            dot_cols(normed_mlp, grad_up).astype(BF),
            dot_cols(inner, out_grad).astype(BF),
        ),
        "seq",
    )
    grad_proj, tail, lead_rows, grad_small, grad_taps, grad_scalars = mixer_back(
        *mixer_args, saved, state_in, grad_mixed, after, later
    )
    following = jnp.concatenate([jnp.zeros((8, width), F32), shifted(lead_rows, "seq", -1)], axis=0)
    kernel = jnp.concatenate([conv_q, conv_k, conv_v], axis=1)
    taps = kernel.shape[0]
    position = lax.axis_index("seq") * tokens + tokens - 8 + jnp.arange(8, dtype=jnp.int32)
    for lag in range(1, taps):
        kept = documents_at(seq_start, position + lag) == documents_at(seq_start, position)
        tail = tail + kernel[taps - 1 - lag] * following[lag : lag + 8] * kept.astype(F32)[:, None]
    grad_proj = jnp.concatenate([grad_proj[: tokens - 8], tail.astype(BF)], axis=0)
    part_attn = (
        dot_rows(grad_proj, mix_weight) + dot_rows(grad_outgate, outgate_weight) + dot_rows(grad_small, small_weight)
    )
    grad_normed = both_halves(head_sum(part_attn))
    grad_x_norm, grad_attn_gain = attn_norm_back(grad_normed)
    grad_input = (grad_hidden + grad_x_norm).astype(BF)
    grad_mix_w, grad_outgate_w, grad_small_w = lax.psum(
        (
            dot_cols(normed, grad_proj).astype(BF),
            dot_cols(normed, grad_outgate).astype(BF),
            dot_cols(normed, grad_small),
        ),
        "seq",
    )
    grad_attn_gain, grad_mlp_gain, grad_taps, grad_scalars = lax.psum(
        (grad_attn_gain, grad_mlp_gain, grad_taps[:taps], grad_scalars), "seq"
    )
    grad_o_gain = lax.psum(grad_o_part, ("seq", "head"))[0]
    grad_out_w, grad_gate_w, grad_up_w, grad_down_w = (a.astype(F32) for a in early)
    grad_mix_w = grad_mix_w.astype(F32)
    q_cols, k_cols, v_cols = slice(0, width_q), slice(width_q, width_q + width_k), slice(width_q + width_k, width)
    return (
        output, grad_input, grad_attn_gain,
        grad_mix_w[:, q_cols], grad_mix_w[:, k_cols], grad_mix_w[:, v_cols],
        grad_taps[:, q_cols], grad_taps[:, k_cols], grad_taps[:, v_cols],
        grad_small_w[:, :betas], grad_small_w[:, betas : betas + heads],
        grad_scalars[0, betas : betas + heads], grad_scalars[1, betas : betas + heads],
        grad_outgate_w.astype(F32), grad_o_gain, grad_out_w, grad_mlp_gain,
        grad_gate_w, grad_up_w, grad_down_w,
    )


def solution(mesh):
    placed = (
        P("seq", None), P(), P(), P(None, "head"), P(None, "head"), P(None, "head"), P(None, "head"),
        P(None, "head"), P(None, "head"), P(None, "head"), P(None, "head"), P("head"), P("head"),
        P(None, "head"), P(), P("head", None), P(), P(None, "head"), P(None, "head"), P("head", None),
        P("seq", None),
    )
    given = (
        P("seq", None), P("seq", None), P(), P(None, "head"), P(None, "head"), P(None, "head"),
        P(None, "head"), P(None, "head"), P(None, "head"), P(None, "head"), P(None, "head"), P("head"),
        P("head"), P(None, "head"), P(), P("head", None), P(), P(None, "head"), P(None, "head"),
        P("head", None),
    )
    return jax.shard_map(local, mesh=mesh, in_specs=placed, out_specs=given, check_vma=False)
```

```python
import functools
import math
import jax
import jax.numpy as jnp
from jax import lax
from jax.experimental import pallas as pl
from jax.experimental.pallas import tpu as pltpu
from jax.sharding import PartitionSpec as P

NH = 2
GROUP = 64
LANES = 128
EPSILON = 1e-06
BF = jnp.bfloat16
F32 = jnp.float32
VMEM = pltpu.VMEM
VMEM_LIMIT = 40 * 1024 * 1024
SMALL_LIMIT = 24 * 1024 * 1024
EARLY = 16


def mm(left, right):
    return jnp.dot(left.astype(BF), right.astype(BF), preferred_element_type=F32)


def mm_nt(left, right):
    return lax.dot_general(
        left.astype(BF), right.astype(BF), (((1,), (1,)), ((), ())), preferred_element_type=F32
    )


def mm_tn(left, right):
    return lax.dot_general(
        left.astype(BF), right.astype(BF), (((0,), (0,)), ((), ())), preferred_element_type=F32
    )


def mm_exact(left, right):
    return jnp.dot(left, right, preferred_element_type=F32, precision=lax.Precision.HIGHEST)


def sigmoid(values):
    return 1.0 / (1.0 + jnp.exp(-values))


def softplus(values):
    return jnp.maximum(values, 0.0) + jnp.log1p(jnp.exp(-jnp.abs(values)))


def documents_at(starts, positions):
    total = jnp.zeros(positions.shape, jnp.int32)
    for k in range(starts.shape[0]):
        total = total + (starts[k] <= positions).astype(jnp.int32)
    return total


def sub_order(index):
    return NH * (index % GROUP) + index // GROUP


def order_pair():
    rows = sub_order(lax.broadcasted_iota(jnp.int32, (LANES, LANES), 0))
    cols = sub_order(lax.broadcasted_iota(jnp.int32, (LANES, LANES), 1))
    return rows, cols


def gate_columns(small, log_rate, bias, heads):
    lane = lax.broadcasted_iota(jnp.int32, (1, LANES), 1)
    rate = jnp.zeros((1, LANES), F32)
    shift = jnp.zeros((1, LANES), F32)
    for h in range(heads):
        at = lane == NH * heads + h
        rate = jnp.where(at, -jnp.exp(jnp.full((1, LANES), log_rate[h], F32)), rate)
        shift = jnp.where(at, bias[h], shift)
    return sigmoid(small), rate * softplus(small + shift), small + shift, rate


def chunk_decays(rows, cols_ref, row_ref, doc_ref, c, h, heads, doc_before):
    cum_col = cols_ref[rows, NH * heads + h : NH * heads + h + 1]
    doc_col = doc_ref[rows, 0:1]
    packed = row_ref[c]
    cum_row = packed[NH * heads + h : NH * heads + h + 1, :]
    doc_row = packed[NH * heads + heads : NH * heads + heads + 1, :]
    token_row = lax.broadcasted_iota(jnp.int32, (GROUP, LANES), 1) % GROUP
    token_col = lax.broadcasted_iota(jnp.int32, (GROUP, LANES), 0)
    seen = (token_col >= token_row) & (doc_col == doc_row)
    pair = jnp.where(seen, jnp.exp(jnp.where(seen, cum_col - cum_row, 0.0)), 0.0)
    start = jnp.where(doc_col == doc_before, jnp.exp(cum_col), 0.0)
    cum_last = cum_col[GROUP - 1 :, :]
    doc_last = doc_col[GROUP - 1 :, :]
    to_end = jnp.where(doc_col == doc_last, jnp.exp(cum_last - cum_col), 0.0)
    return pair, start, to_end


def two(array):
    return jnp.concatenate([array, array], axis=0)


def beta_pair(rows, cols_ref, row_ref, c, h):
    lane = lax.broadcasted_iota(jnp.int32, (1, LANES), 1)
    packed = row_ref[c]
    row = jnp.where(lane < GROUP, packed[NH * h : NH * h + 1, :], packed[NH * h + 1 : NH * h + 2, :])
    col = jnp.concatenate(
        [cols_ref[rows, NH * h : NH * h + 1], cols_ref[rows, NH * h + 1 : NH * h + 2]], axis=0
    )
    return row, col


def prep_kernel(
    heads, starts, log_rate, bias, proj, halo, conv_q, conv_k, conv_v, small,
    out_aug, state_aug, wy_k, wy_v, inverse, step_p, query_map, keys, queries, conv_total, cols, doc, row,
    final_state, final_map,
    ext, vals, score_map, step_b, masks,
):
    tokens = proj.shape[0]
    chunks = tokens // GROUP
    first = lax.axis_index("seq") * tokens
    lead = 8
    lower_r = lax.broadcasted_iota(jnp.int32, (LANES, LANES), 0)
    lower_c = lax.broadcasted_iota(jnp.int32, (LANES, LANES), 1)
    lower = ((lower_r >= lower_c) & (lower_r // GROUP == lower_c // GROUP)).astype(F32)
    lane = lax.broadcasted_iota(jnp.int32, (LANES, LANES), 1)
    per = LANES // GROUP
    for block in range(tokens // LANES):
        at = pl.ds(block * LANES, LANES)
        betas, logdec, _, _ = gate_columns(small[at, :], log_rate, bias, heads)
        cum = mm_exact(lower, logdec)
        where = lax.broadcasted_iota(jnp.int32, (LANES, LANES), 0) + (first + block * LANES)
        document = documents_at(starts, where).astype(F32)
        packed = jnp.where(lane < NH * heads, betas, jnp.where(lane < NH * heads + heads, cum, document))
        cols[at, :] = packed
        doc[at, :] = document
        turned = packed.T
        for part in range(per):
            piece = turned[0:8, part * GROUP : (part + 1) * GROUP]
            row[block * per + part] = jnp.concatenate([piece] * NH, axis=1)
    order_r, order_c = order_pair()
    level = 0
    width = 1
    while width < LANES:
        inside = (order_r // (2 * width) == order_c // (2 * width)) & (order_r // width > order_c // width)
        masks[level] = inside.astype(F32)
        level += 1
        width *= 2
    ext[0:lead, :] = halo[16 - lead : 16, :].astype(F32)
    ext[lead:, :] = proj[...].astype(F32)
    width_q = heads * LANES
    width_k = NH * heads * LANES
    taps = conv_q.shape[0]

    def conv_chunk(c, _):
        base = pl.multiple_of(c * GROUP, GROUP)
        rows = pl.ds(base, GROUP)
        position = lax.broadcasted_iota(jnp.int32, (GROUP, LANES), 0) + (first + base)
        document = doc[rows, :]
        kept = [
            (documents_at(starts, position - lag).astype(F32) == document).astype(F32) for lag in range(1, taps)
        ]
        for group in range((width_q + 2 * width_k) // LANES):
            at = slice(group * LANES, (group + 1) * LANES)
            if group * LANES < width_q:
                kernel, shift = conv_q, 0
            elif group * LANES < width_q + width_k:
                kernel, shift = conv_k, width_q
            else:
                kernel, shift = conv_v, width_q + width_k
            cut = slice(at.start - shift, at.stop - shift)
            window = ext[pl.ds(base, GROUP + lead), at]
            total = kernel[taps - 1 : taps, cut] * window[lead:, :]
            for lag in range(1, taps):
                total += kernel[taps - 1 - lag : taps - lag, cut] * window[lead - lag : lead - lag + GROUP, :] * kept[lag - 1]
            conv_total[rows, at] = total
            active = total * sigmoid(total)
            if group * LANES < width_q:
                unit = active * lax.rsqrt(jnp.sum(active * active, axis=1, keepdims=True) + EPSILON)
                queries[group, c] = (unit * LANES ** (-0.5)).astype(BF)
            elif group * LANES < width_q + width_k:
                piece = group - width_q // LANES
                unit = active * lax.rsqrt(jnp.sum(active * active, axis=1, keepdims=True) + EPSILON)
                keys[piece // NH, c, (piece % NH) * GROUP : (piece % NH + 1) * GROUP] = unit.astype(BF)
            else:
                piece = group - (width_q + width_k) // LANES
                vals[piece // NH, c, (piece % NH) * GROUP : (piece % NH + 1) * GROUP] = active.astype(BF)
        return 0

    lax.fori_loop(0, chunks, conv_chunk, 0)

    strict = order_r > order_c
    eye = (lower_r == lower_c).astype(F32)
    together = 2

    def part_chunks(step, _):
        jobs = []
        for k in range(together):
            c = step * together + k
            rows = pl.ds(pl.multiple_of(c * GROUP, GROUP), GROUP)
            before = documents_at(starts, jnp.full((1, 1), first + c * GROUP - 1, jnp.int32)).astype(F32)
            for h in range(heads):
                pair, start, to_end = chunk_decays(rows, cols, row, doc, c, h, heads, before)
                beta_row, beta_col = beta_pair(rows, cols, row, c, h)
                key = keys[h, c]
                query = queries[h, c]
                grams = mm_nt(jnp.concatenate([key, query], axis=0), key)
                system = jnp.where(strict, grams[:LANES] * two(pair), 0.0) * beta_row
                scores = grams[LANES:] * pair * beta_row
                jobs.append((c, h, start, to_end, beta_col, key, query, system, scores))
        inverses = [eye - job[7] * masks[0] for job in jobs]
        for n in range(1, level):
            halves = [mm(job[7] * masks[n], inv) for job, inv in zip(jobs, inverses)]
            inverses = [inv - mm(inv, half) for inv, half in zip(inverses, halves)]
        for job, inv in zip(jobs, inverses):
            c, h, start, to_end, beta_col, key, query, system, scores = job
            low_inv = inv.astype(BF)
            inverse[h, c] = low_inv
            key_f = key.astype(F32)
            both = mm(low_inv, jnp.concatenate([(two(start) * key_f).astype(BF), vals[h, c]], axis=1)).astype(BF)
            wy_k[h, c] = both[:, :LANES]
            wy_v[h, c] = both[:, LANES:]
            carried = (beta_col * two(to_end) * key_f).astype(BF)
            ahead = mm_tn(carried, both)
            step_p[h, c] = ahead[:, :LANES].astype(BF)
            step_b[h, c] = ahead[:, LANES:]
            scored = mm(scores, both)
            query_map[h, c] = (start * query.astype(F32) - scored[:, :LANES]).astype(BF)
            score_map[h, c] = scored[:, LANES:]
        return 0

    lax.fori_loop(0, chunks // together, part_chunks, 0)

    zero = jnp.zeros((LANES, LANES), F32)

    def advance(c, carry):
        rows = pl.ds(pl.multiple_of(c * GROUP, GROUP), GROUP)
        before = documents_at(starts, jnp.full((1, 1), first + c * GROUP - 1, jnp.int32)).astype(F32)
        new = []
        for h in range(heads):
            state = carry[h]
            low_state = state.astype(BF)
            state_aug[h, c] = low_state
            last = cols[rows, NH * heads + h : NH * heads + h + 1][GROUP - 1 :, :]
            whole = jnp.where(doc[rows, 0:1][GROUP - 1 :, :] == before, jnp.exp(last), 0.0)
            new.append(
                whole * state - mm(step_p[h, c], low_state) + jnp.concatenate([step_b[h, c], zero], axis=1)
            )
            mapped = mm(query_map[h, c], low_state)
            out_aug[h, rows, :] = jnp.concatenate([mapped[:, :LANES] + score_map[h, c], mapped[:, LANES:]], axis=1)
        return tuple(new)

    begin = jnp.concatenate([zero, eye], axis=1)
    end = lax.fori_loop(0, chunks, advance, (begin,) * heads)
    for h in range(heads):
        final_state[h] = end[h][:, :LANES].astype(final_state.dtype)
        final_map[h] = end[h][:, LANES:].astype(final_map.dtype)


def specs(count, space=None):
    return [pl.BlockSpec(memory_space=space or pltpu.VMEM)] * count


def mixer_prep(starts, log_rate, bias, proj, halo, conv_q, conv_k, conv_v, small):
    tokens, width = proj.shape
    heads = log_rate.shape[0]
    chunks = tokens // GROUP
    square = (heads, chunks, LANES, LANES)
    shape = jax.ShapeDtypeStruct
    outs = [
        shape((heads, tokens, 2 * LANES), F32),
        shape((heads, chunks, LANES, 2 * LANES), BF),
        shape(square, BF),
        shape(square, BF),
        shape(square, BF),
        shape(square, BF),
        shape((heads, chunks, GROUP, LANES), BF),
        shape(square, BF),
        shape((heads, chunks, GROUP, LANES), BF),
        shape((tokens, width), F32),
        shape((tokens, LANES), F32),
        shape((tokens, LANES), F32),
        shape((chunks, 8, LANES), F32),
        shape((heads, LANES, LANES), BF),
        shape((heads, LANES, LANES), BF),
    ]
    return pl.pallas_call(
        functools.partial(prep_kernel, heads),
        out_shape=outs,
        in_specs=specs(3, pltpu.SMEM) + specs(6),
        out_specs=specs(len(outs)),
        scratch_shapes=[
            VMEM((tokens + 8, width), F32),
            VMEM(square, BF),
            VMEM((heads, chunks, GROUP, LANES), F32),
            VMEM(square, F32),
            VMEM((8, LANES, LANES), F32),
        ],
        compiler_params=pltpu.CompilerParams(vmem_limit_bytes=VMEM_LIMIT),
        cost_estimate=pl.CostEstimate(flops=2_000_000_000, bytes_accessed=4_000_000, transcendentals=0),
        name="mixer_prep",
    )(starts, log_rate, bias, proj, halo, conv_q, conv_k, conv_v, small)


def back_kernel(
    heads, reach, starts, log_rate, bias, proj, halo, conv_q, conv_k, conv_v, small,
    state_aug, wy_k, wy_v, inverse, step_p, query_map, keys, queries, conv_total, cols, doc, row,
    state_in, d_mixed, *rest,
):
    after = rest[:reach]
    later = rest[reach : 2 * reach - 1]
    (
        d_kq, d_v, tail, d_halo, d_small, d_taps, d_scalars,
        ext, state_grads, d_query, d_key, d_value, col_grads, row_grads, d_total,
    ) = rest[2 * reach - 1 :]
    tokens = proj.shape[0]
    chunks = tokens // GROUP
    first = lax.axis_index("seq") * tokens
    lead = 8
    lane = lax.broadcasted_iota(jnp.int32, (GROUP, LANES), 1)

    def document_before(c):
        return documents_at(starts, jnp.full((1, 1), first + c * GROUP - 1, jnp.int32)).astype(F32)

    def whole_decay(c, h):
        at = pl.ds(pl.multiple_of(c * GROUP, GROUP) + GROUP - 8, 8)
        last = cols[at, NH * heads + h : NH * heads + h + 1][7:8, :]
        return jnp.where(doc[at, 0:1][7:8, :] == document_before(c), jnp.exp(last), 0.0)

    begin = []
    for h in range(heads):
        state = after[reach - 1][h].astype(F32)
        for r in range(reach - 2, -1, -1):
            state = mm_tn(later[r][h], state) + after[r][h].astype(F32)
        begin.append(state)

    def retreat(step, carry):
        c = chunks - 1 - step
        rows = pl.ds(pl.multiple_of(c * GROUP, GROUP), GROUP)
        new = []
        for h in range(heads):
            low_state = carry[h].astype(BF)
            state_grads[h, c] = low_state
            new.append(
                whole_decay(c, h) * carry[h]
                - mm_tn(step_p[h, c], low_state)
                + mm_tn(query_map[h, c], d_mixed[rows, h * LANES : (h + 1) * LANES])
            )
        return tuple(new)

    lax.fori_loop(0, chunks, retreat, tuple(begin))

    order_r, order_c = order_pair()
    strict = order_r > order_c
    together = 2
    last_token = lax.broadcasted_iota(jnp.int32, (GROUP, 1), 0) == GROUP - 1

    def chunk_back(step, _):
        for k in range(together):
            c = step * together + k
            rows = pl.ds(pl.multiple_of(c * GROUP, GROUP), GROUP)
            before = document_before(c)
            col_acc = jnp.zeros((GROUP, LANES), F32)
            row_acc = []
            row_beta = []
            for h in range(heads):
                pair, start, to_end = chunk_decays(rows, cols, row, doc, c, h, heads, before)
                beta_row, beta_col = beta_pair(rows, cols, row, c, h)
                key = keys[h, c]
                query = queries[h, c]
                key_f = key.astype(F32)
                query_f = query.astype(F32)
                d_out = d_mixed[rows, h * LANES : (h + 1) * LANES]
                d_state = state_grads[h, c]
                both = state_aug[h, c]
                state = both[:, :LANES].astype(F32) + mm(both[:, LANES:], state_in[h])
                low_state = state.astype(BF)
                fresh = wy_v[h, c].astype(F32) - mm(wy_k[h, c], low_state)
                grams = mm_nt(jnp.concatenate([key, query], axis=0), key)
                pair2 = two(pair)
                system = jnp.where(strict, grams[:LANES] * pair2, 0.0)
                scores = grams[LANES:] * pair
                key_end = two(to_end) * key_f
                key_start = two(start) * key_f
                d_wide = mm_tn(scores, d_out) + mm(key_end, d_state)
                solved = mm_tn(inverse[h, c], beta_col * d_wide)
                d_value[h, c] = solved
                low_fresh = fresh.astype(BF)
                crossed = mm_nt(
                    jnp.concatenate([solved.astype(BF), d_out], axis=0),
                    jnp.concatenate([low_fresh, low_state], axis=0),
                )
                pairs = jnp.where(strict, crossed[:LANES, :LANES], 0.0)
                solved_state = crossed[:LANES, LANES:]
                out_state = crossed[LANES:, LANES:]
                fresh_grad = mm_nt(beta_col * fresh, d_state)
                system_pairs = system * pairs
                decayed = -(system_pairs * beta_row)
                gram_grad = -(pairs * pair2 * beta_row)
                score_grad = crossed[LANES:, :LANES] * beta_row
                query_key = score_grad * pair
                score_decay = score_grad * scores
                stacked = jnp.concatenate([gram_grad, query_key], axis=0).astype(BF)
                direct = mm(stacked, key)
                turned = mm_tn(stacked, jnp.concatenate([key, query], axis=0))
                d_key[h, c] = direct[:LANES] + turned - two(start) * solved_state + two(to_end) * fresh_grad
                d_query[h, c] = direct[LANES:] + start * out_state
                ending = key_end * fresh_grad
                parts = decayed - key_start * solved_state - ending
                parts = parts[:GROUP] + parts[GROUP:] + score_decay + (start * query_f) * out_state
                at_end = jnp.sum(ending, keepdims=True) + whole_decay(c, h) * jnp.sum(
                    state * d_state.astype(F32), keepdims=True
                )
                decay_col = jnp.sum(parts, axis=1, keepdims=True) + jnp.where(last_token, at_end, 0.0)
                beta_sum = jnp.sum(d_wide * fresh, axis=1, keepdims=True)
                col_acc = jnp.where(lane == NH * heads + h, decay_col, col_acc)
                for s in range(NH):
                    col_acc = jnp.where(lane == NH * h + s, beta_sum[s * GROUP : (s + 1) * GROUP], col_acc)
                beta_row_sum = jnp.sum(system_pairs, axis=0, keepdims=True)
                row_beta.append(-beta_row_sum)
                row_acc.append(beta_row * beta_row_sum - jnp.sum(score_decay, axis=0, keepdims=True))
            col_grads[rows, :] = col_acc
            row_grads[c] = jnp.concatenate(
                row_acc + row_beta + [jnp.zeros((8 - 2 * heads, LANES), F32)], axis=0
            )
        return 0

    lax.fori_loop(0, chunks // together, chunk_back, 0)

    lower_r = lax.broadcasted_iota(jnp.int32, (LANES, LANES), 0)
    lower_c = lax.broadcasted_iota(jnp.int32, (LANES, LANES), 1)
    upper = ((lower_r <= lower_c) & (lower_r // GROUP == lower_c // GROUP)).astype(F32)
    per = LANES // GROUP
    scalar_decay = jnp.zeros((1, LANES), F32)
    scalar_rate = jnp.zeros((1, LANES), F32)
    wide = lax.broadcasted_iota(jnp.int32, (LANES, LANES), 1)
    for block in range(tokens // LANES):
        at = pl.ds(block * LANES, LANES)
        pieces = []
        for part in range(per):
            c = block * per + part
            turned = jnp.concatenate([row_grads[c], jnp.zeros((LANES - 8, LANES), F32)], axis=0).T
            piece = jnp.zeros((GROUP, LANES), F32)
            for h in range(heads):
                decay_col = turned[:GROUP, h : h + 1] + turned[GROUP:, h : h + 1]
                piece = jnp.where(lane == NH * heads + h, decay_col, piece)
                for s in range(NH):
                    beta_col = turned[s * GROUP : (s + 1) * GROUP, heads + h : heads + h + 1]
                    piece = jnp.where(lane == NH * h + s, beta_col, piece)
            pieces.append(piece)
        grads = col_grads[at, :] + jnp.concatenate(pieces, axis=0)
        d_logdec = mm_exact(upper, grads)
        betas, logdec, argument, rate = gate_columns(small[at, :], log_rate, bias, heads)
        d_argument = d_logdec * rate * sigmoid(argument)
        scalar_rate += jnp.sum(d_logdec * logdec, axis=0, keepdims=True)
        scalar_decay += jnp.sum(d_argument, axis=0, keepdims=True)
        d_small[at, :] = jnp.where(
            wide < NH * heads,
            grads * betas * (1.0 - betas),
            jnp.where(wide < NH * heads + heads, d_argument, 0.0),
        ).astype(BF)
    d_scalars[...] = jnp.concatenate([scalar_rate, scalar_decay, jnp.zeros((6, LANES), F32)], axis=0)

    ext[0:lead, :] = halo[16 - lead : 16, :].astype(F32)
    ext[lead:, :] = proj[...].astype(F32)
    width_q = heads * LANES
    width_k = NH * heads * LANES
    width = width_q + 2 * width_k
    taps = conv_q.shape[0]
    d_taps[...] = jnp.zeros(d_taps.shape, F32)
    d_total[tokens:, :] = jnp.zeros((8, width), F32)

    def kernel_of(group):
        if group * LANES < width_q:
            return conv_q, slice(group * LANES, (group + 1) * LANES)
        if group * LANES < width_q + width_k:
            return conv_k, slice(group * LANES - width_q, (group + 1) * LANES - width_q)
        return conv_v, slice(group * LANES - width_q - width_k, (group + 1) * LANES - width_q - width_k)

    def active_back(c, _):
        base = pl.multiple_of(c * GROUP, GROUP)
        rows = pl.ds(base, GROUP)
        position = lax.broadcasted_iota(jnp.int32, (GROUP, LANES), 0) + (first + base)
        document = doc[rows, :]
        kept = [
            (documents_at(starts, position - lag).astype(F32) == document).astype(F32) for lag in range(1, taps)
        ]
        for group in range(width // LANES):
            at = slice(group * LANES, (group + 1) * LANES)
            total = conv_total[rows, at]
            sg = sigmoid(total)
            if group * LANES < width_q + width_k:
                active = total * sg
                scale = lax.rsqrt(jnp.sum(active * active, axis=1, keepdims=True) + EPSILON)
                unit = active * scale
                if group * LANES < width_q:
                    grad = d_query[group, c] * LANES ** (-0.5)
                else:
                    piece = group - width_q // LANES
                    grad = d_key[piece // NH, c, (piece % NH) * GROUP : (piece % NH + 1) * GROUP]
                grad = scale * (grad - unit * jnp.sum(unit * grad, axis=1, keepdims=True))
            else:
                piece = group - (width_q + width_k) // LANES
                grad = d_value[piece // NH, c, (piece % NH) * GROUP : (piece % NH + 1) * GROUP]
            grad = grad * (sg * (1.0 + total * (1.0 - sg)))
            d_total[rows, at] = grad
            window = ext[pl.ds(base, GROUP + lead), at]
            sums = []
            for j in range(taps):
                lag = taps - 1 - j
                term = grad * window[lead - lag : lead - lag + GROUP, :]
                if lag > 0:
                    term = term * kept[lag - 1]
                sums.append(jnp.sum(term, axis=0, keepdims=True))
            d_taps[0:taps, at] += jnp.concatenate(sums, axis=0)
        return 0

    lax.fori_loop(0, chunks, active_back, 0)

    def conv_back(c, _):
        base = pl.multiple_of(c * GROUP, GROUP)
        rows = pl.ds(base, GROUP)
        position = lax.broadcasted_iota(jnp.int32, (GROUP, LANES), 0) + (first + base)
        document = doc[rows, :]
        kept = [
            (documents_at(starts, position + lag).astype(F32) == document).astype(F32) for lag in range(1, taps)
        ]
        for group in range(width // LANES):
            at = slice(group * LANES, (group + 1) * LANES)
            kernel, cut = kernel_of(group)
            window = d_total[pl.ds(base, GROUP + lead), at]
            grad = kernel[taps - 1 : taps, cut] * window[:GROUP]
            for lag in range(1, taps):
                grad += kernel[taps - 1 - lag : taps - lag, cut] * kept[lag - 1] * window[lag : lag + GROUP]
            target = d_v if kernel is conv_v else d_kq
            shift = width_k if kernel is conv_q else 0
            target[rows, cut.start + shift : cut.stop + shift] = grad.astype(BF)
            tail[:, at] = grad[GROUP - 16 :]
        return 0

    lax.fori_loop(0, chunks, conv_back, 0)
    position = lax.broadcasted_iota(jnp.int32, (8, LANES), 0) + (first - 8)
    document = documents_at(starts, position)
    for group in range(width // LANES):
        at = slice(group * LANES, (group + 1) * LANES)
        kernel, cut = kernel_of(group)
        window = jnp.concatenate([jnp.zeros((8, LANES), F32), d_total[0:8, at]], axis=0)
        grad = jnp.zeros((8, LANES), F32)
        for lag in range(1, taps):
            kept = (documents_at(starts, position + lag) == document).astype(F32)
            grad += kernel[taps - 1 - lag : taps - lag, cut] * kept * window[lag : lag + 8]
        d_halo[:, at] = grad


def mixer_back(starts, log_rate, bias, proj, halo, conv_q, conv_k, conv_v, small, saved, state_in, d_mixed, after, later):
    tokens, width = proj.shape
    heads = log_rate.shape[0]
    chunks = tokens // GROUP
    reach = len(after)
    square = (heads, chunks, LANES, LANES)
    shape = jax.ShapeDtypeStruct
    outs = [
        shape((tokens, conv_k.shape[1] + conv_q.shape[1]), BF),
        shape((tokens, conv_v.shape[1]), BF),
        shape((16, width), F32),
        shape((8, width), F32),
        shape((tokens, LANES), BF),
        shape((8, width), F32),
        shape((8, LANES), F32),
    ]
    operands = [starts, log_rate, bias, proj, halo, conv_q, conv_k, conv_v, small, *saved, state_in, d_mixed, *after, *later]
    return pl.pallas_call(
        functools.partial(back_kernel, heads, reach),
        out_shape=outs,
        in_specs=specs(3, pltpu.SMEM) + specs(len(operands) - 3),
        out_specs=specs(len(outs)),
        scratch_shapes=[
            VMEM((tokens + 8, width), F32),
            VMEM(square, BF),
            VMEM((heads, chunks, GROUP, LANES), F32),
            VMEM(square, F32),
            VMEM(square, F32),
            VMEM((tokens, LANES), F32),
            VMEM((chunks, 8, LANES), F32),
            VMEM((tokens + 8, width), F32),
        ],
        compiler_params=pltpu.CompilerParams(vmem_limit_bytes=VMEM_LIMIT),
        cost_estimate=pl.CostEstimate(flops=2_000_000_000, bytes_accessed=4_000_000, transcendentals=0),
        name="mixer_back",
    )(*operands)


def call(kernel, name, outs, operands, smem=0, scratch=(), flops=0, limit=SMALL_LIMIT):
    moved = sum(a.size * a.dtype.itemsize for a in operands) + sum(
        math.prod(o.shape) * jnp.dtype(o.dtype).itemsize for o in outs
    )
    return pl.pallas_call(
        kernel,
        out_shape=outs,
        in_specs=specs(smem, pltpu.SMEM) + specs(len(operands) - smem),
        out_specs=specs(len(outs)),
        scratch_shapes=list(scratch),
        compiler_params=pltpu.CompilerParams(vmem_limit_bytes=limit),
        cost_estimate=pl.CostEstimate(flops=flops // EARLY, bytes_accessed=moved // EARLY, transcendentals=0),
        name=name,
    )(*operands)


def shaped(dims, kind):
    return jax.ShapeDtypeStruct(dims, kind)


def half_rows(ref, own):
    half = ref.shape[0] // 2
    low = lax.axis_index("head") % 2
    return pl.ds(pl.multiple_of((low if own else 1 - low) * half, half), half)


def seq_bits():
    at = lax.axis_index("seq")
    z = at // 2 % 4
    low, high = z % 2, z // 2
    return {"x": at % 2, "pair": low ^ high, "cross": high}


PARTNER = {"x": 1, "pair": 2, "cross": 6}
X_FIRST = ("x", "pair", "cross")
Z_FIRST = ("pair", "cross", "x")


def half_width(ref, own, stage="x"):
    half = ref.shape[1] // 2
    low = seq_bits()[stage]
    return pl.ds(pl.multiple_of((low if own else 1 - low) * half, half), half)


def project_kernel(x, gain, q_w, k_w, v_w, gate_w, beta_w, decay_w, normed, projected, outgate, small, edge, side_w):
    x_float = x[...].astype(F32)
    low = (x_float * lax.rsqrt(jnp.mean(x_float * x_float, axis=1, keepdims=True) + EPSILON) * gain[...]).astype(BF)
    normed[...] = low
    last = x.shape[0] - edge.shape[0]
    at = 0
    for weight in (q_w, k_w, v_w):
        piece = mm(low, weight[...]).astype(BF)
        projected[:, at : at + weight.shape[1]] = piece
        edge[:, at : at + weight.shape[1]] = piece[last:, :]
        at += weight.shape[1]
    edge[:, at:] = low[last:, :]
    outgate[...] = mm(low, gate_w[...])
    gather_side(side_w, beta_w, decay_w)
    small[...] = mm_nt(low, side_w[...])


def gather_side(side_w, beta_w, decay_w):
    betas = beta_w.shape[0]
    side_w[...] = jnp.zeros(side_w.shape, F32)
    side_w[0:betas, :] = beta_w[...].astype(F32)
    side_w[betas : betas + decay_w.shape[0], :] = decay_w[...].astype(F32)


def project(x, gain, q_w, k_w, v_w, gate_w, beta_w, decay_w):
    tokens, wide = x.shape
    width = q_w.shape[1] + k_w.shape[1] + v_w.shape[1]
    outs = [
        shaped((tokens, wide), BF), shaped((tokens, width), BF),
        shaped((tokens, gate_w.shape[1]), F32), shaped((tokens, LANES), F32), shaped((16, width + wide), BF),
    ]
    operands = [x, gain.reshape(1, -1), q_w, k_w, v_w, gate_w, beta_w, decay_w]
    return call(
        project_kernel, "project", outs, operands, flops=2 * tokens * wide * (width + 384),
        scratch=[VMEM((LANES, wide), F32)],
    )


def attend_kernel(heads, reach, out_aug, outgate, o_gain, out_weight, *rest):
    before = rest[:reach]
    mixed, branch, give, keep, state_in = rest[reach:]
    gain = o_gain[...]
    for h in range(heads):
        at = slice(h * LANES, (h + 1) * LANES)
        state = before[reach - 1][0, h].astype(F32)
        for r in range(reach - 2, -1, -1):
            state = mm(before[r][1, h], state) + before[r][0, h].astype(F32)
        state_in[h] = state
        mix = out_aug[h, :, :LANES] + mm(out_aug[h, :, LANES:], state)
        mixed[:, at] = mix
        gate = outgate[:, at]
        normed = mix * lax.rsqrt(jnp.mean(mix * mix, axis=1, keepdims=True) + EPSILON)
        branch[:, at] = (normed * gain * (gate * sigmoid(gate))).astype(BF)
    give[...] = mm(branch[half_rows(branch, False), :], out_weight[...]).astype(BF)
    keep[...] = mm(branch[half_rows(branch, True), :], out_weight[...])


def attend(out_aug, outgate, o_gain, out_weight, before):
    heads, tokens, _ = out_aug.shape
    wide = out_weight.shape[1]
    outs = [
        shaped((tokens, heads * LANES), F32), shaped((tokens, heads * LANES), BF),
        shaped((tokens // 2, wide), BF), shaped((tokens // 2, wide), F32), shaped((heads, LANES, LANES), F32),
    ]
    operands = [out_aug, outgate, o_gain.reshape(1, -1), out_weight, *before]
    return call(
        functools.partial(attend_kernel, heads, len(before)), "attend", outs, operands,
        flops=2 * tokens * wide * heads * LANES,
    )


def enter_kernel(x, mine, other, gain, hidden, normed):
    value = x[half_rows(x, True), :].astype(F32) + mine[...].astype(F32) + other[...].astype(F32)
    hidden[...] = value
    normed[...] = (
        value * lax.rsqrt(jnp.mean(value * value, axis=1, keepdims=True) + EPSILON) * gain[...]
    ).astype(BF)


def enter(x, mine, other, gain):
    outs = [shaped(mine.shape, F32), shaped(mine.shape, BF)]
    return call(enter_kernel, "enter", outs, [x, mine, other, gain.reshape(1, -1)])


def feed_kernel(
    own, other, gate_w, up_w, down_w, out_grad,
    normed, d_gate, d_up, inner, part_give, part_keep, feed_give, feed_keep,
):
    for mine, source, part, fed in ((False, other, part_give, feed_give), (True, own, part_keep, feed_keep)):
        rows = half_rows(normed, mine)
        low = source[...]
        normed[rows, :] = low
        gate = mm_nt(low, gate_w[...])
        up = mm_nt(low, up_w[...])
        d_inner = mm_nt(out_grad[rows, :], down_w[...])
        sg = sigmoid(gate)
        active = gate * sg
        low_inner = (active * up).astype(BF)
        inner[rows, :] = low_inner
        low_gate = (d_inner * up * (sg * (1.0 + gate * (1.0 - sg)))).astype(BF)
        low_up = (d_inner * active).astype(BF)
        d_gate[rows, :] = low_gate
        d_up[rows, :] = low_up
        part[...] = (mm(low_gate, gate_w[...]) + mm(low_up, up_w[...])).astype(part.dtype)
        fed[...] = mm(low_inner, down_w[...]).astype(fed.dtype)


def feed(own, other, gate_w, up_w, down_w, out_grad):
    tokens, wide = out_grad.shape
    units = gate_w.shape[0]
    half = (tokens // 2, wide)
    outs = [shaped((tokens, wide), BF)] + [shaped((tokens, units), BF)] * 3 + [
        shaped(half, BF), shaped(half, F32), shaped(half, BF), shaped(half, F32),
    ]
    operands = [own, other, gate_w, up_w, down_w, out_grad]
    return call(feed_kernel, "feed", outs, operands, flops=12 * tokens * wide * units)


def leave_kernel(mine, other, hidden, gain, out_grad, d_hidden, low, d_gain):
    grad = mine[...].astype(F32) + other[...].astype(F32)
    value = hidden[...]
    scale = lax.rsqrt(jnp.mean(value * value, axis=1, keepdims=True) + EPSILON)
    unit = value * scale
    d_gain[...] = jnp.sum(grad * unit, axis=0, keepdims=True)
    d_unit = grad * gain[...]
    total = out_grad[half_rows(out_grad, True), :].astype(F32) + scale * (
        d_unit - unit * jnp.mean(d_unit * unit, axis=1, keepdims=True)
    )
    d_hidden[...] = total
    low[...] = total.astype(BF)


def leave(mine, other, hidden, gain, out_grad):
    outs = [shaped(mine.shape, F32), shaped(mine.shape, BF), shaped((1, mine.shape[1]), F32)]
    return call(leave_kernel, "leave", outs, [mine, other, hidden, gain.reshape(1, -1), out_grad])


def finish_kernel(mine, other, x, gain, d_hidden, low, d_gain):
    grad = mine[...].astype(F32) + other[...].astype(F32)
    value = x[half_rows(x, True), :].astype(F32)
    scale = lax.rsqrt(jnp.mean(value * value, axis=1, keepdims=True) + EPSILON)
    unit = value * scale
    d_gain[...] = jnp.sum(grad * unit, axis=0, keepdims=True)
    d_unit = grad * gain[...]
    low[...] = (
        d_hidden[...] + scale * (d_unit - unit * jnp.mean(d_unit * unit, axis=1, keepdims=True))
    ).astype(BF)


def finish(mine, other, x, gain, d_hidden):
    outs = [shaped(mine.shape, BF), shaped((1, mine.shape[1]), F32)]
    return call(finish_kernel, "finish", outs, [mine, other, x, gain.reshape(1, -1), d_hidden])


def attend_back_kernel(
    heads, own, other, out_weight, mixed, outgate, o_gain, out_aug,
    grad, d_mixed, d_outgate, d_gain, carry,
):
    gain = o_gain[...]
    gain_sum = jnp.zeros((1, LANES), F32)
    carries = [jnp.zeros((LANES, LANES), F32)] * heads
    for mine, source in ((True, own), (False, other)):
        rows = half_rows(grad, mine)
        low = source[...]
        grad[rows, :] = low
        d_branch = mm_nt(low, out_weight[...])
        for h in range(heads):
            at = slice(h * LANES, (h + 1) * LANES)
            mix = mixed[rows, at]
            gate = outgate[rows, at]
            grad_h = d_branch[:, at]
            scale = lax.rsqrt(jnp.mean(mix * mix, axis=1, keepdims=True) + EPSILON)
            normed = mix * scale
            sg = sigmoid(gate)
            through = grad_h * (gate * sg)
            gain_sum += jnp.sum(through * normed, axis=0, keepdims=True)
            d_normed = through * gain
            d_mix = (scale * (d_normed - normed * jnp.mean(d_normed * normed, axis=1, keepdims=True))).astype(BF)
            d_mixed[rows, at] = d_mix
            d_outgate[rows, at] = (grad_h * normed * gain * (sg * (1.0 + gate * (1.0 - sg)))).astype(BF)
            carries[h] += mm_tn(out_aug[h, rows, LANES:], d_mix)
    for h in range(heads):
        carry[h] = carries[h].astype(carry.dtype)
    d_gain[...] = gain_sum


def attend_back(own, other, out_weight, mixed, outgate, o_gain, out_aug):
    heads, tokens, _ = out_aug.shape
    wide = out_weight.shape[1]
    outs = [
        shaped((tokens, wide), BF), shaped((tokens, heads * LANES), BF), shaped((tokens, heads * LANES), BF),
        shaped((1, LANES), F32), shaped((heads, LANES, LANES), BF),
    ]
    operands = [own, other, out_weight, mixed, outgate, o_gain.reshape(1, -1), out_aug]
    return call(
        functools.partial(attend_back_kernel, heads), "attend_back", outs, operands,
        flops=2 * tokens * wide * heads * LANES,
    )


def store_rows_cut(part, at, piece):
    quarters = part.shape[0]
    rows = piece.shape[0] // quarters
    for q in range(quarters):
        for i in range(piece.shape[1] // LANES):
            part[q, at + i * rows : at + (i + 1) * rows, :] = piece[
                q * rows : (q + 1) * rows, i * LANES : (i + 1) * LANES
            ].astype(BF)


def store_cols_cut(part, at, piece):
    for q in range(part.shape[0]):
        part[q, at : at + piece.shape[0], :] = piece[:, q * LANES : (q + 1) * LANES].astype(BF)


def feed_weights_kernel(normed, d_gate, d_up, inner, out_grad, grads):
    units = inner.shape[1]
    for k, (left, right) in enumerate(((d_gate, normed), (d_up, normed), (inner, out_grad))):
        grads[k * units : (k + 1) * units, :] = mm_tn(left[...], right[...]).astype(BF)


def feed_weights(normed, d_gate, d_up, inner, out_grad):
    tokens, wide = normed.shape
    rows = 3 * inner.shape[1]
    operands = [normed, d_gate, d_up, inner, out_grad]
    (grads,) = call(
        feed_weights_kernel, "feed_weights", [shaped((rows, wide), BF)], operands, flops=2 * tokens * wide * rows
    )
    return grads


def gate_weights_kernel(normed, d_outgate, branch, grad, give, keep):
    for own, part in ((False, give), (True, keep)):
        store_rows_cut(part, 0, mm_tn(normed[:, half_width(normed, own)], d_outgate[...]))
        store_cols_cut(part, d_outgate.shape[1], mm_tn(branch[...], grad[:, half_width(grad, own)]))


def gate_weights(normed, d_outgate, branch, grad):
    rows = d_outgate.shape[1] + branch.shape[1]
    outs = [shaped((4, rows, LANES), BF)] * 2
    operands = [normed, d_outgate, branch, grad]
    return call(
        gate_weights_kernel, "gate_weights", outs, operands, flops=2 * normed.shape[0] * normed.shape[1] * rows
    )


def mix_weights_kernel(first, normed, halo, d_cols, d_halo, *rest):
    *side, give, keep = rest
    low_halo = d_halo[...].astype(BF)
    for own, part in ((False, give), (True, keep)):
        at = half_width(normed, own, first)
        left = normed[:, at]
        total = mm_tn(left, d_cols[...]) + mm_tn(halo[halo.shape[0] - d_halo.shape[0] :, at], low_halo)
        store_rows_cut(part, 0, total)
        if side:
            store_cols_cut(part, d_cols.shape[1], mm_tn(side[0][...], left)[:16])


def mix_weights(first, normed, halo, d_cols, d_halo, *side):
    tokens, wide = normed.shape
    rows = d_cols.shape[1] + 16 * len(side)
    operands = [normed, halo, d_cols, d_halo, *side]
    return call(
        functools.partial(mix_weights_kernel, first), "mix_weights", [shaped((4, rows, LANES), BF)] * 2,
        operands, flops=2 * tokens * wide * rows,
    )


def unproject_kernel(
    d_kq, d_v, tail, following, d_outgate, d_small, q_w, k_w, v_w, gate_w, beta_w, decay_w, give, keep,
    joined, side_w,
):
    tokens, width = joined.shape
    wide_q, wide_k = q_w.shape[1], k_w.shape[1]
    joined[:, 0:wide_q] = d_kq[:, wide_k:]
    joined[:, wide_q : wide_q + wide_k] = d_kq[:, :wide_k]
    joined[:, wide_q + wide_k :] = d_v[...]
    joined[tokens - 16 :, :] = jnp.concatenate([tail[0:8, :], tail[8:16, :] + following[...]], axis=0).astype(BF)
    gather_side(side_w, beta_w, decay_w)
    for own, part in ((False, give), (True, keep)):
        rows = half_rows(joined, own)
        total = mm_nt(d_outgate[rows, :], gate_w[...]) + mm(d_small[rows, :], side_w[...])
        at = 0
        for weight in (q_w, k_w, v_w):
            total += mm_nt(joined[rows, at : at + weight.shape[1]], weight[...])
            at += weight.shape[1]
        part[...] = total.astype(part.dtype)


def unproject(d_kq, d_v, tail, following, d_outgate, d_small, q_w, k_w, v_w, gate_w, beta_w, decay_w):
    tokens = d_v.shape[0]
    wide, width = q_w.shape[0], tail.shape[1]
    half = (tokens // 2, wide)
    operands = [d_kq, d_v, tail, following, d_outgate, d_small, q_w, k_w, v_w, gate_w, beta_w, decay_w]
    return call(
        unproject_kernel, "unproject", [shaped(half, BF), shaped(half, F32)], operands,
        scratch=[VMEM((tokens, width), BF), VMEM((LANES, wide), F32)],
        flops=2 * tokens * (width + 384) * wide,
    )


def fold_kernel(stage, keep, got, *outs):
    if len(outs) == 1:
        outs[0][...] = (keep[...].astype(F32) + got[...].astype(F32)).astype(BF)
        return
    mine = seq_bits()[stage]
    half = keep.shape[0] // 2
    for own, out in ((False, outs[0]), (True, outs[1])):
        at = (mine if own else 1 - mine) * half
        for k in range(half):
            out[k] = (keep[at + k].astype(F32) + got[at + k].astype(F32)).astype(BF)


def fold(stage, keep, got):
    count, rows, lanes = keep.shape
    outs = [shaped((count // 2, rows, lanes), BF)] * 2 if stage else [shaped(keep.shape, BF)]
    return call(functools.partial(fold_kernel, stage), "fold", outs, [keep, got])


class Line:
    def __init__(self):
        self.last = None

    def after(self, *arrays):
        if self.last is None:
            return arrays
        return lax.optimization_barrier((*arrays, self.last))[:-1]

    def step(self, function, *arrays):
        result = function(*self.after(*arrays))
        self.last = jax.tree.leaves(result)[0]
        return result


class Sum:
    def __init__(self, line, order, give, keep):
        self.line, self.order, self.keep, self.at = line, order, keep, 0
        self.got = swapped(give, "seq", PARTNER[order[0]])

    def next(self):
        stages = len(self.order)
        self.at += 1
        if self.at < stages:
            give, self.keep = self.line.step(
                functools.partial(fold, self.order[self.at]), self.keep, self.got
            )
            self.got = swapped(give, "seq", PARTNER[self.order[self.at]])
            return
        if self.at == stages:
            (mine,) = self.line.step(functools.partial(fold, None), self.keep, self.got)
            bit = 8
            while bit < lax.axis_size("seq"):
                mine = (mine.astype(F32) + swapped(mine, "seq", bit).astype(F32)).astype(BF)
                bit *= 2
        else:
            mine = self.line.step(lambda *parts: jnp.concatenate(parts, axis=0), self.keep, self.got)
        self.keep = mine
        self.got = swapped(mine, "seq", PARTNER[self.order[2 * stages - 1 - self.at]])

    def finish(self, kernel, name, outs):
        return self.line.step(
            lambda *parts: call(functools.partial(kernel, self.order), name, outs, list(parts)), self.keep, self.got
        )


def blocks_of(order, mine, other):
    bits = seq_bits()
    first, second, third = (bits[stage] for stage in order)
    for flip, ref in ((0, mine), (1, other)):
        for slot in range(4):
            yield 4 * (first ^ flip) + 2 * (second ^ (slot // 2)) + (third ^ (slot % 2)), ref, slot


def at_block(index):
    return pl.ds(pl.multiple_of(index * LANES, LANES), LANES)


def load_rows_cut(ref, slot, at, count):
    return [ref[slot, at + i * LANES : at + (i + 1) * LANES, :].astype(F32) for i in range(count)]


def gate_out_kernel(order, mine, other, outgate, out):
    for index, ref, slot in blocks_of(order, mine, other):
        width = outgate.shape[1]
        for i, piece in enumerate(load_rows_cut(ref, slot, 0, width // LANES)):
            outgate[at_block(index), i * LANES : (i + 1) * LANES] = piece
        out[:, at_block(index)] = ref[slot, width : width + out.shape[0], :].astype(F32)


def mix_out_kernel(side, order, mine, other, *outs):
    wide = outs if not side else outs[:-2]
    for index, ref, slot in blocks_of(order, mine, other):
        at = 0
        for out in wide:
            for i, piece in enumerate(load_rows_cut(ref, slot, at, out.shape[1] // LANES)):
                out[at_block(index), i * LANES : (i + 1) * LANES] = piece
            at += out.shape[1]
        if side:
            pieces = ref[slot, at : at + 16, :].astype(F32)
            at = 0
            for part in outs[-2:]:
                part[:, at_block(index)] = pieces[at : at + part.shape[0], :]
                at += part.shape[0]


def shifted(value, axis, steps):
    count = lax.axis_size(axis)
    leading, last = max(0, -steps), min(count, count - steps)
    return lax.ppermute(value, axis, [(source, source + steps) for source in range(leading, last)])


def swapped(value, axis, bit):
    return lax.ppermute(value, axis, [(s, s ^ bit) for s in range(lax.axis_size(axis))])


def head_sum(give, keep):
    total = keep + swapped(give, "head", 1).astype(F32)
    mine = total.astype(BF)
    other = swapped(mine, "head", 2)
    bit = 4
    while bit < lax.axis_size("head"):
        mine = (mine.astype(F32) + other.astype(F32)).astype(BF)
        other = swapped(mine, "head", bit)
        bit *= 2
    return mine, other


def both_halves(mine):
    low = lax.axis_index("head") % 2
    other = swapped(mine, "head", 1)
    return jnp.concatenate([jnp.where(low == 0, mine, other), jnp.where(low == 0, other, mine)], axis=0)


def reach_of(tokens, count):
    whole = tokens * count
    longest = whole // 4 + 2 * (whole // 64 - 1)
    return max(1, min(count - 1, -(-(longest - 1) // tokens)))


def local(
    block_in, seq_start, attn_gain, q_weight, k_weight, v_weight, conv_q, conv_k, conv_v,
    beta_weight, decay_weight, a_log, dt_bias, outgate_weight, o_gain, out_weight,
    mlp_gain, gate_weight, up_weight, down_weight, out_grad,
):
    tokens = block_in.shape[0]
    heads = a_log.shape[0]
    width_q = q_weight.shape[1]
    width_k = k_weight.shape[1]
    width = width_q + 2 * width_k
    betas = beta_weight.shape[1]
    reach = reach_of(tokens, lax.axis_size("seq"))
    wide = block_in.shape[1]
    units = gate_weight.shape[1]
    beta_rows, decay_rows = beta_weight.T, decay_weight.T
    normed, projected, outgate, small, edge = project(
        block_in, attn_gain, q_weight, k_weight, v_weight, outgate_weight, beta_rows, decay_rows
    )
    halo = shifted(edge, "seq", 1)
    halo, normed_halo = halo[:, :width], halo[:, width:]
    mixer_args = (seq_start, a_log, dt_bias, projected, halo, conv_q, conv_k, conv_v, small)
    prepared = mixer_prep(*mixer_args)
    out_aug, saved, final_state, final_map = prepared[0], prepared[1:13], prepared[13], prepared[14]
    pair = jnp.stack([final_state, final_map])
    before = [shifted(pair, "seq", r) for r in range(1, reach)] + [shifted(final_state[None], "seq", reach)]
    later = [shifted(final_map, "seq", -r) for r in range(1, reach)]
    mixed, branch, give, keep, state_in = attend(out_aug, outgate, o_gain, out_weight, before)
    hidden, normed_own = enter(block_in, *head_sum(give, keep), mlp_gain)
    normed_mlp, d_gate, d_up, inner, part_give, part_keep, feed_give, feed_keep = feed(
        normed_own, swapped(normed_own, "head", 1), gate_weight.T, up_weight.T, down_weight, out_grad
    )
    line = Line()
    part_mine, part_other = head_sum(part_give, part_keep)
    line.last = part_mine
    feed_grads = line.step(feed_weights, normed_mlp, d_gate, d_up, inner, out_grad)
    feed_sums = lax.psum(feed_grads, "seq")
    d_hidden, attention_own, grad_mlp_gain = line.step(leave, part_mine, part_other, hidden, mlp_gain, out_grad)
    attention_gradient, grad_mixed, grad_outgate, grad_o_part, carry = line.step(
        attend_back, attention_own, swapped(attention_own, "head", 1), out_weight, mixed, outgate, o_gain, out_aug
    )
    after = [shifted(carry, "seq", -r) for r in range(1, reach + 1)]
    sum_out = Sum(line, X_FIRST, *line.step(gate_weights, normed, grad_outgate, branch, attention_gradient))
    feed_mine, feed_other = head_sum(feed_give, feed_keep)
    output = both_halves((hidden + feed_mine.astype(F32) + feed_other.astype(F32)).astype(BF))
    d_kq, d_v, tail, d_halo, grad_small, grad_taps, grad_scalars = line.step(
        lambda d_mixed: mixer_back(*mixer_args, saved, state_in, d_mixed, after, later), grad_mixed
    )
    following = shifted(d_halo, "seq", -1)
    cut_q, cut_k, cut_v = slice(0, width_q), slice(width_q, width_q + width_k), slice(width_q + width_k, width)
    halo_kq = jnp.concatenate([d_halo[:, cut_k], d_halo[:, cut_q]], axis=1)
    sum_kq = Sum(
        line, X_FIRST, *line.step(functools.partial(mix_weights, X_FIRST[0]), normed, normed_halo, d_kq, halo_kq)
    )
    sum_v = Sum(
        line, Z_FIRST,
        *line.step(functools.partial(mix_weights, Z_FIRST[0]), normed, normed_halo, d_v, d_halo[:, cut_v], grad_small),
    )
    mine, other = head_sum(
        *line.step(
            unproject, d_kq, d_v, tail, following, grad_outgate, grad_small,
            q_weight, k_weight, v_weight, outgate_weight, beta_rows, decay_rows,
        )
    )
    taps = conv_q.shape[0]

    def padded(*rows):
        joined = jnp.concatenate(rows, axis=1)
        return jnp.pad(joined, ((0, 0), (0, width - joined.shape[1])))

    for part in (sum_out, sum_kq, sum_v):
        part.next()
    for part in (sum_out, sum_kq, sum_v):
        part.next()
    line.last = feed_sums
    input_own, grad_attn_gain = line.step(finish, mine, other, block_in, attn_gain, d_hidden)
    grad_input = both_halves(input_own)
    small_sums = jnp.concatenate(
        [
            grad_taps[:taps], padded(grad_scalars[0:1], grad_scalars[1:2]),
            padded(grad_attn_gain), padded(grad_mlp_gain), padded(grad_o_part),
        ],
        axis=0,
    )
    small_got = swapped(small_sums, "seq", 1)
    bit = 2
    rounds = 3
    while small_got is not None or rounds > 0:
        for part in (sum_out, sum_kq, sum_v) if rounds > 0 else ():
            part.next()
        rounds -= 1
        if small_got is not None:
            small_sums = line.step(jnp.add, small_sums, small_got)
            small_got = swapped(small_sums, "seq", bit) if bit < lax.axis_size("seq") else None
            bit *= 2
    gains = small_sums[taps + 1 : taps + 4]
    gains = gains + swapped(gains, "head", 1)
    grad_o_gain = gains[2:3, :LANES]
    bit = 2
    while bit < lax.axis_size("head"):
        grad_o_gain = grad_o_gain + swapped(grad_o_gain, "head", bit)
        bit *= 2
    grad_outgate_w, grad_out_w = sum_out.finish(
        gate_out_kernel, "gate_out", [shaped((wide, width_q), F32), shaped((width_q, wide), F32)]
    )
    grad_v_w, grad_beta_w, grad_decay_w = sum_v.finish(
        functools.partial(mix_out_kernel, True), "mix_out",
        [shaped((wide, width_k), F32), shaped((betas, wide), F32), shaped((heads, wide), F32)],
    )
    grad_k_w, grad_q_w = sum_kq.finish(
        functools.partial(mix_out_kernel, False), "mix_out",
        [shaped((wide, width_k), F32), shaped((wide, width_q), F32)],
    )
    grad_gate_w, grad_up_w, grad_down_w = (
        feed_sums[k * units : (k + 1) * units].astype(F32) for k in range(3)
    )
    rate, shift = small_sums[taps, betas : betas + heads], small_sums[taps, LANES + betas : LANES + betas + heads]
    return (
        output, grad_input, gains[0, :wide], grad_q_w, grad_k_w, grad_v_w,
        small_sums[:taps, cut_q], small_sums[:taps, cut_k], small_sums[:taps, cut_v],
        grad_beta_w.T, grad_decay_w.T, rate, shift, grad_outgate_w, grad_o_gain[0], grad_out_w, gains[1, :wide],
        grad_gate_w.T, grad_up_w.T, grad_down_w,
    )


def solution(mesh):
    placed = (
        P("seq", None), P(), P(), P(None, "head"), P(None, "head"), P(None, "head"), P(None, "head"),
        P(None, "head"), P(None, "head"), P(None, "head"), P(None, "head"), P("head"), P("head"),
        P(None, "head"), P(), P("head", None), P(), P(None, "head"), P(None, "head"), P("head", None),
        P("seq", None),
    )
    given = (
        P("seq", None), P("seq", None), P(), P(None, "head"), P(None, "head"), P(None, "head"),
        P(None, "head"), P(None, "head"), P(None, "head"), P(None, "head"), P(None, "head"), P("head"),
        P("head"), P(None, "head"), P(), P("head", None), P(), P(None, "head"), P(None, "head"),
        P("head", None),
    )
    return jax.shard_map(local, mesh=mesh, in_specs=placed, out_specs=given, check_vma=False)
```

```python
import functools
import math
import jax
import jax.numpy as jnp
from jax import lax
from jax.experimental import pallas as pl
from jax.experimental.pallas import tpu as pltpu
from jax.sharding import PartitionSpec as P

NH = 2
GROUP = 64
LANES = 128
EPSILON = 1e-06
BF = jnp.bfloat16
F32 = jnp.float32
VMEM = pltpu.VMEM
HBM = pltpu.HBM
VMEM_LIMIT = 60 * 1024 * 1024
SMALL_LIMIT = 24 * 1024 * 1024
EARLY = 16
SEQ = ("far", "near")


def seq_index():
    return lax.axis_index("far") * 2 + lax.axis_index("near")


def seq_size():
    return lax.axis_size("far") * lax.axis_size("near")


def mm(left, right):
    return jnp.dot(left.astype(BF), right.astype(BF), preferred_element_type=F32)


def mm_nt(left, right):
    return lax.dot_general(
        left.astype(BF), right.astype(BF), (((1,), (1,)), ((), ())), preferred_element_type=F32
    )


def mm_tn(left, right):
    return lax.dot_general(
        left.astype(BF), right.astype(BF), (((0,), (0,)), ((), ())), preferred_element_type=F32
    )


def mm_exact(left, right):
    return jnp.dot(left, right, preferred_element_type=F32, precision=lax.Precision.HIGHEST)


def sigmoid(values):
    return 1.0 / (1.0 + jnp.exp(-values))


def softplus(values):
    return jnp.maximum(values, 0.0) + jnp.log1p(jnp.exp(-jnp.abs(values)))


def documents_at(starts, positions):
    total = jnp.zeros(positions.shape, jnp.int32)
    for k in range(starts.shape[0]):
        total = total + (starts[k] <= positions).astype(jnp.int32)
    return total


def sub_order(index):
    return NH * (index % GROUP) + index // GROUP


def order_pair():
    rows = sub_order(lax.broadcasted_iota(jnp.int32, (LANES, LANES), 0))
    cols = sub_order(lax.broadcasted_iota(jnp.int32, (LANES, LANES), 1))
    return rows, cols


def gate_columns(small, log_rate, bias, heads):
    lane = lax.broadcasted_iota(jnp.int32, (1, LANES), 1)
    rate = jnp.zeros((1, LANES), F32)
    shift = jnp.zeros((1, LANES), F32)
    for h in range(heads):
        at = lane == NH * heads + h
        rate = jnp.where(at, -jnp.exp(jnp.full((1, LANES), log_rate[h], F32)), rate)
        shift = jnp.where(at, bias[h], shift)
    return sigmoid(small), rate * softplus(small + shift), small + shift, rate


def chunk_decays(rows, cols_ref, row_ref, doc_ref, c, h, heads, doc_before):
    cum_col = cols_ref[rows, NH * heads + h : NH * heads + h + 1]
    doc_col = doc_ref[rows, 0:1]
    packed = row_ref[c]
    cum_row = packed[NH * heads + h : NH * heads + h + 1, :]
    doc_row = packed[NH * heads + heads : NH * heads + heads + 1, :]
    token_row = lax.broadcasted_iota(jnp.int32, (GROUP, LANES), 1) % GROUP
    token_col = lax.broadcasted_iota(jnp.int32, (GROUP, LANES), 0)
    seen = (token_col >= token_row) & (doc_col == doc_row)
    pair = jnp.where(seen, jnp.exp(jnp.where(seen, cum_col - cum_row, 0.0)), 0.0)
    start = jnp.where(doc_col == doc_before, jnp.exp(cum_col), 0.0)
    cum_last = cum_col[GROUP - 1 :, :]
    doc_last = doc_col[GROUP - 1 :, :]
    to_end = jnp.where(doc_col == doc_last, jnp.exp(cum_last - cum_col), 0.0)
    return pair, start, to_end


def two(array):
    return jnp.concatenate([array, array], axis=0)


def beta_pair(rows, cols_ref, row_ref, c, h):
    lane = lax.broadcasted_iota(jnp.int32, (1, LANES), 1)
    packed = row_ref[c]
    row = jnp.where(lane < GROUP, packed[NH * h : NH * h + 1, :], packed[NH * h + 1 : NH * h + 2, :])
    col = jnp.concatenate(
        [cols_ref[rows, NH * h : NH * h + 1], cols_ref[rows, NH * h + 1 : NH * h + 2]], axis=0
    )
    return row, col


def copies(pairs, sems, first=0):
    return [
        pltpu.make_async_copy(source, target, sems.at[first + k]) for k, (source, target) in enumerate(pairs)
    ]


def begin(waiting):
    for copy in waiting:
        copy.start()
    return waiting


def end(waiting):
    for copy in waiting:
        copy.wait()


def prep_kernel(
    heads, starts, log_rate, bias, far_proj, halo, conv_q, conv_k, conv_v, far_small,
    out_aug, far_state_aug, far_wy_k, far_wy_v, far_inverse, far_step_p, far_query_map, far_keys, far_queries,
    far_conv_total, far_cols, far_doc, far_row,
    final_state, final_map,
    proj, small, state_aug, wy_k, wy_v, inverse, step_p, query_map, keys, queries, conv_total, cols, doc, row,
    ext, vals, score_map, step_b, masks, sems,
):
    arriving = begin(copies([(far_small, small), (far_proj, proj)], sems))
    tokens = proj.shape[0]
    chunks = tokens // GROUP
    first = seq_index() * tokens
    lead = 8
    lower_r = lax.broadcasted_iota(jnp.int32, (LANES, LANES), 0)
    lower_c = lax.broadcasted_iota(jnp.int32, (LANES, LANES), 1)
    lower = ((lower_r >= lower_c) & (lower_r // GROUP == lower_c // GROUP)).astype(F32)
    lane = lax.broadcasted_iota(jnp.int32, (LANES, LANES), 1)
    per = LANES // GROUP
    end(arriving[:1])
    for block in range(tokens // LANES):
        at = pl.ds(block * LANES, LANES)
        betas, logdec, _, _ = gate_columns(small[at, :], log_rate, bias, heads)
        cum = mm_exact(lower, logdec)
        where = lax.broadcasted_iota(jnp.int32, (LANES, LANES), 0) + (first + block * LANES)
        document = documents_at(starts, where).astype(F32)
        packed = jnp.where(lane < NH * heads, betas, jnp.where(lane < NH * heads + heads, cum, document))
        cols[at, :] = packed
        doc[at, :] = document
        turned = packed.T
        for part in range(per):
            piece = turned[0:8, part * GROUP : (part + 1) * GROUP]
            row[block * per + part] = jnp.concatenate([piece] * NH, axis=1)
    order_r, order_c = order_pair()
    level = 0
    width = 1
    while width < LANES:
        inside = (order_r // (2 * width) == order_c // (2 * width)) & (order_r // width > order_c // width)
        masks[level] = inside.astype(F32)
        level += 1
        width *= 2
    end(arriving[1:])
    ext[0:lead, :] = halo[16 - lead : 16, :].astype(F32)
    ext[lead:, :] = proj[...].astype(F32)
    width_q = heads * LANES
    width_k = NH * heads * LANES
    taps = conv_q.shape[0]

    def conv_chunk(c, _):
        base = pl.multiple_of(c * GROUP, GROUP)
        rows = pl.ds(base, GROUP)
        position = lax.broadcasted_iota(jnp.int32, (GROUP, LANES), 0) + (first + base)
        document = doc[rows, :]
        kept = [
            (documents_at(starts, position - lag).astype(F32) == document).astype(F32) for lag in range(1, taps)
        ]
        for group in range((width_q + 2 * width_k) // LANES):
            at = slice(group * LANES, (group + 1) * LANES)
            if group * LANES < width_q:
                kernel, shift = conv_q, 0
            elif group * LANES < width_q + width_k:
                kernel, shift = conv_k, width_q
            else:
                kernel, shift = conv_v, width_q + width_k
            cut = slice(at.start - shift, at.stop - shift)
            window = ext[pl.ds(base, GROUP + lead), at]
            total = kernel[taps - 1 : taps, cut] * window[lead:, :]
            for lag in range(1, taps):
                total += kernel[taps - 1 - lag : taps - lag, cut] * window[lead - lag : lead - lag + GROUP, :] * kept[lag - 1]
            conv_total[rows, at] = total
            active = total * sigmoid(total)
            if group * LANES < width_q:
                unit = active * lax.rsqrt(jnp.sum(active * active, axis=1, keepdims=True) + EPSILON)
                queries[group, c] = (unit * LANES ** (-0.5)).astype(BF)
            elif group * LANES < width_q + width_k:
                piece = group - width_q // LANES
                unit = active * lax.rsqrt(jnp.sum(active * active, axis=1, keepdims=True) + EPSILON)
                keys[piece // NH, c, (piece % NH) * GROUP : (piece % NH + 1) * GROUP] = unit.astype(BF)
            else:
                piece = group - (width_q + width_k) // LANES
                vals[piece // NH, c, (piece % NH) * GROUP : (piece % NH + 1) * GROUP] = active.astype(BF)
        return 0

    lax.fori_loop(0, chunks, conv_chunk, 0)
    leaving = begin(
        copies(
            [
                (conv_total, far_conv_total), (keys, far_keys), (queries, far_queries),
                (cols, far_cols), (doc, far_doc), (row, far_row),
            ],
            sems, 2,
        )
    )

    strict = order_r > order_c
    eye = (lower_r == lower_c).astype(F32)
    together = 2

    def part_chunks(step, _):
        jobs = []
        for k in range(together):
            c = step * together + k
            rows = pl.ds(pl.multiple_of(c * GROUP, GROUP), GROUP)
            before = documents_at(starts, jnp.full((1, 1), first + c * GROUP - 1, jnp.int32)).astype(F32)
            for h in range(heads):
                pair, start, to_end = chunk_decays(rows, cols, row, doc, c, h, heads, before)
                beta_row, beta_col = beta_pair(rows, cols, row, c, h)
                key = keys[h, c]
                query = queries[h, c]
                grams = mm_nt(jnp.concatenate([key, query], axis=0), key)
                system = jnp.where(strict, grams[:LANES] * two(pair), 0.0) * beta_row
                scores = grams[LANES:] * pair * beta_row
                jobs.append((c, h, start, to_end, beta_col, key, query, system, scores))
        inverses = [eye - job[7] * masks[0] for job in jobs]
        for n in range(1, level):
            halves = [mm(job[7] * masks[n], inv) for job, inv in zip(jobs, inverses)]
            inverses = [inv - mm(inv, half) for inv, half in zip(inverses, halves)]
        for job, inv in zip(jobs, inverses):
            c, h, start, to_end, beta_col, key, query, system, scores = job
            low_inv = inv.astype(BF)
            inverse[h, c] = low_inv
            key_f = key.astype(F32)
            both = mm(low_inv, jnp.concatenate([(two(start) * key_f).astype(BF), vals[h, c]], axis=1)).astype(BF)
            wy_k[h, c] = both[:, :LANES]
            wy_v[h, c] = both[:, LANES:]
            carried = (beta_col * two(to_end) * key_f).astype(BF)
            ahead = mm_tn(carried, both)
            step_p[h, c] = ahead[:, :LANES].astype(BF)
            step_b[h, c] = ahead[:, LANES:]
            scored = mm(scores, both)
            query_map[h, c] = (start * query.astype(F32) - scored[:, :LANES]).astype(BF)
            score_map[h, c] = scored[:, LANES:]
        return 0

    lax.fori_loop(0, chunks // together, part_chunks, 0)
    leaving += begin(
        copies(
            [
                (wy_k, far_wy_k), (wy_v, far_wy_v), (inverse, far_inverse), (step_p, far_step_p),
                (query_map, far_query_map),
            ],
            sems, 8,
        )
    )

    zero = jnp.zeros((LANES, LANES), F32)

    def advance(c, carry):
        rows = pl.ds(pl.multiple_of(c * GROUP, GROUP), GROUP)
        before = documents_at(starts, jnp.full((1, 1), first + c * GROUP - 1, jnp.int32)).astype(F32)
        new = []
        for h in range(heads):
            state = carry[h]
            low_state = state.astype(BF)
            state_aug[h, c] = low_state
            last = cols[rows, NH * heads + h : NH * heads + h + 1][GROUP - 1 :, :]
            whole = jnp.where(doc[rows, 0:1][GROUP - 1 :, :] == before, jnp.exp(last), 0.0)
            new.append(
                whole * state - mm(step_p[h, c], low_state) + jnp.concatenate([step_b[h, c], zero], axis=1)
            )
            mapped = mm(query_map[h, c], low_state)
            out_aug[h, rows, :] = jnp.concatenate([mapped[:, :LANES] + score_map[h, c], mapped[:, LANES:]], axis=1)
        return tuple(new)

    initial = jnp.concatenate([zero, eye], axis=1)
    last = lax.fori_loop(0, chunks, advance, (initial,) * heads)
    leaving += begin(copies([(state_aug, far_state_aug)], sems, 13))
    for h in range(heads):
        final_state[h] = last[h][:, :LANES].astype(final_state.dtype)
        final_map[h] = last[h][:, LANES:].astype(final_map.dtype)
    end(leaving)


def specs(count, space=None):
    return [pl.BlockSpec(memory_space=space or pltpu.VMEM)] * count


def mixer_prep(starts, log_rate, bias, proj, halo, conv_q, conv_k, conv_v, small):
    tokens, width = proj.shape
    heads = log_rate.shape[0]
    chunks = tokens // GROUP
    square = (heads, chunks, LANES, LANES)
    shape = jax.ShapeDtypeStruct
    outs = [
        shape((heads, tokens, 2 * LANES), F32),
        shape((heads, chunks, LANES, 2 * LANES), BF),
        shape(square, BF),
        shape(square, BF),
        shape(square, BF),
        shape(square, BF),
        shape((heads, chunks, GROUP, LANES), BF),
        shape(square, BF),
        shape((heads, chunks, GROUP, LANES), BF),
        shape((tokens, width), F32),
        shape((tokens, LANES), F32),
        shape((tokens, LANES), F32),
        shape((chunks, 8, LANES), F32),
        shape((heads, LANES, LANES), BF),
        shape((heads, LANES, LANES), BF),
    ]
    return pl.pallas_call(
        functools.partial(prep_kernel, heads),
        out_shape=outs,
        in_specs=specs(3, pltpu.SMEM) + specs(1, HBM) + specs(4) + specs(1, HBM),
        out_specs=specs(1) + specs(12, HBM) + specs(2),
        scratch_shapes=[VMEM(proj.shape, BF), VMEM(small.shape, F32)]
        + [VMEM(out.shape, out.dtype) for out in outs[1:13]]
        + [
            VMEM((tokens + 8, width), F32),
            VMEM(square, BF),
            VMEM((heads, chunks, GROUP, LANES), F32),
            VMEM(square, F32),
            VMEM((8, LANES, LANES), F32),
            pltpu.SemaphoreType.DMA((14,)),
        ],
        compiler_params=pltpu.CompilerParams(vmem_limit_bytes=VMEM_LIMIT),
        cost_estimate=pl.CostEstimate(flops=24_000_000_000, bytes_accessed=4_000_000, transcendentals=0),
        name="mixer_prep",
    )(starts, log_rate, bias, proj, halo, conv_q, conv_k, conv_v, small)


def back_kernel(
    heads, reach, starts, log_rate, bias, far_proj, halo, conv_q, conv_k, conv_v, far_small,
    far_state_aug, far_wy_k, far_wy_v, far_inverse, far_step_p, far_query_map, far_keys, far_queries,
    far_conv_total, far_cols, far_doc, far_row, state_in, d_mixed, *rest,
):
    after = rest[:reach]
    later = rest[reach : 2 * reach - 1]
    (
        d_kq, d_v, tail, d_halo, d_small, d_taps, d_scalars,
        proj, small, state_aug, wy_k, wy_v, inverse, step_p, query_map, keys, queries, conv_total, cols, doc, row,
        ext, state_grads, d_query, d_key, d_value, col_grads, row_grads, d_total, sems,
    ) = rest[2 * reach - 1 :]
    arriving = begin(
        copies(
            [
                (far_step_p, step_p), (far_query_map, query_map), (far_cols, cols), (far_doc, doc), (far_row, row),
                (far_state_aug, state_aug), (far_wy_k, wy_k), (far_wy_v, wy_v), (far_inverse, inverse),
                (far_keys, keys), (far_queries, queries),
                (far_small, small), (far_conv_total, conv_total), (far_proj, proj),
            ],
            sems,
        )
    )
    tokens = proj.shape[0]
    chunks = tokens // GROUP
    first = seq_index() * tokens
    lead = 8
    lane = lax.broadcasted_iota(jnp.int32, (GROUP, LANES), 1)

    def document_before(c):
        return documents_at(starts, jnp.full((1, 1), first + c * GROUP - 1, jnp.int32)).astype(F32)

    def whole_decay(c, h):
        at = pl.ds(pl.multiple_of(c * GROUP, GROUP) + GROUP - 8, 8)
        last = cols[at, NH * heads + h : NH * heads + h + 1][7:8, :]
        return jnp.where(doc[at, 0:1][7:8, :] == document_before(c), jnp.exp(last), 0.0)

    at_end = []
    for h in range(heads):
        state = after[reach - 1][h].astype(F32)
        for r in range(reach - 2, -1, -1):
            state = mm_tn(later[r][h], state) + after[r][h].astype(F32)
        at_end.append(state)
    end(arriving[:5])

    def retreat(step, carry):
        c = chunks - 1 - step
        rows = pl.ds(pl.multiple_of(c * GROUP, GROUP), GROUP)
        new = []
        for h in range(heads):
            low_state = carry[h].astype(BF)
            state_grads[h, c] = low_state
            new.append(
                whole_decay(c, h) * carry[h]
                - mm_tn(step_p[h, c], low_state)
                + mm_tn(query_map[h, c], d_mixed[rows, h * LANES : (h + 1) * LANES])
            )
        return tuple(new)

    lax.fori_loop(0, chunks, retreat, tuple(at_end))
    end(arriving[5:11])

    order_r, order_c = order_pair()
    strict = order_r > order_c
    together = 2
    last_token = lax.broadcasted_iota(jnp.int32, (GROUP, 1), 0) == GROUP - 1

    def chunk_back(step, _):
        for k in range(together):
            c = step * together + k
            rows = pl.ds(pl.multiple_of(c * GROUP, GROUP), GROUP)
            before = document_before(c)
            col_acc = jnp.zeros((GROUP, LANES), F32)
            row_acc = []
            row_beta = []
            for h in range(heads):
                pair, start, to_end = chunk_decays(rows, cols, row, doc, c, h, heads, before)
                beta_row, beta_col = beta_pair(rows, cols, row, c, h)
                key = keys[h, c]
                query = queries[h, c]
                key_f = key.astype(F32)
                query_f = query.astype(F32)
                d_out = d_mixed[rows, h * LANES : (h + 1) * LANES]
                d_state = state_grads[h, c]
                both = state_aug[h, c]
                state = both[:, :LANES].astype(F32) + mm(both[:, LANES:], state_in[h])
                low_state = state.astype(BF)
                fresh = wy_v[h, c].astype(F32) - mm(wy_k[h, c], low_state)
                grams = mm_nt(jnp.concatenate([key, query], axis=0), key)
                pair2 = two(pair)
                system = jnp.where(strict, grams[:LANES] * pair2, 0.0)
                scores = grams[LANES:] * pair
                key_end = two(to_end) * key_f
                key_start = two(start) * key_f
                d_wide = mm_tn(scores, d_out) + mm(key_end, d_state)
                solved = mm_tn(inverse[h, c], beta_col * d_wide)
                d_value[h, c] = solved
                low_fresh = fresh.astype(BF)
                crossed = mm_nt(
                    jnp.concatenate([solved.astype(BF), d_out], axis=0),
                    jnp.concatenate([low_fresh, low_state], axis=0),
                )
                pairs = jnp.where(strict, crossed[:LANES, :LANES], 0.0)
                solved_state = crossed[:LANES, LANES:]
                out_state = crossed[LANES:, LANES:]
                fresh_grad = mm_nt(beta_col * fresh, d_state)
                system_pairs = system * pairs
                decayed = -(system_pairs * beta_row)
                gram_grad = -(pairs * pair2 * beta_row)
                score_grad = crossed[LANES:, :LANES] * beta_row
                query_key = score_grad * pair
                score_decay = score_grad * scores
                stacked = jnp.concatenate([gram_grad, query_key], axis=0).astype(BF)
                direct = mm(stacked, key)
                turned = mm_tn(stacked, jnp.concatenate([key, query], axis=0))
                d_key[h, c] = direct[:LANES] + turned - two(start) * solved_state + two(to_end) * fresh_grad
                d_query[h, c] = direct[LANES:] + start * out_state
                ending = key_end * fresh_grad
                parts = decayed - key_start * solved_state - ending
                parts = parts[:GROUP] + parts[GROUP:] + score_decay + (start * query_f) * out_state
                last_grad = jnp.sum(ending, keepdims=True) + whole_decay(c, h) * jnp.sum(
                    state * d_state.astype(F32), keepdims=True
                )
                decay_col = jnp.sum(parts, axis=1, keepdims=True) + jnp.where(last_token, last_grad, 0.0)
                beta_sum = jnp.sum(d_wide * fresh, axis=1, keepdims=True)
                col_acc = jnp.where(lane == NH * heads + h, decay_col, col_acc)
                for s in range(NH):
                    col_acc = jnp.where(lane == NH * h + s, beta_sum[s * GROUP : (s + 1) * GROUP], col_acc)
                beta_row_sum = jnp.sum(system_pairs, axis=0, keepdims=True)
                row_beta.append(-beta_row_sum)
                row_acc.append(beta_row * beta_row_sum - jnp.sum(score_decay, axis=0, keepdims=True))
            col_grads[rows, :] = col_acc
            row_grads[c] = jnp.concatenate(
                row_acc + row_beta + [jnp.zeros((8 - 2 * heads, LANES), F32)], axis=0
            )
        return 0

    lax.fori_loop(0, chunks // together, chunk_back, 0)

    end(arriving[11:])

    lower_r = lax.broadcasted_iota(jnp.int32, (LANES, LANES), 0)
    lower_c = lax.broadcasted_iota(jnp.int32, (LANES, LANES), 1)
    upper = ((lower_r <= lower_c) & (lower_r // GROUP == lower_c // GROUP)).astype(F32)
    per = LANES // GROUP
    scalar_decay = jnp.zeros((1, LANES), F32)
    scalar_rate = jnp.zeros((1, LANES), F32)
    wide = lax.broadcasted_iota(jnp.int32, (LANES, LANES), 1)
    for block in range(tokens // LANES):
        at = pl.ds(block * LANES, LANES)
        pieces = []
        for part in range(per):
            c = block * per + part
            turned = jnp.concatenate([row_grads[c], jnp.zeros((LANES - 8, LANES), F32)], axis=0).T
            piece = jnp.zeros((GROUP, LANES), F32)
            for h in range(heads):
                decay_col = turned[:GROUP, h : h + 1] + turned[GROUP:, h : h + 1]
                piece = jnp.where(lane == NH * heads + h, decay_col, piece)
                for s in range(NH):
                    beta_col = turned[s * GROUP : (s + 1) * GROUP, heads + h : heads + h + 1]
                    piece = jnp.where(lane == NH * h + s, beta_col, piece)
            pieces.append(piece)
        grads = col_grads[at, :] + jnp.concatenate(pieces, axis=0)
        d_logdec = mm_exact(upper, grads)
        betas, logdec, argument, rate = gate_columns(small[at, :], log_rate, bias, heads)
        d_argument = d_logdec * rate * sigmoid(argument)
        scalar_rate += jnp.sum(d_logdec * logdec, axis=0, keepdims=True)
        scalar_decay += jnp.sum(d_argument, axis=0, keepdims=True)
        d_small[at, :] = jnp.where(
            wide < NH * heads,
            grads * betas * (1.0 - betas),
            jnp.where(wide < NH * heads + heads, d_argument, 0.0),
        ).astype(BF)
    d_scalars[...] = jnp.concatenate([scalar_rate, scalar_decay, jnp.zeros((6, LANES), F32)], axis=0)

    ext[0:lead, :] = halo[16 - lead : 16, :].astype(F32)
    ext[lead:, :] = proj[...].astype(F32)
    width_q = heads * LANES
    width_k = NH * heads * LANES
    width = width_q + 2 * width_k
    taps = conv_q.shape[0]
    d_taps[...] = jnp.zeros(d_taps.shape, F32)
    d_total[tokens:, :] = jnp.zeros((8, width), F32)

    def kernel_of(group):
        if group * LANES < width_q:
            return conv_q, slice(group * LANES, (group + 1) * LANES)
        if group * LANES < width_q + width_k:
            return conv_k, slice(group * LANES - width_q, (group + 1) * LANES - width_q)
        return conv_v, slice(group * LANES - width_q - width_k, (group + 1) * LANES - width_q - width_k)

    def active_back(c, _):
        base = pl.multiple_of(c * GROUP, GROUP)
        rows = pl.ds(base, GROUP)
        position = lax.broadcasted_iota(jnp.int32, (GROUP, LANES), 0) + (first + base)
        document = doc[rows, :]
        kept = [
            (documents_at(starts, position - lag).astype(F32) == document).astype(F32) for lag in range(1, taps)
        ]
        for group in range(width // LANES):
            at = slice(group * LANES, (group + 1) * LANES)
            total = conv_total[rows, at]
            sg = sigmoid(total)
            if group * LANES < width_q + width_k:
                active = total * sg
                scale = lax.rsqrt(jnp.sum(active * active, axis=1, keepdims=True) + EPSILON)
                unit = active * scale
                if group * LANES < width_q:
                    grad = d_query[group, c] * LANES ** (-0.5)
                else:
                    piece = group - width_q // LANES
                    grad = d_key[piece // NH, c, (piece % NH) * GROUP : (piece % NH + 1) * GROUP]
                grad = scale * (grad - unit * jnp.sum(unit * grad, axis=1, keepdims=True))
            else:
                piece = group - (width_q + width_k) // LANES
                grad = d_value[piece // NH, c, (piece % NH) * GROUP : (piece % NH + 1) * GROUP]
            grad = grad * (sg * (1.0 + total * (1.0 - sg)))
            d_total[rows, at] = grad
            window = ext[pl.ds(base, GROUP + lead), at]
            sums = []
            for j in range(taps):
                lag = taps - 1 - j
                term = grad * window[lead - lag : lead - lag + GROUP, :]
                if lag > 0:
                    term = term * kept[lag - 1]
                sums.append(jnp.sum(term, axis=0, keepdims=True))
            d_taps[0:taps, at] += jnp.concatenate(sums, axis=0)
        return 0

    lax.fori_loop(0, chunks, active_back, 0)

    def conv_back(c, _):
        base = pl.multiple_of(c * GROUP, GROUP)
        rows = pl.ds(base, GROUP)
        position = lax.broadcasted_iota(jnp.int32, (GROUP, LANES), 0) + (first + base)
        document = doc[rows, :]
        kept = [
            (documents_at(starts, position + lag).astype(F32) == document).astype(F32) for lag in range(1, taps)
        ]
        for group in range(width // LANES):
            at = slice(group * LANES, (group + 1) * LANES)
            kernel, cut = kernel_of(group)
            window = d_total[pl.ds(base, GROUP + lead), at]
            grad = kernel[taps - 1 : taps, cut] * window[:GROUP]
            for lag in range(1, taps):
                grad += kernel[taps - 1 - lag : taps - lag, cut] * kept[lag - 1] * window[lag : lag + GROUP]
            target = d_v if kernel is conv_v else d_kq
            shift = width_k if kernel is conv_q else 0
            target[rows, cut.start + shift : cut.stop + shift] = grad.astype(BF)
            tail[:, at] = grad[GROUP - 16 :]
        return 0

    lax.fori_loop(0, chunks, conv_back, 0)
    position = lax.broadcasted_iota(jnp.int32, (8, LANES), 0) + (first - 8)
    document = documents_at(starts, position)
    for group in range(width // LANES):
        at = slice(group * LANES, (group + 1) * LANES)
        kernel, cut = kernel_of(group)
        window = jnp.concatenate([jnp.zeros((8, LANES), F32), d_total[0:8, at]], axis=0)
        grad = jnp.zeros((8, LANES), F32)
        for lag in range(1, taps):
            kept = (documents_at(starts, position + lag) == document).astype(F32)
            grad += kernel[taps - 1 - lag : taps - lag, cut] * kept * window[lag : lag + 8]
        d_halo[:, at] = grad


def mixer_back(starts, log_rate, bias, proj, halo, conv_q, conv_k, conv_v, small, saved, state_in, d_mixed, after, later):
    tokens, width = proj.shape
    heads = log_rate.shape[0]
    chunks = tokens // GROUP
    reach = len(after)
    square = (heads, chunks, LANES, LANES)
    shape = jax.ShapeDtypeStruct
    outs = [
        shape((tokens, conv_k.shape[1] + conv_q.shape[1]), BF),
        shape((tokens, conv_v.shape[1]), BF),
        shape((16, width), F32),
        shape((8, width), F32),
        shape((tokens, LANES), BF),
        shape((8, width), F32),
        shape((8, LANES), F32),
    ]
    operands = [starts, log_rate, bias, proj, halo, conv_q, conv_k, conv_v, small, *saved, state_in, d_mixed, *after, *later]
    return pl.pallas_call(
        functools.partial(back_kernel, heads, reach),
        out_shape=outs,
        in_specs=specs(3, pltpu.SMEM) + specs(1, HBM) + specs(4) + specs(13, HBM) + specs(len(operands) - 21),
        out_specs=specs(len(outs)),
        scratch_shapes=[VMEM(a.shape, a.dtype) for a in (proj, small, *saved)]
        + [
            VMEM((tokens + 8, width), F32),
            VMEM(square, BF),
            VMEM((heads, chunks, GROUP, LANES), F32),
            VMEM(square, F32),
            VMEM(square, F32),
            VMEM((tokens, LANES), F32),
            VMEM((chunks, 8, LANES), F32),
            VMEM((tokens + 8, width), F32),
            pltpu.SemaphoreType.DMA((14,)),
        ],
        compiler_params=pltpu.CompilerParams(vmem_limit_bytes=VMEM_LIMIT),
        cost_estimate=pl.CostEstimate(flops=2_000_000_000, bytes_accessed=4_000_000, transcendentals=0),
        name="mixer_back",
    )(*operands)


def call(kernel, name, outs, operands, smem=0, scratch=(), flops=0, limit=SMALL_LIMIT):
    moved = sum(a.size * a.dtype.itemsize for a in operands) + sum(
        math.prod(o.shape) * jnp.dtype(o.dtype).itemsize for o in outs
    )
    return pl.pallas_call(
        kernel,
        out_shape=outs,
        in_specs=specs(smem, pltpu.SMEM) + specs(len(operands) - smem),
        out_specs=specs(len(outs)),
        scratch_shapes=list(scratch),
        compiler_params=pltpu.CompilerParams(vmem_limit_bytes=limit),
        cost_estimate=pl.CostEstimate(flops=flops // EARLY, bytes_accessed=moved // EARLY, transcendentals=0),
        name=name,
    )(*operands)


def shaped(dims, kind):
    return jax.ShapeDtypeStruct(dims, kind)


def half_rows(ref, own):
    half = ref.shape[0] // 2
    low = lax.axis_index("head") % 2
    return pl.ds(pl.multiple_of((low if own else 1 - low) * half, half), half)


def seq_bits():
    at = seq_index()
    z = at // 2 % 4
    low, high = z % 2, z // 2
    return {"x": at % 2, "pair": low ^ high, "cross": high}


PARTNER = {"x": 1, "pair": 2, "cross": 6}
X_FIRST = ("x", "pair", "cross")
Z_FIRST = ("pair", "cross", "x")


def half_width(ref, own, stage="x"):
    half = ref.shape[1] // 2
    low = seq_bits()[stage]
    return pl.ds(pl.multiple_of((low if own else 1 - low) * half, half), half)


def project_kernel(
    far_x, gain, far_q, far_k, far_v, far_gate, beta_w, decay_w, far_normed, far_projected, far_outgate, far_small, edge,
    x, q_w, k_w, v_w, gate_w, normed, projected, outgate, small, side_w, sems,
):
    arriving = begin(
        copies([(far_x, x), (far_q, q_w), (far_k, k_w), (far_v, v_w), (far_gate, gate_w)], sems)
    )
    gather_side(side_w, beta_w, decay_w)
    end(arriving[:1])
    x_float = x[...].astype(F32)
    low = (x_float * lax.rsqrt(jnp.mean(x_float * x_float, axis=1, keepdims=True) + EPSILON) * gain[...]).astype(BF)
    normed[...] = low
    leaving = begin(copies([(normed, far_normed)], sems, 5))
    last = x.shape[0] - edge.shape[0]
    small[...] = mm_nt(low, side_w[...])
    leaving += begin(copies([(small, far_small)], sems, 6))
    at = 0
    for k, weight in enumerate((q_w, k_w, v_w)):
        end(arriving[1 + k : 2 + k])
        piece = mm(low, weight[...]).astype(BF)
        projected[:, at : at + weight.shape[1]] = piece
        edge[:, at : at + weight.shape[1]] = piece[last:, :]
        at += weight.shape[1]
    edge[:, at:] = low[last:, :]
    leaving += begin(copies([(projected, far_projected)], sems, 7))
    end(arriving[4:])
    outgate[...] = mm(low, gate_w[...])
    leaving += begin(copies([(outgate, far_outgate)], sems, 8))
    end(leaving)


def gather_side(side_w, beta_w, decay_w):
    betas = beta_w.shape[0]
    side_w[...] = jnp.zeros(side_w.shape, F32)
    side_w[0:betas, :] = beta_w[...].astype(F32)
    side_w[betas : betas + decay_w.shape[0], :] = decay_w[...].astype(F32)


def project(x, gain, q_w, k_w, v_w, gate_w, beta_w, decay_w):
    tokens, wide = x.shape
    width = q_w.shape[1] + k_w.shape[1] + v_w.shape[1]
    outs = [
        shaped((tokens, wide), BF), shaped((tokens, width), BF),
        shaped((tokens, gate_w.shape[1]), F32), shaped((tokens, LANES), F32), shaped((16, width + wide), BF),
    ]
    operands = [x, gain.reshape(1, -1), q_w, k_w, v_w, gate_w, beta_w, decay_w]
    moved = 8 * x.size
    return pl.pallas_call(
        project_kernel,
        out_shape=outs,
        in_specs=specs(1, HBM) + specs(1) + specs(4, HBM) + specs(2),
        out_specs=specs(4, HBM) + specs(1),
        scratch_shapes=[VMEM(a.shape, a.dtype) for a in (x, q_w, k_w, v_w, gate_w)]
        + [VMEM(out.shape, out.dtype) for out in outs[:4]]
        + [VMEM((LANES, wide), F32), pltpu.SemaphoreType.DMA((9,))],
        compiler_params=pltpu.CompilerParams(vmem_limit_bytes=VMEM_LIMIT),
        cost_estimate=pl.CostEstimate(flops=8 * tokens * wide * width, bytes_accessed=moved, transcendentals=0),
        name="project",
    )(*operands)


def attend_kernel(heads, reach, out_aug, outgate, o_gain, out_weight, *rest):
    before = rest[:reach]
    mixed, branch, give, keep, state_in = rest[reach:]
    gain = o_gain[...]
    for h in range(heads):
        at = slice(h * LANES, (h + 1) * LANES)
        state = before[reach - 1][0, h].astype(F32)
        for r in range(reach - 2, -1, -1):
            state = mm(before[r][1, h], state) + before[r][0, h].astype(F32)
        state_in[h] = state
        mix = out_aug[h, :, :LANES] + mm(out_aug[h, :, LANES:], state)
        mixed[:, at] = mix
        gate = outgate[:, at]
        normed = mix * lax.rsqrt(jnp.mean(mix * mix, axis=1, keepdims=True) + EPSILON)
        branch[:, at] = (normed * gain * (gate * sigmoid(gate))).astype(BF)
    give[...] = mm(branch[half_rows(branch, False), :], out_weight[...]).astype(BF)
    keep[...] = mm(branch[half_rows(branch, True), :], out_weight[...])


def attend(out_aug, outgate, o_gain, out_weight, before):
    heads, tokens, _ = out_aug.shape
    wide = out_weight.shape[1]
    outs = [
        shaped((tokens, heads * LANES), F32), shaped((tokens, heads * LANES), BF),
        shaped((tokens // 2, wide), BF), shaped((tokens // 2, wide), F32), shaped((heads, LANES, LANES), F32),
    ]
    operands = [out_aug, outgate, o_gain.reshape(1, -1), out_weight, *before]
    return call(
        functools.partial(attend_kernel, heads, len(before)), "attend", outs, operands,
        flops=2 * tokens * wide * heads * LANES,
    )


def enter_kernel(x, mine, other, gain, hidden, normed):
    value = x[half_rows(x, True), :].astype(F32) + mine[...].astype(F32) + other[...].astype(F32)
    hidden[...] = value
    normed[...] = (
        value * lax.rsqrt(jnp.mean(value * value, axis=1, keepdims=True) + EPSILON) * gain[...]
    ).astype(BF)


def enter(x, mine, other, gain):
    outs = [shaped(mine.shape, F32), shaped(mine.shape, BF)]
    return call(enter_kernel, "enter", outs, [x, mine, other, gain.reshape(1, -1)])


def near_units(units, own):
    near = lax.axis_index("near")
    return pl.ds(pl.multiple_of((near if own else 1 - near) * (units // 2), 16), units // 2)


def half_lanes(ref, own):
    half = ref.shape[1] // 2
    low = lax.axis_index("head") % 2
    return pl.ds(pl.multiple_of((low if own else 1 - low) * half, half), half)


def feed_kernel(
    own, other, gate_w, up_w, down_w, out_grad,
    normed, d_give, d_keep, part_give, part_keep, feed_give, feed_keep,
):
    units = gate_w.shape[0]
    half = units // 2
    for mine, source, part, fed in ((False, other, part_give, feed_give), (True, own, part_keep, feed_keep)):
        rows = half_rows(normed, mine)
        lanes = half_lanes(d_give, mine)
        low = source[...]
        normed[rows, :] = low
        part_sum = jnp.zeros(part.shape, F32)
        feed_sum = jnp.zeros(fed.shape, F32)
        for near, out in ((False, d_give), (True, d_keep)):
            cut = near_units(units, near)
            gate = mm_nt(gate_w[cut, :], low)
            up = mm_nt(up_w[cut, :], low)
            d_inner = mm_nt(down_w[cut, :], out_grad[rows, :])
            sg = sigmoid(gate)
            active = gate * sg
            low_inner = (active * up).astype(BF)
            low_gate = (d_inner * up * (sg * (1.0 + gate * (1.0 - sg)))).astype(BF)
            low_up = (d_inner * active).astype(BF)
            out[0:half, lanes] = low_gate
            out[half : 2 * half, lanes] = low_up
            out[2 * half : 3 * half, lanes] = low_inner
            part_sum += mm_tn(low_gate, gate_w[cut, :]) + mm_tn(low_up, up_w[cut, :])
            feed_sum += mm_tn(low_inner, down_w[cut, :])
        part[...] = part_sum.astype(part.dtype)
        fed[...] = feed_sum.astype(fed.dtype)


def feed(own, other, gate_w, up_w, down_w, out_grad):
    tokens, wide = out_grad.shape
    units = gate_w.shape[0]
    half = (tokens // 2, wide)
    outs = [shaped((tokens, wide), BF)] + [shaped((3 * units // 2, tokens), BF)] * 2 + [
        shaped(half, BF), shaped(half, F32), shaped(half, BF), shaped(half, F32),
    ]
    operands = [own, other, gate_w, up_w, down_w, out_grad]
    return call(feed_kernel, "feed", outs, operands, flops=12 * tokens * wide * units)


def leave_kernel(mine, other, hidden, gain, out_grad, d_hidden, low, d_gain):
    grad = mine[...].astype(F32) + other[...].astype(F32)
    value = hidden[...]
    scale = lax.rsqrt(jnp.mean(value * value, axis=1, keepdims=True) + EPSILON)
    unit = value * scale
    d_gain[...] = jnp.sum(grad * unit, axis=0, keepdims=True)
    d_unit = grad * gain[...]
    total = out_grad[half_rows(out_grad, True), :].astype(F32) + scale * (
        d_unit - unit * jnp.mean(d_unit * unit, axis=1, keepdims=True)
    )
    d_hidden[...] = total
    low[...] = total.astype(BF)


def leave(mine, other, hidden, gain, out_grad):
    outs = [shaped(mine.shape, F32), shaped(mine.shape, BF), shaped((1, mine.shape[1]), F32)]
    return call(leave_kernel, "leave", outs, [mine, other, hidden, gain.reshape(1, -1), out_grad])


def finish_kernel(mine, other, x, gain, d_hidden, low, d_gain):
    grad = mine[...].astype(F32) + other[...].astype(F32)
    value = x[half_rows(x, True), :].astype(F32)
    scale = lax.rsqrt(jnp.mean(value * value, axis=1, keepdims=True) + EPSILON)
    unit = value * scale
    d_gain[...] = jnp.sum(grad * unit, axis=0, keepdims=True)
    d_unit = grad * gain[...]
    low[...] = (
        d_hidden[...] + scale * (d_unit - unit * jnp.mean(d_unit * unit, axis=1, keepdims=True))
    ).astype(BF)


def finish(mine, other, x, gain, d_hidden):
    outs = [shaped(mine.shape, BF), shaped((1, mine.shape[1]), F32)]
    return call(finish_kernel, "finish", outs, [mine, other, x, gain.reshape(1, -1), d_hidden])


def attend_back_kernel(
    heads, own, other, out_weight, mixed, outgate, o_gain, out_aug,
    grad, d_mixed, d_outgate, d_gain, carry,
):
    gain = o_gain[...]
    gain_sum = jnp.zeros((1, LANES), F32)
    carries = [jnp.zeros((LANES, LANES), F32)] * heads
    for mine, source in ((True, own), (False, other)):
        rows = half_rows(grad, mine)
        low = source[...]
        grad[rows, :] = low
        d_branch = mm_nt(low, out_weight[...])
        for h in range(heads):
            at = slice(h * LANES, (h + 1) * LANES)
            mix = mixed[rows, at]
            gate = outgate[rows, at]
            grad_h = d_branch[:, at]
            scale = lax.rsqrt(jnp.mean(mix * mix, axis=1, keepdims=True) + EPSILON)
            normed = mix * scale
            sg = sigmoid(gate)
            through = grad_h * (gate * sg)
            gain_sum += jnp.sum(through * normed, axis=0, keepdims=True)
            d_normed = through * gain
            d_mix = (scale * (d_normed - normed * jnp.mean(d_normed * normed, axis=1, keepdims=True))).astype(BF)
            d_mixed[rows, at] = d_mix
            d_outgate[rows, at] = (grad_h * normed * gain * (sg * (1.0 + gate * (1.0 - sg)))).astype(BF)
            carries[h] += mm_tn(out_aug[h, rows, LANES:], d_mix)
    for h in range(heads):
        carry[h] = carries[h].astype(carry.dtype)
    d_gain[...] = gain_sum


def attend_back(own, other, out_weight, mixed, outgate, o_gain, out_aug):
    heads, tokens, _ = out_aug.shape
    wide = out_weight.shape[1]
    outs = [
        shaped((tokens, wide), BF), shaped((tokens, heads * LANES), BF), shaped((tokens, heads * LANES), BF),
        shaped((1, LANES), F32), shaped((heads, LANES, LANES), BF),
    ]
    operands = [own, other, out_weight, mixed, outgate, o_gain.reshape(1, -1), out_aug]
    return call(
        functools.partial(attend_back_kernel, heads), "attend_back", outs, operands,
        flops=2 * tokens * wide * heads * LANES,
    )


def store_rows_cut(part, at, piece):
    quarters = part.shape[0]
    rows = piece.shape[0] // quarters
    for q in range(quarters):
        for i in range(piece.shape[1] // LANES):
            part[q, at + i * rows : at + (i + 1) * rows, :] = piece[
                q * rows : (q + 1) * rows, i * LANES : (i + 1) * LANES
            ].astype(BF)


def store_cols_cut(part, at, piece):
    for q in range(part.shape[0]):
        part[q, at : at + piece.shape[0], :] = piece[:, q * LANES : (q + 1) * LANES].astype(BF)


def feed_weights_kernel(
    d_own, normed, out_grad, d_near, normed_mine, normed_other, grad_mine, grad_other, grads
):
    half = d_own.shape[0] // 3
    for k in range(3):
        right, mine, other = (out_grad, grad_mine, grad_other) if k == 2 else (normed, normed_mine, normed_other)
        rows = slice(k * half, (k + 1) * half)
        total = mm(d_own[rows, :], right[...])
        total += mm(d_near[rows, half_lanes(d_near, True)], mine[...])
        total += mm(d_near[rows, half_lanes(d_near, False)], other[...])
        grads[rows, :] = total.astype(BF)


def feed_weights(d_own, normed, out_grad, d_near, normed_mine, normed_other, grad_mine, grad_other):
    tokens, wide = normed.shape
    rows = d_own.shape[0]
    operands = [d_own, normed, out_grad, d_near, normed_mine, normed_other, grad_mine, grad_other]
    (grads,) = call(
        feed_weights_kernel, "feed_weights", [shaped((rows, wide), BF)], operands, flops=4 * tokens * wide * rows
    )
    return grads


def feed_out_kernel(mine, other, *outs):
    units = outs[0].shape[0]
    half = units // 2
    for own, ref in ((True, mine), (False, other)):
        for k, out in enumerate(outs):
            out[near_units(units, own), :] = ref[k * half : (k + 1) * half, :].astype(F32)


def gate_weights_kernel(normed, d_outgate, branch, grad, give, keep):
    for own, part in ((False, give), (True, keep)):
        store_rows_cut(part, 0, mm_tn(normed[:, half_width(normed, own)], d_outgate[...]))
        store_cols_cut(part, d_outgate.shape[1], mm_tn(branch[...], grad[:, half_width(grad, own)]))


def gate_weights(normed, d_outgate, branch, grad):
    rows = d_outgate.shape[1] + branch.shape[1]
    outs = [shaped((4, rows, LANES), BF)] * 2
    operands = [normed, d_outgate, branch, grad]
    return call(
        gate_weights_kernel, "gate_weights", outs, operands, flops=2 * normed.shape[0] * normed.shape[1] * rows
    )


def mix_weights_kernel(first, normed, halo, d_cols, d_halo, *rest):
    *side, give, keep = rest
    low_halo = d_halo[...].astype(BF)
    for own, part in ((False, give), (True, keep)):
        at = half_width(normed, own, first)
        left = normed[:, at]
        total = mm_tn(left, d_cols[...]) + mm_tn(halo[halo.shape[0] - d_halo.shape[0] :, at], low_halo)
        store_rows_cut(part, 0, total)
        if side:
            store_cols_cut(part, d_cols.shape[1], mm_tn(side[0][...], left)[:16])


def mix_weights(first, normed, halo, d_cols, d_halo, *side):
    tokens, wide = normed.shape
    rows = d_cols.shape[1] + 16 * len(side)
    operands = [normed, halo, d_cols, d_halo, *side]
    return call(
        functools.partial(mix_weights_kernel, first), "mix_weights", [shaped((4, rows, LANES), BF)] * 2,
        operands, flops=2 * tokens * wide * rows,
    )


def unproject_kernel(
    d_kq, d_v, tail, following, d_outgate, d_small, q_w, k_w, v_w, gate_w, beta_w, decay_w, give, keep,
    joined, side_w,
):
    tokens, width = joined.shape
    wide_q, wide_k = q_w.shape[1], k_w.shape[1]
    joined[:, 0:wide_q] = d_kq[:, wide_k:]
    joined[:, wide_q : wide_q + wide_k] = d_kq[:, :wide_k]
    joined[:, wide_q + wide_k :] = d_v[...]
    joined[tokens - 16 :, :] = jnp.concatenate([tail[0:8, :], tail[8:16, :] + following[...]], axis=0).astype(BF)
    gather_side(side_w, beta_w, decay_w)
    for own, part in ((False, give), (True, keep)):
        rows = half_rows(joined, own)
        total = mm_nt(d_outgate[rows, :], gate_w[...]) + mm(d_small[rows, :], side_w[...])
        at = 0
        for weight in (q_w, k_w, v_w):
            total += mm_nt(joined[rows, at : at + weight.shape[1]], weight[...])
            at += weight.shape[1]
        part[...] = total.astype(part.dtype)


def unproject(d_kq, d_v, tail, following, d_outgate, d_small, q_w, k_w, v_w, gate_w, beta_w, decay_w):
    tokens = d_v.shape[0]
    wide, width = q_w.shape[0], tail.shape[1]
    half = (tokens // 2, wide)
    operands = [d_kq, d_v, tail, following, d_outgate, d_small, q_w, k_w, v_w, gate_w, beta_w, decay_w]
    return call(
        unproject_kernel, "unproject", [shaped(half, BF), shaped(half, F32)], operands,
        scratch=[VMEM((tokens, width), BF), VMEM((LANES, wide), F32)],
        flops=2 * tokens * (width + 384) * wide,
    )


def fold_kernel(stage, keep, got, *outs):
    if len(outs) == 1:
        outs[0][...] = (keep[...].astype(F32) + got[...].astype(F32)).astype(BF)
        return
    mine = seq_bits()[stage]
    half = keep.shape[0] // 2
    for own, out in ((False, outs[0]), (True, outs[1])):
        at = (mine if own else 1 - mine) * half
        for k in range(half):
            out[k] = (keep[at + k].astype(F32) + got[at + k].astype(F32)).astype(BF)


def fold(stage, keep, got):
    count, rows, lanes = keep.shape
    outs = [shaped((count // 2, rows, lanes), BF)] * 2 if stage else [shaped(keep.shape, BF)]
    return call(functools.partial(fold_kernel, stage), "fold", outs, [keep, got])


class Line:
    def __init__(self):
        self.last = None

    def after(self, *arrays):
        if self.last is None:
            return arrays
        return lax.optimization_barrier((*arrays, self.last))[:-1]

    def step(self, function, *arrays):
        result = function(*self.after(*arrays))
        self.last = jax.tree.leaves(result)[0]
        return result


class Sum:
    def __init__(self, line, order, give, keep):
        self.line, self.order, self.keep, self.at = line, order, keep, 0
        self.got = swapped(give, SEQ, PARTNER[order[0]])

    def next(self):
        stages = len(self.order)
        self.at += 1
        if self.at < stages:
            give, self.keep = self.line.step(
                functools.partial(fold, self.order[self.at]), self.keep, self.got
            )
            self.got = swapped(give, SEQ, PARTNER[self.order[self.at]])
            return
        if self.at == stages:
            (mine,) = self.line.step(functools.partial(fold, None), self.keep, self.got)
            bit = 8
            while bit < seq_size():
                mine = (mine.astype(F32) + swapped(mine, SEQ, bit).astype(F32)).astype(BF)
                bit *= 2
        else:
            mine = self.line.step(lambda *parts: jnp.concatenate(parts, axis=0), self.keep, self.got)
        self.keep = mine
        self.got = swapped(mine, SEQ, PARTNER[self.order[2 * stages - 1 - self.at]])

    def finish(self, kernel, name, outs):
        return self.line.step(
            lambda *parts: call(functools.partial(kernel, self.order), name, outs, list(parts)), self.keep, self.got
        )


def blocks_of(order, mine, other):
    bits = seq_bits()
    first, second, third = (bits[stage] for stage in order)
    for flip, ref in ((0, mine), (1, other)):
        for slot in range(4):
            yield 4 * (first ^ flip) + 2 * (second ^ (slot // 2)) + (third ^ (slot % 2)), ref, slot


def at_block(index):
    return pl.ds(pl.multiple_of(index * LANES, LANES), LANES)


def load_rows_cut(ref, slot, at, count):
    return [ref[slot, at + i * LANES : at + (i + 1) * LANES, :].astype(F32) for i in range(count)]


def gate_out_kernel(order, mine, other, outgate, out):
    for index, ref, slot in blocks_of(order, mine, other):
        width = outgate.shape[1]
        for i, piece in enumerate(load_rows_cut(ref, slot, 0, width // LANES)):
            outgate[at_block(index), i * LANES : (i + 1) * LANES] = piece
        out[:, at_block(index)] = ref[slot, width : width + out.shape[0], :].astype(F32)


def mix_out_kernel(side, order, mine, other, *outs):
    wide = outs if not side else outs[:-2]
    for index, ref, slot in blocks_of(order, mine, other):
        at = 0
        for out in wide:
            for i, piece in enumerate(load_rows_cut(ref, slot, at, out.shape[1] // LANES)):
                out[at_block(index), i * LANES : (i + 1) * LANES] = piece
            at += out.shape[1]
        if side:
            pieces = ref[slot, at : at + 16, :].astype(F32)
            at = 0
            for part in outs[-2:]:
                part[:, at_block(index)] = pieces[at : at + part.shape[0], :]
                at += part.shape[0]


def shifted(value, axis, steps):
    count = seq_size()
    leading, last = max(0, -steps), min(count, count - steps)
    return lax.ppermute(value, axis, [(source, source + steps) for source in range(leading, last)])


def swapped(value, axis, bit):
    return lax.ppermute(value, axis, [(s, s ^ bit) for s in range(seq_size() if axis == SEQ else lax.axis_size(axis))])


def head_sum(give, keep):
    total = keep + swapped(give, "head", 1).astype(F32)
    mine = total.astype(BF)
    other = swapped(mine, "head", 2)
    bit = 4
    while bit < lax.axis_size("head"):
        mine = (mine.astype(F32) + other.astype(F32)).astype(BF)
        other = swapped(mine, "head", bit)
        bit *= 2
    return mine, other


def both_halves(mine):
    low = lax.axis_index("head") % 2
    other = swapped(mine, "head", 1)
    return jnp.concatenate([jnp.where(low == 0, mine, other), jnp.where(low == 0, other, mine)], axis=0)


def reach_of(tokens, count):
    whole = tokens * count
    longest = whole // 4 + 2 * (whole // 64 - 1)
    return max(1, min(count - 1, -(-(longest - 1) // tokens)))


def local(
    block_in, seq_start, attn_gain, q_weight, k_weight, v_weight, conv_q, conv_k, conv_v,
    beta_weight, decay_weight, a_log, dt_bias, outgate_weight, o_gain, out_weight,
    mlp_gain, gate_weight, up_weight, down_weight, out_grad,
):
    tokens = block_in.shape[0]
    heads = a_log.shape[0]
    width_q = q_weight.shape[1]
    width_k = k_weight.shape[1]
    width = width_q + 2 * width_k
    betas = beta_weight.shape[1]
    reach = reach_of(tokens, seq_size())
    wide = block_in.shape[1]
    units = gate_weight.shape[1]
    beta_rows, decay_rows = beta_weight.T, decay_weight.T
    core = lax.axis_index("head") % 2
    grad_mine = swapped(lax.dynamic_slice_in_dim(out_grad, core * (tokens // 2), tokens // 2, 0), SEQ, 1)
    normed, projected, outgate, small, edge = project(
        block_in, attn_gain, q_weight, k_weight, v_weight, outgate_weight, beta_rows, decay_rows
    )
    halo = shifted(edge, SEQ, 1)
    halo, normed_halo = halo[:, :width], halo[:, width:]
    mixer_args = (seq_start, a_log, dt_bias, projected, halo, conv_q, conv_k, conv_v, small)
    prepared = mixer_prep(*mixer_args)
    out_aug, saved, final_state, final_map = prepared[0], prepared[1:13], prepared[13], prepared[14]
    final_state, grad_mine = lax.optimization_barrier((final_state, grad_mine))
    grad_other = swapped(grad_mine, "head", 1)
    pair = jnp.stack([final_state, final_map])
    before = [shifted(pair, SEQ, r) for r in range(1, reach)] + [shifted(final_state[None], SEQ, reach)]
    later = [shifted(final_map, SEQ, -r) for r in range(1, reach)]
    mixed, branch, give, keep, state_in = attend(out_aug, outgate, o_gain, out_weight, before)
    hidden, normed_own = enter(block_in, *head_sum(give, keep), mlp_gain)
    near_mine = swapped(normed_own, SEQ, 1)
    normed_mlp, d_give, d_keep, part_give, part_keep, feed_give, feed_keep = feed(
        normed_own, swapped(normed_own, "head", 1), gate_weight.T, up_weight.T, down_weight, out_grad
    )
    line = Line()
    part_mine, part_other = head_sum(part_give, part_keep)
    line.last = part_mine
    d_give, near_mine = lax.optimization_barrier((d_give, near_mine))
    d_near = swapped(d_give, SEQ, 1)
    near_other = swapped(near_mine, "head", 1)
    d_hidden, attention_own, grad_mlp_gain = line.step(leave, part_mine, part_other, hidden, mlp_gain, out_grad)
    attention_gradient, grad_mixed, grad_outgate, grad_o_part, carry = line.step(
        attend_back, attention_own, swapped(attention_own, "head", 1), out_weight, mixed, outgate, o_gain, out_aug
    )
    after = [shifted(carry, SEQ, -r) for r in range(1, reach + 1)]
    feed_grads = line.step(
        feed_weights, d_keep, normed_mlp, out_grad, d_near, near_mine, near_other, grad_mine, grad_other
    )
    feed_sums = lax.psum(feed_grads, "far")
    feed_near = swapped(feed_sums, SEQ, 1)
    sum_out = Sum(line, X_FIRST, *line.step(gate_weights, normed, grad_outgate, branch, attention_gradient))
    feed_mine, feed_other = head_sum(feed_give, feed_keep)
    output = both_halves((hidden + feed_mine.astype(F32) + feed_other.astype(F32)).astype(BF))
    d_kq, d_v, tail, d_halo, grad_small, grad_taps, grad_scalars = line.step(
        lambda d_mixed: mixer_back(*mixer_args, saved, state_in, d_mixed, after, later), grad_mixed
    )
    following = shifted(d_halo, SEQ, -1)
    cut_q, cut_k, cut_v = slice(0, width_q), slice(width_q, width_q + width_k), slice(width_q + width_k, width)
    halo_kq = jnp.concatenate([d_halo[:, cut_k], d_halo[:, cut_q]], axis=1)
    sum_kq = Sum(
        line, X_FIRST, *line.step(functools.partial(mix_weights, X_FIRST[0]), normed, normed_halo, d_kq, halo_kq)
    )
    sum_v = Sum(
        line, Z_FIRST,
        *line.step(functools.partial(mix_weights, Z_FIRST[0]), normed, normed_halo, d_v, d_halo[:, cut_v], grad_small),
    )
    taps = conv_q.shape[0]

    def padded(*rows):
        joined = jnp.concatenate(rows, axis=1)
        return jnp.pad(joined, ((0, 0), (0, width - joined.shape[1])))

    for part in (sum_out, sum_kq, sum_v):
        part.next()
    mine, other = head_sum(
        *line.step(
            unproject, d_kq, d_v, tail, following, grad_outgate, grad_small,
            q_weight, k_weight, v_weight, outgate_weight, beta_rows, decay_rows,
        )
    )
    for part in (sum_out, sum_kq, sum_v):
        part.next()
    line.last = feed_sums
    input_own, grad_attn_gain = line.step(finish, mine, other, block_in, attn_gain, d_hidden)
    grad_input = both_halves(input_own)
    small_sums = jnp.concatenate(
        [
            grad_taps[:taps], padded(grad_scalars[0:1], grad_scalars[1:2]),
            padded(grad_attn_gain), padded(grad_mlp_gain), padded(grad_o_part),
        ],
        axis=0,
    )
    small_got = swapped(small_sums, SEQ, 1)
    bit = 2
    rounds = 3
    while small_got is not None or rounds > 0:
        if rounds == 1:
            line.last = feed_near
        for part in (sum_out, sum_kq, sum_v) if rounds > 0 else ():
            part.next()
        rounds -= 1
        if small_got is not None:
            small_sums = line.step(jnp.add, small_sums, small_got)
            small_got = swapped(small_sums, SEQ, bit) if bit < seq_size() else None
            bit *= 2
    gains = small_sums[taps + 1 : taps + 4]
    gains = gains + swapped(gains, "head", 1)
    grad_o_gain = gains[2:3, :LANES]
    bit = 2
    while bit < lax.axis_size("head"):
        grad_o_gain = grad_o_gain + swapped(grad_o_gain, "head", bit)
        bit *= 2
    grad_outgate_w, grad_out_w = sum_out.finish(
        gate_out_kernel, "gate_out", [shaped((wide, width_q), F32), shaped((width_q, wide), F32)]
    )
    grad_v_w, grad_beta_w, grad_decay_w = sum_v.finish(
        functools.partial(mix_out_kernel, True), "mix_out",
        [shaped((wide, width_k), F32), shaped((betas, wide), F32), shaped((heads, wide), F32)],
    )
    grad_k_w, grad_q_w = sum_kq.finish(
        functools.partial(mix_out_kernel, False), "mix_out",
        [shaped((wide, width_k), F32), shaped((wide, width_q), F32)],
    )
    grad_gate_w, grad_up_w, grad_down_w = call(
        feed_out_kernel, "feed_out", [shaped((units, wide), F32)] * 3, [feed_sums, feed_near]
    )
    rate, shift = small_sums[taps, betas : betas + heads], small_sums[taps, LANES + betas : LANES + betas + heads]
    return (
        output, grad_input, gains[0, :wide], grad_q_w, grad_k_w, grad_v_w,
        small_sums[:taps, cut_q], small_sums[:taps, cut_k], small_sums[:taps, cut_v],
        grad_beta_w.T, grad_decay_w.T, rate, shift, grad_outgate_w, grad_o_gain[0], grad_out_w, gains[1, :wide],
        grad_gate_w.T, grad_up_w.T, grad_down_w,
    )


def solution(mesh):
    placed = (
        P(SEQ, None), P(), P(), P(None, "head"), P(None, "head"), P(None, "head"), P(None, "head"),
        P(None, "head"), P(None, "head"), P(None, "head"), P(None, "head"), P("head"), P("head"),
        P(None, "head"), P(), P("head", None), P(), P(None, "head"), P(None, "head"), P("head", None),
        P(SEQ, None),
    )
    given = (
        P(SEQ, None), P(SEQ, None), P(), P(None, "head"), P(None, "head"), P(None, "head"),
        P(None, "head"), P(None, "head"), P(None, "head"), P(None, "head"), P(None, "head"), P("head"),
        P("head"), P(None, "head"), P(), P("head", None), P(), P(None, "head"), P(None, "head"),
        P("head", None),
    )
    seq, head = mesh.devices.shape
    mesh = jax.sharding.Mesh(mesh.devices.reshape(seq // 2, 2, head), ("far", "near", "head"))
    return jax.shard_map(local, mesh=mesh, in_specs=placed, out_specs=given, check_vma=False)
```

```python
import functools
import math
import jax
import jax.numpy as jnp
from jax import lax
from jax.experimental import pallas as pl
from jax.experimental.pallas import tpu as pltpu
from jax.sharding import PartitionSpec as P

NH = 2
GROUP = 64
LANES = 128
EPSILON = 1e-06
BF = jnp.bfloat16
F32 = jnp.float32
VMEM = pltpu.VMEM
HBM = pltpu.HBM
VMEM_LIMIT = 60 * 1024 * 1024
SMALL_LIMIT = 24 * 1024 * 1024
EARLY = 64
SEQ = ("far", "near")


def seq_index():
    return lax.axis_index("far") * 2 + lax.axis_index("near")


def seq_size():
    return lax.axis_size("far") * lax.axis_size("near")


def mm(left, right):
    return jnp.dot(left.astype(BF), right.astype(BF), preferred_element_type=F32)


def mm_nt(left, right):
    return lax.dot_general(
        left.astype(BF), right.astype(BF), (((1,), (1,)), ((), ())), preferred_element_type=F32
    )


def mm_tn(left, right):
    return lax.dot_general(
        left.astype(BF), right.astype(BF), (((0,), (0,)), ((), ())), preferred_element_type=F32
    )


def mm_exact(left, right):
    return jnp.dot(left, right, preferred_element_type=F32, precision=lax.Precision.HIGHEST)


def sigmoid(values):
    return 1.0 / (1.0 + jnp.exp(-values))


def softplus(values):
    return jnp.maximum(values, 0.0) + jnp.log1p(jnp.exp(-jnp.abs(values)))


def documents_at(starts, positions):
    total = jnp.zeros(positions.shape, jnp.int32)
    for k in range(starts.shape[0]):
        total = total + (starts[k] <= positions).astype(jnp.int32)
    return total


def sub_order(index):
    return NH * (index % GROUP) + index // GROUP


def order_pair():
    rows = sub_order(lax.broadcasted_iota(jnp.int32, (LANES, LANES), 0))
    cols = sub_order(lax.broadcasted_iota(jnp.int32, (LANES, LANES), 1))
    return rows, cols


def gate_columns(small, log_rate, bias, heads):
    lane = lax.broadcasted_iota(jnp.int32, (1, LANES), 1)
    rate = jnp.zeros((1, LANES), F32)
    shift = jnp.zeros((1, LANES), F32)
    for h in range(heads):
        at = lane == NH * heads + h
        rate = jnp.where(at, -jnp.exp(jnp.full((1, LANES), log_rate[h], F32)), rate)
        shift = jnp.where(at, bias[h], shift)
    return sigmoid(small), rate * softplus(small + shift), small + shift, rate


def chunk_decays(rows, cols_ref, row_ref, doc_ref, c, h, heads, doc_before):
    cum_col = cols_ref[rows, NH * heads + h : NH * heads + h + 1]
    doc_col = doc_ref[rows, 0:1]
    packed = row_ref[c]
    cum_row = packed[NH * heads + h : NH * heads + h + 1, :]
    doc_row = packed[NH * heads + heads : NH * heads + heads + 1, :]
    token_row = lax.broadcasted_iota(jnp.int32, (GROUP, LANES), 1) % GROUP
    token_col = lax.broadcasted_iota(jnp.int32, (GROUP, LANES), 0)
    seen = (token_col >= token_row) & (doc_col == doc_row)
    pair = jnp.where(seen, jnp.exp(jnp.where(seen, cum_col - cum_row, 0.0)), 0.0)
    start = jnp.where(doc_col == doc_before, jnp.exp(cum_col), 0.0)
    cum_last = cum_col[GROUP - 1 :, :]
    doc_last = doc_col[GROUP - 1 :, :]
    to_end = jnp.where(doc_col == doc_last, jnp.exp(cum_last - cum_col), 0.0)
    return pair, start, to_end


def two(array):
    return jnp.concatenate([array, array], axis=0)


def beta_pair(rows, cols_ref, row_ref, c, h):
    lane = lax.broadcasted_iota(jnp.int32, (1, LANES), 1)
    packed = row_ref[c]
    row = jnp.where(lane < GROUP, packed[NH * h : NH * h + 1, :], packed[NH * h + 1 : NH * h + 2, :])
    col = jnp.concatenate(
        [cols_ref[rows, NH * h : NH * h + 1], cols_ref[rows, NH * h + 1 : NH * h + 2]], axis=0
    )
    return row, col


def copies(pairs, sems, first=0):
    return [
        pltpu.make_async_copy(source, target, sems.at[first + k]) for k, (source, target) in enumerate(pairs)
    ]


def begin(waiting):
    for copy in waiting:
        copy.start()
    return waiting


def end(waiting):
    for copy in waiting:
        copy.wait()


def prep_kernel(
    heads, starts, log_rate, bias, far_proj, halo, conv_q, conv_k, conv_v, far_small,
    out_aug, far_state_aug, far_wy_k, far_wy_v, far_inverse, far_step_p, far_query_map, far_keys, far_queries,
    far_conv_total, far_cols, far_doc, far_row,
    final_state, final_map,
    proj, small, state_aug, wy_k, wy_v, inverse, step_p, query_map, keys, queries, conv_total, cols, doc, row,
    ext, vals, score_map, step_b, masks, sems,
):
    arriving = begin(copies([(far_small, small), (far_proj, proj)], sems))
    tokens = proj.shape[0]
    chunks = tokens // GROUP
    first = seq_index() * tokens
    lead = 8
    lower_r = lax.broadcasted_iota(jnp.int32, (LANES, LANES), 0)
    lower_c = lax.broadcasted_iota(jnp.int32, (LANES, LANES), 1)
    lower = ((lower_r >= lower_c) & (lower_r // GROUP == lower_c // GROUP)).astype(F32)
    lane = lax.broadcasted_iota(jnp.int32, (LANES, LANES), 1)
    per = LANES // GROUP
    end(arriving[:1])
    for block in range(tokens // LANES):
        at = pl.ds(block * LANES, LANES)
        betas, logdec, _, _ = gate_columns(small[at, :], log_rate, bias, heads)
        cum = mm_exact(lower, logdec)
        where = lax.broadcasted_iota(jnp.int32, (LANES, LANES), 0) + (first + block * LANES)
        document = documents_at(starts, where).astype(F32)
        packed = jnp.where(lane < NH * heads, betas, jnp.where(lane < NH * heads + heads, cum, document))
        cols[at, :] = packed
        doc[at, :] = document
        turned = packed.T
        for part in range(per):
            piece = turned[0:8, part * GROUP : (part + 1) * GROUP]
            row[block * per + part] = jnp.concatenate([piece] * NH, axis=1)
    order_r, order_c = order_pair()
    level = 0
    width = 1
    while width < LANES:
        inside = (order_r // (2 * width) == order_c // (2 * width)) & (order_r // width > order_c // width)
        masks[level] = inside.astype(F32)
        level += 1
        width *= 2
    end(arriving[1:])
    ext[0:lead, :] = halo[16 - lead : 16, :].astype(F32)
    ext[lead:, :] = proj[...].astype(F32)
    width_q = heads * LANES
    width_k = NH * heads * LANES
    taps = conv_q.shape[0]

    def conv_chunk(c, _):
        base = pl.multiple_of(c * GROUP, GROUP)
        rows = pl.ds(base, GROUP)
        position = lax.broadcasted_iota(jnp.int32, (GROUP, LANES), 0) + (first + base)
        document = doc[rows, :]
        kept = [
            (documents_at(starts, position - lag).astype(F32) == document).astype(F32) for lag in range(1, taps)
        ]
        for group in range((width_q + 2 * width_k) // LANES):
            at = slice(group * LANES, (group + 1) * LANES)
            if group * LANES < width_q:
                kernel, shift = conv_q, 0
            elif group * LANES < width_q + width_k:
                kernel, shift = conv_k, width_q
            else:
                kernel, shift = conv_v, width_q + width_k
            cut = slice(at.start - shift, at.stop - shift)
            window = ext[pl.ds(base, GROUP + lead), at]
            total = kernel[taps - 1 : taps, cut] * window[lead:, :]
            for lag in range(1, taps):
                total += kernel[taps - 1 - lag : taps - lag, cut] * window[lead - lag : lead - lag + GROUP, :] * kept[lag - 1]
            conv_total[rows, at] = total
            active = total * sigmoid(total)
            if group * LANES < width_q:
                unit = active * lax.rsqrt(jnp.sum(active * active, axis=1, keepdims=True) + EPSILON)
                queries[group, c] = (unit * LANES ** (-0.5)).astype(BF)
            elif group * LANES < width_q + width_k:
                piece = group - width_q // LANES
                unit = active * lax.rsqrt(jnp.sum(active * active, axis=1, keepdims=True) + EPSILON)
                keys[piece // NH, c, (piece % NH) * GROUP : (piece % NH + 1) * GROUP] = unit.astype(BF)
            else:
                piece = group - (width_q + width_k) // LANES
                vals[piece // NH, c, (piece % NH) * GROUP : (piece % NH + 1) * GROUP] = active.astype(BF)
        return 0

    lax.fori_loop(0, chunks, conv_chunk, 0)
    leaving = begin(
        copies(
            [
                (conv_total, far_conv_total), (keys, far_keys), (queries, far_queries),
                (cols, far_cols), (doc, far_doc), (row, far_row),
            ],
            sems, 2,
        )
    )

    strict = order_r > order_c
    eye = (lower_r == lower_c).astype(F32)
    together = 4

    def part_chunks(step, _):
        jobs = []
        for k in range(together):
            c = step * together + k
            rows = pl.ds(pl.multiple_of(c * GROUP, GROUP), GROUP)
            before = documents_at(starts, jnp.full((1, 1), first + c * GROUP - 1, jnp.int32)).astype(F32)
            for h in range(heads):
                pair, start, to_end = chunk_decays(rows, cols, row, doc, c, h, heads, before)
                beta_row, beta_col = beta_pair(rows, cols, row, c, h)
                key = keys[h, c]
                query = queries[h, c]
                grams = mm_nt(jnp.concatenate([key, query], axis=0), key)
                system = jnp.where(strict, grams[:LANES] * two(pair), 0.0) * beta_row
                scores = grams[LANES:] * pair * beta_row
                jobs.append((c, h, start, to_end, beta_col, key, query, system, scores))
        inverses = [eye - job[7] * masks[0] for job in jobs]
        for n in range(1, level):
            halves = [mm(job[7] * masks[n], inv) for job, inv in zip(jobs, inverses)]
            inverses = [inv - mm(inv, half) for inv, half in zip(inverses, halves)]
        for job, inv in zip(jobs, inverses):
            c, h, start, to_end, beta_col, key, query, system, scores = job
            low_inv = inv.astype(BF)
            inverse[h, c] = low_inv
            key_f = key.astype(F32)
            both = mm(low_inv, jnp.concatenate([(two(start) * key_f).astype(BF), vals[h, c]], axis=1)).astype(BF)
            wy_k[h, c] = both[:, :LANES]
            wy_v[h, c] = both[:, LANES:]
            carried = (beta_col * two(to_end) * key_f).astype(BF)
            ahead = mm_tn(carried, both)
            step_p[h, c] = ahead[:, :LANES].astype(BF)
            step_b[h, c] = ahead[:, LANES:]
            scored = mm(scores, both)
            query_map[h, c] = (start * query.astype(F32) - scored[:, :LANES]).astype(BF)
            score_map[h, c] = scored[:, LANES:]
        return 0

    lax.fori_loop(0, chunks // together, part_chunks, 0)
    leaving += begin(
        copies(
            [
                (wy_k, far_wy_k), (wy_v, far_wy_v), (inverse, far_inverse), (step_p, far_step_p),
                (query_map, far_query_map),
            ],
            sems, 8,
        )
    )

    zero = jnp.zeros((LANES, LANES), F32)

    def advance(c, carry):
        rows = pl.ds(pl.multiple_of(c * GROUP, GROUP), GROUP)
        before = documents_at(starts, jnp.full((1, 1), first + c * GROUP - 1, jnp.int32)).astype(F32)
        new = []
        for h in range(heads):
            state = carry[h]
            low_state = state.astype(BF)
            state_aug[h, c] = low_state
            last = cols[rows, NH * heads + h : NH * heads + h + 1][GROUP - 1 :, :]
            whole = jnp.where(doc[rows, 0:1][GROUP - 1 :, :] == before, jnp.exp(last), 0.0)
            new.append(
                whole * state - mm(step_p[h, c], low_state) + jnp.concatenate([step_b[h, c], zero], axis=1)
            )
            mapped = mm(query_map[h, c], low_state)
            out_aug[h, rows, :] = jnp.concatenate([mapped[:, :LANES] + score_map[h, c], mapped[:, LANES:]], axis=1)
        return tuple(new)

    initial = jnp.concatenate([zero, eye], axis=1)
    last = lax.fori_loop(0, chunks, advance, (initial,) * heads)
    leaving += begin(copies([(state_aug, far_state_aug)], sems, 13))
    for h in range(heads):
        final_state[h] = last[h][:, :LANES].astype(final_state.dtype)
        final_map[h] = last[h][:, LANES:].astype(final_map.dtype)
    end(leaving)


def specs(count, space=None):
    return [pl.BlockSpec(memory_space=space or pltpu.VMEM)] * count


def mixer_prep(starts, log_rate, bias, proj, halo, conv_q, conv_k, conv_v, small):
    tokens, width = proj.shape
    heads = log_rate.shape[0]
    chunks = tokens // GROUP
    square = (heads, chunks, LANES, LANES)
    shape = jax.ShapeDtypeStruct
    outs = [
        shape((heads, tokens, 2 * LANES), F32),
        shape((heads, chunks, LANES, 2 * LANES), BF),
        shape(square, BF),
        shape(square, BF),
        shape(square, BF),
        shape(square, BF),
        shape((heads, chunks, GROUP, LANES), BF),
        shape(square, BF),
        shape((heads, chunks, GROUP, LANES), BF),
        shape((tokens, width), F32),
        shape((tokens, LANES), F32),
        shape((tokens, LANES), F32),
        shape((chunks, 8, LANES), F32),
        shape((heads, LANES, LANES), BF),
        shape((heads, LANES, LANES), BF),
    ]
    return pl.pallas_call(
        functools.partial(prep_kernel, heads),
        out_shape=outs,
        in_specs=specs(3, pltpu.SMEM) + specs(1, HBM) + specs(4) + specs(1, HBM),
        out_specs=specs(1) + specs(12, HBM) + specs(2),
        scratch_shapes=[VMEM(proj.shape, BF), VMEM(small.shape, F32)]
        + [VMEM(out.shape, out.dtype) for out in outs[1:13]]
        + [
            VMEM((tokens + 8, width), F32),
            VMEM(square, BF),
            VMEM((heads, chunks, GROUP, LANES), F32),
            VMEM(square, F32),
            VMEM((8, LANES, LANES), F32),
            pltpu.SemaphoreType.DMA((14,)),
        ],
        compiler_params=pltpu.CompilerParams(vmem_limit_bytes=VMEM_LIMIT),
        cost_estimate=pl.CostEstimate(flops=24_000_000_000, bytes_accessed=4_000_000, transcendentals=0),
        name="mixer_prep",
    )(starts, log_rate, bias, proj, halo, conv_q, conv_k, conv_v, small)


def back_kernel(
    heads, reach, starts, log_rate, bias, far_proj, halo, conv_q, conv_k, conv_v, far_small,
    far_state_aug, far_wy_k, far_wy_v, far_inverse, far_step_p, far_query_map, far_keys, far_queries,
    far_conv_total, far_cols, far_doc, far_row, state_in, d_mixed, *rest,
):
    after = rest[:reach]
    later = rest[reach : 2 * reach - 1]
    (
        d_kq, d_v, tail, d_halo, d_small, d_taps, d_scalars,
        proj, small, state_aug, wy_k, wy_v, inverse, step_p, query_map, keys, queries, conv_total, cols, doc, row,
        ext, state_grads, d_query, d_key, d_value, col_grads, row_grads, d_total, sems,
    ) = rest[2 * reach - 1 :]
    arriving = begin(
        copies(
            [
                (far_step_p, step_p), (far_query_map, query_map), (far_cols, cols), (far_doc, doc), (far_row, row),
                (far_state_aug, state_aug), (far_wy_k, wy_k), (far_wy_v, wy_v), (far_inverse, inverse),
                (far_keys, keys), (far_queries, queries),
                (far_small, small), (far_conv_total, conv_total), (far_proj, proj),
            ],
            sems,
        )
    )
    tokens = proj.shape[0]
    chunks = tokens // GROUP
    first = seq_index() * tokens
    lead = 8
    lane = lax.broadcasted_iota(jnp.int32, (GROUP, LANES), 1)

    def document_before(c):
        return documents_at(starts, jnp.full((1, 1), first + c * GROUP - 1, jnp.int32)).astype(F32)

    def whole_decay(c, h):
        at = pl.ds(pl.multiple_of(c * GROUP, GROUP) + GROUP - 8, 8)
        last = cols[at, NH * heads + h : NH * heads + h + 1][7:8, :]
        return jnp.where(doc[at, 0:1][7:8, :] == document_before(c), jnp.exp(last), 0.0)

    at_end = []
    for h in range(heads):
        state = after[reach - 1][h].astype(F32)
        for r in range(reach - 2, -1, -1):
            state = mm_tn(later[r][h], state) + after[r][h].astype(F32)
        at_end.append(state)
    end(arriving[:5])

    def retreat(step, carry):
        c = chunks - 1 - step
        rows = pl.ds(pl.multiple_of(c * GROUP, GROUP), GROUP)
        new = []
        for h in range(heads):
            low_state = carry[h].astype(BF)
            state_grads[h, c] = low_state
            new.append(
                whole_decay(c, h) * carry[h]
                - mm_tn(step_p[h, c], low_state)
                + mm_tn(query_map[h, c], d_mixed[rows, h * LANES : (h + 1) * LANES])
            )
        return tuple(new)

    lax.fori_loop(0, chunks, retreat, tuple(at_end))
    end(arriving[5:11])

    order_r, order_c = order_pair()
    strict = order_r > order_c
    together = 2
    last_token = lax.broadcasted_iota(jnp.int32, (GROUP, 1), 0) == GROUP - 1

    def chunk_back(step, _):
        for k in range(together):
            c = step * together + k
            rows = pl.ds(pl.multiple_of(c * GROUP, GROUP), GROUP)
            before = document_before(c)
            col_acc = jnp.zeros((GROUP, LANES), F32)
            row_acc = []
            row_beta = []
            for h in range(heads):
                pair, start, to_end = chunk_decays(rows, cols, row, doc, c, h, heads, before)
                beta_row, beta_col = beta_pair(rows, cols, row, c, h)
                key = keys[h, c]
                query = queries[h, c]
                key_f = key.astype(F32)
                query_f = query.astype(F32)
                d_out = d_mixed[rows, h * LANES : (h + 1) * LANES]
                d_state = state_grads[h, c]
                both = state_aug[h, c]
                state = both[:, :LANES].astype(F32) + mm(both[:, LANES:], state_in[h])
                low_state = state.astype(BF)
                fresh = wy_v[h, c].astype(F32) - mm(wy_k[h, c], low_state)
                grams = mm_nt(jnp.concatenate([key, query], axis=0), key)
                pair2 = two(pair)
                system = jnp.where(strict, grams[:LANES] * pair2, 0.0)
                scores = grams[LANES:] * pair
                key_end = two(to_end) * key_f
                key_start = two(start) * key_f
                d_wide = mm_tn(scores, d_out) + mm(key_end, d_state)
                solved = mm_tn(inverse[h, c], beta_col * d_wide)
                d_value[h, c] = solved
                low_fresh = fresh.astype(BF)
                crossed = mm_nt(
                    jnp.concatenate([solved.astype(BF), d_out], axis=0),
                    jnp.concatenate([low_fresh, low_state], axis=0),
                )
                pairs = jnp.where(strict, crossed[:LANES, :LANES], 0.0)
                solved_state = crossed[:LANES, LANES:]
                out_state = crossed[LANES:, LANES:]
                fresh_grad = mm_nt(beta_col * fresh, d_state)
                system_pairs = system * pairs
                decayed = -(system_pairs * beta_row)
                gram_grad = -(pairs * pair2 * beta_row)
                score_grad = crossed[LANES:, :LANES] * beta_row
                query_key = score_grad * pair
                score_decay = score_grad * scores
                stacked = jnp.concatenate([gram_grad, query_key], axis=0).astype(BF)
                direct = mm(stacked, key)
                turned = mm_tn(stacked, jnp.concatenate([key, query], axis=0))
                d_key[h, c] = direct[:LANES] + turned - two(start) * solved_state + two(to_end) * fresh_grad
                d_query[h, c] = direct[LANES:] + start * out_state
                ending = key_end * fresh_grad
                parts = decayed - key_start * solved_state - ending
                parts = parts[:GROUP] + parts[GROUP:] + score_decay + (start * query_f) * out_state
                last_grad = jnp.sum(ending, keepdims=True) + whole_decay(c, h) * jnp.sum(
                    state * d_state.astype(F32), keepdims=True
                )
                decay_col = jnp.sum(parts, axis=1, keepdims=True) + jnp.where(last_token, last_grad, 0.0)
                beta_sum = jnp.sum(d_wide * fresh, axis=1, keepdims=True)
                col_acc = jnp.where(lane == NH * heads + h, decay_col, col_acc)
                for s in range(NH):
                    col_acc = jnp.where(lane == NH * h + s, beta_sum[s * GROUP : (s + 1) * GROUP], col_acc)
                beta_row_sum = jnp.sum(system_pairs, axis=0, keepdims=True)
                row_beta.append(-beta_row_sum)
                row_acc.append(beta_row * beta_row_sum - jnp.sum(score_decay, axis=0, keepdims=True))
            col_grads[rows, :] = col_acc
            row_grads[c] = jnp.concatenate(
                row_acc + row_beta + [jnp.zeros((8 - 2 * heads, LANES), F32)], axis=0
            )
        return 0

    lax.fori_loop(0, chunks // together, chunk_back, 0)

    end(arriving[11:])

    lower_r = lax.broadcasted_iota(jnp.int32, (LANES, LANES), 0)
    lower_c = lax.broadcasted_iota(jnp.int32, (LANES, LANES), 1)
    upper = ((lower_r <= lower_c) & (lower_r // GROUP == lower_c // GROUP)).astype(F32)
    per = LANES // GROUP
    scalar_decay = jnp.zeros((1, LANES), F32)
    scalar_rate = jnp.zeros((1, LANES), F32)
    wide = lax.broadcasted_iota(jnp.int32, (LANES, LANES), 1)
    for block in range(tokens // LANES):
        at = pl.ds(block * LANES, LANES)
        pieces = []
        for part in range(per):
            c = block * per + part
            turned = jnp.concatenate([row_grads[c], jnp.zeros((LANES - 8, LANES), F32)], axis=0).T
            piece = jnp.zeros((GROUP, LANES), F32)
            for h in range(heads):
                decay_col = turned[:GROUP, h : h + 1] + turned[GROUP:, h : h + 1]
                piece = jnp.where(lane == NH * heads + h, decay_col, piece)
                for s in range(NH):
                    beta_col = turned[s * GROUP : (s + 1) * GROUP, heads + h : heads + h + 1]
                    piece = jnp.where(lane == NH * h + s, beta_col, piece)
            pieces.append(piece)
        grads = col_grads[at, :] + jnp.concatenate(pieces, axis=0)
        d_logdec = mm_exact(upper, grads)
        betas, logdec, argument, rate = gate_columns(small[at, :], log_rate, bias, heads)
        d_argument = d_logdec * rate * sigmoid(argument)
        scalar_rate += jnp.sum(d_logdec * logdec, axis=0, keepdims=True)
        scalar_decay += jnp.sum(d_argument, axis=0, keepdims=True)
        d_small[at, :] = jnp.where(
            wide < NH * heads,
            grads * betas * (1.0 - betas),
            jnp.where(wide < NH * heads + heads, d_argument, 0.0),
        ).astype(BF)
    d_scalars[...] = jnp.concatenate([scalar_rate, scalar_decay, jnp.zeros((6, LANES), F32)], axis=0)

    ext[0:lead, :] = halo[16 - lead : 16, :].astype(F32)
    ext[lead:, :] = proj[...].astype(F32)
    width_q = heads * LANES
    width_k = NH * heads * LANES
    width = width_q + 2 * width_k
    taps = conv_q.shape[0]
    d_taps[...] = jnp.zeros(d_taps.shape, F32)
    d_total[tokens:, :] = jnp.zeros((8, width), F32)

    def kernel_of(group):
        if group * LANES < width_q:
            return conv_q, slice(group * LANES, (group + 1) * LANES)
        if group * LANES < width_q + width_k:
            return conv_k, slice(group * LANES - width_q, (group + 1) * LANES - width_q)
        return conv_v, slice(group * LANES - width_q - width_k, (group + 1) * LANES - width_q - width_k)

    def active_back(c, _):
        base = pl.multiple_of(c * GROUP, GROUP)
        rows = pl.ds(base, GROUP)
        position = lax.broadcasted_iota(jnp.int32, (GROUP, LANES), 0) + (first + base)
        document = doc[rows, :]
        kept = [
            (documents_at(starts, position - lag).astype(F32) == document).astype(F32) for lag in range(1, taps)
        ]
        for group in range(width // LANES):
            at = slice(group * LANES, (group + 1) * LANES)
            total = conv_total[rows, at]
            sg = sigmoid(total)
            if group * LANES < width_q + width_k:
                active = total * sg
                scale = lax.rsqrt(jnp.sum(active * active, axis=1, keepdims=True) + EPSILON)
                unit = active * scale
                if group * LANES < width_q:
                    grad = d_query[group, c] * LANES ** (-0.5)
                else:
                    piece = group - width_q // LANES
                    grad = d_key[piece // NH, c, (piece % NH) * GROUP : (piece % NH + 1) * GROUP]
                grad = scale * (grad - unit * jnp.sum(unit * grad, axis=1, keepdims=True))
            else:
                piece = group - (width_q + width_k) // LANES
                grad = d_value[piece // NH, c, (piece % NH) * GROUP : (piece % NH + 1) * GROUP]
            grad = grad * (sg * (1.0 + total * (1.0 - sg)))
            d_total[rows, at] = grad
            window = ext[pl.ds(base, GROUP + lead), at]
            sums = []
            for j in range(taps):
                lag = taps - 1 - j
                term = grad * window[lead - lag : lead - lag + GROUP, :]
                if lag > 0:
                    term = term * kept[lag - 1]
                sums.append(jnp.sum(term, axis=0, keepdims=True))
            d_taps[0:taps, at] += jnp.concatenate(sums, axis=0)
        return 0

    lax.fori_loop(0, chunks, active_back, 0)

    def conv_back(c, _):
        base = pl.multiple_of(c * GROUP, GROUP)
        rows = pl.ds(base, GROUP)
        position = lax.broadcasted_iota(jnp.int32, (GROUP, LANES), 0) + (first + base)
        document = doc[rows, :]
        kept = [
            (documents_at(starts, position + lag).astype(F32) == document).astype(F32) for lag in range(1, taps)
        ]
        for group in range(width // LANES):
            at = slice(group * LANES, (group + 1) * LANES)
            kernel, cut = kernel_of(group)
            window = d_total[pl.ds(base, GROUP + lead), at]
            grad = kernel[taps - 1 : taps, cut] * window[:GROUP]
            for lag in range(1, taps):
                grad += kernel[taps - 1 - lag : taps - lag, cut] * kept[lag - 1] * window[lag : lag + GROUP]
            target = d_v if kernel is conv_v else d_kq
            shift = width_k if kernel is conv_q else 0
            target[rows, cut.start + shift : cut.stop + shift] = grad.astype(BF)
            tail[:, at] = grad[GROUP - 16 :]
        return 0

    lax.fori_loop(0, chunks, conv_back, 0)
    position = lax.broadcasted_iota(jnp.int32, (8, LANES), 0) + (first - 8)
    document = documents_at(starts, position)
    for group in range(width // LANES):
        at = slice(group * LANES, (group + 1) * LANES)
        kernel, cut = kernel_of(group)
        window = jnp.concatenate([jnp.zeros((8, LANES), F32), d_total[0:8, at]], axis=0)
        grad = jnp.zeros((8, LANES), F32)
        for lag in range(1, taps):
            kept = (documents_at(starts, position + lag) == document).astype(F32)
            grad += kernel[taps - 1 - lag : taps - lag, cut] * kept * window[lag : lag + 8]
        d_halo[:, at] = grad


def mixer_back(starts, log_rate, bias, proj, halo, conv_q, conv_k, conv_v, small, saved, state_in, d_mixed, after, later):
    tokens, width = proj.shape
    heads = log_rate.shape[0]
    chunks = tokens // GROUP
    reach = len(after)
    square = (heads, chunks, LANES, LANES)
    shape = jax.ShapeDtypeStruct
    outs = [
        shape((tokens, conv_k.shape[1] + conv_q.shape[1]), BF),
        shape((tokens, conv_v.shape[1]), BF),
        shape((16, width), F32),
        shape((8, width), F32),
        shape((tokens, LANES), BF),
        shape((8, width), F32),
        shape((8, LANES), F32),
    ]
    operands = [starts, log_rate, bias, proj, halo, conv_q, conv_k, conv_v, small, *saved, state_in, d_mixed, *after, *later]
    return pl.pallas_call(
        functools.partial(back_kernel, heads, reach),
        out_shape=outs,
        in_specs=specs(3, pltpu.SMEM) + specs(1, HBM) + specs(4) + specs(13, HBM) + specs(len(operands) - 21),
        out_specs=specs(len(outs)),
        scratch_shapes=[VMEM(a.shape, a.dtype) for a in (proj, small, *saved)]
        + [
            VMEM((tokens + 8, width), F32),
            VMEM(square, BF),
            VMEM((heads, chunks, GROUP, LANES), F32),
            VMEM(square, F32),
            VMEM(square, F32),
            VMEM((tokens, LANES), F32),
            VMEM((chunks, 8, LANES), F32),
            VMEM((tokens + 8, width), F32),
            pltpu.SemaphoreType.DMA((14,)),
        ],
        compiler_params=pltpu.CompilerParams(vmem_limit_bytes=VMEM_LIMIT),
        cost_estimate=pl.CostEstimate(flops=2_000_000_000, bytes_accessed=4_000_000, transcendentals=0),
        name="mixer_back",
    )(*operands)


def call(kernel, name, outs, operands, smem=0, scratch=(), flops=0, limit=SMALL_LIMIT):
    moved = sum(a.size * a.dtype.itemsize for a in operands) + sum(
        math.prod(o.shape) * jnp.dtype(o.dtype).itemsize for o in outs
    )
    return pl.pallas_call(
        kernel,
        out_shape=outs,
        in_specs=specs(smem, pltpu.SMEM) + specs(len(operands) - smem),
        out_specs=specs(len(outs)),
        scratch_shapes=list(scratch),
        compiler_params=pltpu.CompilerParams(vmem_limit_bytes=limit),
        cost_estimate=pl.CostEstimate(flops=flops // EARLY, bytes_accessed=moved // EARLY, transcendentals=0),
        name=name,
    )(*operands)


def shaped(dims, kind):
    return jax.ShapeDtypeStruct(dims, kind)


def half_rows(ref, own):
    half = ref.shape[0] // 2
    low = lax.axis_index("head") % 2
    return pl.ds(pl.multiple_of((low if own else 1 - low) * half, half), half)


def seq_bits():
    at = seq_index()
    z = at // 2 % 4
    low, high = z % 2, z // 2
    return {"x": at % 2, "pair": low ^ high, "cross": high}


PARTNER = {"x": 1, "pair": 2, "cross": 6}
X_FIRST = ("x", "pair", "cross")
V_BACK = ("x", "cross", "pair")
Z_FIRST = ("pair", "cross", "x")


def half_width(ref, own, stage="x"):
    half = ref.shape[1] // 2
    low = seq_bits()[stage]
    return pl.ds(pl.multiple_of((low if own else 1 - low) * half, half), half)


def project_kernel(
    far_x, gain, far_q, far_k, far_v, far_gate, beta_w, decay_w, far_normed, far_projected, far_outgate, far_small, edge,
    x, q_w, k_w, v_w, gate_w, normed, projected, outgate, small, side_w, sems,
):
    arriving = begin(
        copies([(far_x, x), (far_q, q_w), (far_k, k_w), (far_v, v_w), (far_gate, gate_w)], sems)
    )
    gather_side(side_w, beta_w, decay_w)
    end(arriving[:1])
    x_float = x[...].astype(F32)
    low = (x_float * lax.rsqrt(jnp.mean(x_float * x_float, axis=1, keepdims=True) + EPSILON) * gain[...]).astype(BF)
    normed[...] = low
    leaving = begin(copies([(normed, far_normed)], sems, 5))
    last = x.shape[0] - edge.shape[0]
    small[...] = mm_nt(low, side_w[...])
    leaving += begin(copies([(small, far_small)], sems, 6))
    at = 0
    for k, weight in enumerate((q_w, k_w, v_w)):
        end(arriving[1 + k : 2 + k])
        piece = mm(low, weight[...]).astype(BF)
        projected[:, at : at + weight.shape[1]] = piece
        edge[:, at : at + weight.shape[1]] = piece[last:, :]
        at += weight.shape[1]
    edge[:, at:] = low[last:, :]
    leaving += begin(copies([(projected, far_projected)], sems, 7))
    end(arriving[4:])
    outgate[...] = mm(low, gate_w[...])
    leaving += begin(copies([(outgate, far_outgate)], sems, 8))
    end(leaving)


def gather_side(side_w, beta_w, decay_w):
    betas = beta_w.shape[0]
    side_w[...] = jnp.zeros(side_w.shape, F32)
    side_w[0:betas, :] = beta_w[...].astype(F32)
    side_w[betas : betas + decay_w.shape[0], :] = decay_w[...].astype(F32)


def project(x, gain, q_w, k_w, v_w, gate_w, beta_w, decay_w):
    tokens, wide = x.shape
    width = q_w.shape[1] + k_w.shape[1] + v_w.shape[1]
    outs = [
        shaped((tokens, wide), BF), shaped((tokens, width), BF),
        shaped((tokens, gate_w.shape[1]), F32), shaped((tokens, LANES), F32), shaped((16, width + wide), BF),
    ]
    operands = [x, gain.reshape(1, -1), q_w, k_w, v_w, gate_w, beta_w, decay_w]
    moved = 8 * x.size
    return pl.pallas_call(
        project_kernel,
        out_shape=outs,
        in_specs=specs(1, HBM) + specs(1) + specs(4, HBM) + specs(2),
        out_specs=specs(4, HBM) + specs(1),
        scratch_shapes=[VMEM(a.shape, a.dtype) for a in (x, q_w, k_w, v_w, gate_w)]
        + [VMEM(out.shape, out.dtype) for out in outs[:4]]
        + [VMEM((LANES, wide), F32), pltpu.SemaphoreType.DMA((9,))],
        compiler_params=pltpu.CompilerParams(vmem_limit_bytes=VMEM_LIMIT),
        cost_estimate=pl.CostEstimate(flops=8 * tokens * wide * width, bytes_accessed=moved, transcendentals=0),
        name="project",
    )(*operands)


def attend_kernel(heads, reach, out_aug, outgate, o_gain, out_weight, *rest):
    before = rest[:reach]
    mixed, branch, give, keep, state_in = rest[reach:]
    gain = o_gain[...]
    for h in range(heads):
        at = slice(h * LANES, (h + 1) * LANES)
        state = before[reach - 1][0, h].astype(F32)
        for r in range(reach - 2, -1, -1):
            state = mm(before[r][1, h], state) + before[r][0, h].astype(F32)
        state_in[h] = state
        mix = out_aug[h, :, :LANES] + mm(out_aug[h, :, LANES:], state)
        mixed[:, at] = mix
        gate = outgate[:, at]
        normed = mix * lax.rsqrt(jnp.mean(mix * mix, axis=1, keepdims=True) + EPSILON)
        branch[:, at] = (normed * gain * (gate * sigmoid(gate))).astype(BF)
    give[...] = mm(branch[half_rows(branch, False), :], out_weight[...]).astype(BF)
    keep[...] = mm(branch[half_rows(branch, True), :], out_weight[...])


def attend(out_aug, outgate, o_gain, out_weight, before):
    heads, tokens, _ = out_aug.shape
    wide = out_weight.shape[1]
    outs = [
        shaped((tokens, heads * LANES), F32), shaped((tokens, heads * LANES), BF),
        shaped((tokens // 2, wide), BF), shaped((tokens // 2, wide), F32), shaped((heads, LANES, LANES), F32),
    ]
    operands = [out_aug, outgate, o_gain.reshape(1, -1), out_weight, *before]
    return call(
        functools.partial(attend_kernel, heads, len(before)), "attend", outs, operands,
        flops=2 * tokens * wide * heads * LANES,
    )


def enter_kernel(x, mine, other, gain, hidden, normed):
    value = x[half_rows(x, True), :].astype(F32) + mine[...].astype(F32) + other[...].astype(F32)
    hidden[...] = value
    normed[...] = (
        value * lax.rsqrt(jnp.mean(value * value, axis=1, keepdims=True) + EPSILON) * gain[...]
    ).astype(BF)


def enter(x, mine, other, gain):
    outs = [shaped(mine.shape, F32), shaped(mine.shape, BF)]
    return call(enter_kernel, "enter", outs, [x, mine, other, gain.reshape(1, -1)])


def near_units(units, own):
    near = lax.axis_index("near")
    return pl.ds(pl.multiple_of((near if own else 1 - near) * (units // 2), 16), units // 2)


def half_lanes(ref, own):
    half = ref.shape[1] // 2
    low = lax.axis_index("head") % 2
    return pl.ds(pl.multiple_of((low if own else 1 - low) * half, half), half)


def feed_kernel(
    own, other, gate_w, up_w, down_w, out_grad,
    normed, d_give, d_keep, part_give, part_keep, feed_give, feed_keep,
):
    units = gate_w.shape[0]
    half = units // 2
    for mine, source, part, fed in ((False, other, part_give, feed_give), (True, own, part_keep, feed_keep)):
        rows = half_rows(normed, mine)
        lanes = half_lanes(d_give, mine)
        low = source[...]
        normed[rows, :] = low
        part_sum = jnp.zeros(part.shape, F32)
        feed_sum = jnp.zeros(fed.shape, F32)
        for near, out in ((False, d_give), (True, d_keep)):
            cut = near_units(units, near)
            gate = mm_nt(gate_w[cut, :], low)
            up = mm_nt(up_w[cut, :], low)
            d_inner = mm_nt(down_w[cut, :], out_grad[rows, :])
            sg = sigmoid(gate)
            active = gate * sg
            low_inner = (active * up).astype(BF)
            low_gate = (d_inner * up * (sg * (1.0 + gate * (1.0 - sg)))).astype(BF)
            low_up = (d_inner * active).astype(BF)
            out[0:half, lanes] = low_gate
            out[half : 2 * half, lanes] = low_up
            out[2 * half : 3 * half, lanes] = low_inner
            part_sum += mm_tn(low_gate, gate_w[cut, :]) + mm_tn(low_up, up_w[cut, :])
            feed_sum += mm_tn(low_inner, down_w[cut, :])
        part[...] = part_sum.astype(part.dtype)
        fed[...] = feed_sum.astype(fed.dtype)


def feed(own, other, gate_w, up_w, down_w, out_grad):
    tokens, wide = out_grad.shape
    units = gate_w.shape[0]
    half = (tokens // 2, wide)
    outs = [shaped((tokens, wide), BF)] + [shaped((3 * units // 2, tokens), BF)] * 2 + [
        shaped(half, BF), shaped(half, F32), shaped(half, BF), shaped(half, F32),
    ]
    operands = [own, other, gate_w, up_w, down_w, out_grad]
    return call(feed_kernel, "feed", outs, operands, flops=12 * tokens * wide * units)


def leave_kernel(mine, other, hidden, gain, out_grad, d_hidden, low, d_gain):
    grad = mine[...].astype(F32) + other[...].astype(F32)
    value = hidden[...]
    scale = lax.rsqrt(jnp.mean(value * value, axis=1, keepdims=True) + EPSILON)
    unit = value * scale
    d_gain[...] = jnp.sum(grad * unit, axis=0, keepdims=True)
    d_unit = grad * gain[...]
    total = out_grad[half_rows(out_grad, True), :].astype(F32) + scale * (
        d_unit - unit * jnp.mean(d_unit * unit, axis=1, keepdims=True)
    )
    d_hidden[...] = total
    low[...] = total.astype(BF)


def leave(mine, other, hidden, gain, out_grad):
    outs = [shaped(mine.shape, F32), shaped(mine.shape, BF), shaped((1, mine.shape[1]), F32)]
    return call(leave_kernel, "leave", outs, [mine, other, hidden, gain.reshape(1, -1), out_grad])


def finish_kernel(mine, other, x, gain, d_hidden, low, d_gain):
    grad = mine[...].astype(F32) + other[...].astype(F32)
    value = x[half_rows(x, True), :].astype(F32)
    scale = lax.rsqrt(jnp.mean(value * value, axis=1, keepdims=True) + EPSILON)
    unit = value * scale
    d_gain[...] = jnp.sum(grad * unit, axis=0, keepdims=True)
    d_unit = grad * gain[...]
    low[...] = (
        d_hidden[...] + scale * (d_unit - unit * jnp.mean(d_unit * unit, axis=1, keepdims=True))
    ).astype(BF)


def finish(mine, other, x, gain, d_hidden):
    outs = [shaped(mine.shape, BF), shaped((1, mine.shape[1]), F32)]
    return call(finish_kernel, "finish", outs, [mine, other, x, gain.reshape(1, -1), d_hidden])


def attend_back_kernel(
    heads, own, other, out_weight, mixed, outgate, o_gain, out_aug,
    grad, d_mixed, d_outgate, d_gain, carry,
):
    gain = o_gain[...]
    gain_sum = jnp.zeros((1, LANES), F32)
    carries = [jnp.zeros((LANES, LANES), F32)] * heads
    for mine, source in ((True, own), (False, other)):
        rows = half_rows(grad, mine)
        low = source[...]
        grad[rows, :] = low
        d_branch = mm_nt(low, out_weight[...])
        for h in range(heads):
            at = slice(h * LANES, (h + 1) * LANES)
            mix = mixed[rows, at]
            gate = outgate[rows, at]
            grad_h = d_branch[:, at]
            scale = lax.rsqrt(jnp.mean(mix * mix, axis=1, keepdims=True) + EPSILON)
            normed = mix * scale
            sg = sigmoid(gate)
            through = grad_h * (gate * sg)
            gain_sum += jnp.sum(through * normed, axis=0, keepdims=True)
            d_normed = through * gain
            d_mix = (scale * (d_normed - normed * jnp.mean(d_normed * normed, axis=1, keepdims=True))).astype(BF)
            d_mixed[rows, at] = d_mix
            d_outgate[rows, at] = (grad_h * normed * gain * (sg * (1.0 + gate * (1.0 - sg)))).astype(BF)
            carries[h] += mm_tn(out_aug[h, rows, LANES:], d_mix)
    for h in range(heads):
        carry[h] = carries[h].astype(carry.dtype)
    d_gain[...] = gain_sum


def attend_back(own, other, out_weight, mixed, outgate, o_gain, out_aug):
    heads, tokens, _ = out_aug.shape
    wide = out_weight.shape[1]
    outs = [
        shaped((tokens, wide), BF), shaped((tokens, heads * LANES), BF), shaped((tokens, heads * LANES), BF),
        shaped((1, LANES), F32), shaped((heads, LANES, LANES), BF),
    ]
    operands = [own, other, out_weight, mixed, outgate, o_gain.reshape(1, -1), out_aug]
    return call(
        functools.partial(attend_back_kernel, heads), "attend_back", outs, operands,
        flops=2 * tokens * wide * heads * LANES,
    )


def store_rows_cut(part, at, piece):
    quarters = part.shape[0]
    rows = piece.shape[0] // quarters
    for q in range(quarters):
        for i in range(piece.shape[1] // LANES):
            part[q, at + i * rows : at + (i + 1) * rows, :] = piece[
                q * rows : (q + 1) * rows, i * LANES : (i + 1) * LANES
            ].astype(BF)


def store_cols_cut(part, at, piece):
    for q in range(part.shape[0]):
        part[q, at : at + piece.shape[0], :] = piece[:, q * LANES : (q + 1) * LANES].astype(BF)


def feed_weights_kernel(
    d_own, normed, out_grad, d_near, normed_mine, normed_other, grad_mine, grad_other, grads
):
    half = d_own.shape[0] // 3
    for k in range(3):
        right, mine, other = (out_grad, grad_mine, grad_other) if k == 2 else (normed, normed_mine, normed_other)
        rows = slice(k * half, (k + 1) * half)
        total = mm(d_own[rows, :], right[...])
        total += mm(d_near[rows, half_lanes(d_near, True)], mine[...])
        total += mm(d_near[rows, half_lanes(d_near, False)], other[...])
        grads[rows, :] = total.astype(BF)


def feed_weights(d_own, normed, out_grad, d_near, normed_mine, normed_other, grad_mine, grad_other):
    tokens, wide = normed.shape
    rows = d_own.shape[0]
    operands = [d_own, normed, out_grad, d_near, normed_mine, normed_other, grad_mine, grad_other]
    (grads,) = call(
        feed_weights_kernel, "feed_weights", [shaped((rows, wide), BF)], operands, flops=4 * tokens * wide * rows
    )
    return grads


def feed_out_kernel(mine, other, *outs):
    units = outs[0].shape[0]
    half = units // 2
    for own, ref in ((True, mine), (False, other)):
        for k, out in enumerate(outs):
            out[near_units(units, own), :] = ref[k * half : (k + 1) * half, :].astype(F32)


def gate_weights_kernel(normed, d_outgate, branch, grad, give, keep):
    for own, part in ((False, give), (True, keep)):
        store_rows_cut(part, 0, mm_tn(normed[:, half_width(normed, own)], d_outgate[...]))
        store_cols_cut(part, d_outgate.shape[1], mm_tn(branch[...], grad[:, half_width(grad, own)]))


def gate_weights(normed, d_outgate, branch, grad):
    rows = d_outgate.shape[1] + branch.shape[1]
    outs = [shaped((4, rows, LANES), BF)] * 2
    operands = [normed, d_outgate, branch, grad]
    return call(
        gate_weights_kernel, "gate_weights", outs, operands, flops=2 * normed.shape[0] * normed.shape[1] * rows
    )


def mix_weights_kernel(first, normed, halo, d_cols, d_halo, *rest):
    *side, give, keep = rest
    low_halo = d_halo[...].astype(BF)
    for own, part in ((False, give), (True, keep)):
        at = half_width(normed, own, first)
        left = normed[:, at]
        total = mm_tn(left, d_cols[...]) + mm_tn(halo[halo.shape[0] - d_halo.shape[0] :, at], low_halo)
        store_rows_cut(part, 0, total)
        if side:
            store_cols_cut(part, d_cols.shape[1], mm_tn(side[0][...], left)[:16])


def mix_weights(first, normed, halo, d_cols, d_halo, *side):
    tokens, wide = normed.shape
    rows = d_cols.shape[1] + 16 * len(side)
    operands = [normed, halo, d_cols, d_halo, *side]
    return call(
        functools.partial(mix_weights_kernel, first), "mix_weights", [shaped((4, rows, LANES), BF)] * 2,
        operands, flops=2 * tokens * wide * rows,
    )


def unproject_kernel(
    d_kq, d_v, tail, following, d_outgate, d_small, q_w, k_w, v_w, gate_w, beta_w, decay_w, give, keep,
    joined, side_w,
):
    tokens, width = joined.shape
    wide_q, wide_k = q_w.shape[1], k_w.shape[1]
    joined[:, 0:wide_q] = d_kq[:, wide_k:]
    joined[:, wide_q : wide_q + wide_k] = d_kq[:, :wide_k]
    joined[:, wide_q + wide_k :] = d_v[...]
    joined[tokens - 16 :, :] = jnp.concatenate([tail[0:8, :], tail[8:16, :] + following[...]], axis=0).astype(BF)
    gather_side(side_w, beta_w, decay_w)
    for own, part in ((False, give), (True, keep)):
        rows = half_rows(joined, own)
        total = mm_nt(d_outgate[rows, :], gate_w[...]) + mm(d_small[rows, :], side_w[...])
        at = 0
        for weight in (q_w, k_w, v_w):
            total += mm_nt(joined[rows, at : at + weight.shape[1]], weight[...])
            at += weight.shape[1]
        part[...] = total.astype(part.dtype)


def unproject(d_kq, d_v, tail, following, d_outgate, d_small, q_w, k_w, v_w, gate_w, beta_w, decay_w):
    tokens = d_v.shape[0]
    wide, width = q_w.shape[0], tail.shape[1]
    half = (tokens // 2, wide)
    operands = [d_kq, d_v, tail, following, d_outgate, d_small, q_w, k_w, v_w, gate_w, beta_w, decay_w]
    return call(
        unproject_kernel, "unproject", [shaped(half, BF), shaped(half, F32)], operands,
        scratch=[VMEM((tokens, width), BF), VMEM((LANES, wide), F32)],
        flops=2 * tokens * (width + 384) * wide,
    )


def fold_kernel(stage, keep, got, *outs):
    if len(outs) == 1:
        outs[0][...] = (keep[...].astype(F32) + got[...].astype(F32)).astype(BF)
        return
    mine = seq_bits()[stage]
    half = keep.shape[0] // 2
    for own, out in ((False, outs[0]), (True, outs[1])):
        at = (mine if own else 1 - mine) * half
        for k in range(half):
            out[k] = (keep[at + k].astype(F32) + got[at + k].astype(F32)).astype(BF)


def fold(stage, keep, got):
    count, rows, lanes = keep.shape
    outs = [shaped((count // 2, rows, lanes), BF)] * 2 if stage else [shaped(keep.shape, BF)]
    return call(functools.partial(fold_kernel, stage), "fold", outs, [keep, got])


class Line:
    def __init__(self):
        self.last = None

    def after(self, *arrays):
        if self.last is None:
            return arrays
        return lax.optimization_barrier((*arrays, self.last))[:-1]

    def step(self, function, *arrays):
        result = function(*self.after(*arrays))
        self.last = jax.tree.leaves(result)[0]
        return result


class Sum:
    def __init__(self, line, order, give, keep, back=None):
        self.line, self.order, self.keep, self.at = line, order, keep, 0
        self.back = order[::-1] if back is None else back
        self.got = swapped(give, SEQ, PARTNER[order[0]])

    def next(self):
        stages = len(self.order)
        self.at += 1
        if self.at < stages:
            give, self.keep = self.line.step(
                functools.partial(fold, self.order[self.at]), self.keep, self.got
            )
            self.got = swapped(give, SEQ, PARTNER[self.order[self.at]])
            return
        if self.at == stages:
            (mine,) = self.line.step(functools.partial(fold, None), self.keep, self.got)
            bit = 8
            while bit < seq_size():
                mine = (mine.astype(F32) + swapped(mine, SEQ, bit).astype(F32)).astype(BF)
                bit *= 2
        else:
            mine = self.line.step(lambda *parts: jnp.concatenate(parts, axis=0), self.keep, self.got)
        self.keep = mine
        self.got = swapped(mine, SEQ, PARTNER[self.back[self.at - stages]])

    def finish(self, kernel, name, outs):
        return self.line.step(
            lambda *parts: call(functools.partial(kernel, (self.order, self.back)), name, outs, list(parts)), self.keep, self.got
        )


def blocks_of(orders, mine, other):
    order, back = orders
    bits = seq_bits()
    for last, ref in ((0, mine), (1, other)):
        for slot in range(4):
            flips = dict(zip(back, (slot % 2, slot // 2, last)))
            first, second, third = (bits[stage] ^ flips[stage] for stage in order)
            yield 4 * first + 2 * second + third, ref, slot


def at_block(index):
    return pl.ds(pl.multiple_of(index * LANES, LANES), LANES)


def load_rows_cut(ref, slot, at, count):
    return [ref[slot, at + i * LANES : at + (i + 1) * LANES, :].astype(F32) for i in range(count)]


def gate_out_kernel(order, mine, other, outgate, out):
    for index, ref, slot in blocks_of(order, mine, other):
        width = outgate.shape[1]
        for i, piece in enumerate(load_rows_cut(ref, slot, 0, width // LANES)):
            outgate[at_block(index), i * LANES : (i + 1) * LANES] = piece
        out[:, at_block(index)] = ref[slot, width : width + out.shape[0], :].astype(F32)


def mix_out_kernel(side, order, mine, other, *outs):
    wide = outs if not side else outs[:-2]
    for index, ref, slot in blocks_of(order, mine, other):
        at = 0
        for out in wide:
            for i, piece in enumerate(load_rows_cut(ref, slot, at, out.shape[1] // LANES)):
                out[at_block(index), i * LANES : (i + 1) * LANES] = piece
            at += out.shape[1]
        if side:
            pieces = ref[slot, at : at + 16, :].astype(F32)
            at = 0
            for part in outs[-2:]:
                part[:, at_block(index)] = pieces[at : at + part.shape[0], :]
                at += part.shape[0]


def shifted(value, axis, steps):
    count = seq_size()
    leading, last = max(0, -steps), min(count, count - steps)
    return lax.ppermute(value, axis, [(source, source + steps) for source in range(leading, last)])


def swapped(value, axis, bit):
    return lax.ppermute(value, axis, [(s, s ^ bit) for s in range(seq_size() if axis == SEQ else lax.axis_size(axis))])


def head_sum(give, keep):
    total = keep + swapped(give, "head", 1).astype(F32)
    mine = total.astype(BF)
    other = swapped(mine, "head", 2)
    bit = 4
    while bit < lax.axis_size("head"):
        mine = (mine.astype(F32) + other.astype(F32)).astype(BF)
        other = swapped(mine, "head", bit)
        bit *= 2
    return mine, other


def both_halves(mine):
    low = lax.axis_index("head") % 2
    other = swapped(mine, "head", 1)
    return jnp.concatenate([jnp.where(low == 0, mine, other), jnp.where(low == 0, other, mine)], axis=0)


def reach_of(tokens, count):
    whole = tokens * count
    longest = whole // 4 + 2 * (whole // 64 - 1)
    return max(1, min(count - 1, -(-(longest - 1) // tokens)))


def local(
    block_in, seq_start, attn_gain, q_weight, k_weight, v_weight, conv_q, conv_k, conv_v,
    beta_weight, decay_weight, a_log, dt_bias, outgate_weight, o_gain, out_weight,
    mlp_gain, gate_weight, up_weight, down_weight, out_grad,
):
    tokens = block_in.shape[0]
    heads = a_log.shape[0]
    width_q = q_weight.shape[1]
    width_k = k_weight.shape[1]
    width = width_q + 2 * width_k
    betas = beta_weight.shape[1]
    reach = reach_of(tokens, seq_size())
    wide = block_in.shape[1]
    units = gate_weight.shape[1]
    beta_rows, decay_rows = beta_weight.T, decay_weight.T
    core = lax.axis_index("head") % 2
    grad_mine = swapped(lax.dynamic_slice_in_dim(out_grad, core * (tokens // 2), tokens // 2, 0), SEQ, 1)
    normed, projected, outgate, small, edge = project(
        block_in, attn_gain, q_weight, k_weight, v_weight, outgate_weight, beta_rows, decay_rows
    )
    halo = shifted(edge, SEQ, 1)
    halo, normed_halo = halo[:, :width], halo[:, width:]
    mixer_args = (seq_start, a_log, dt_bias, projected, halo, conv_q, conv_k, conv_v, small)
    prepared = mixer_prep(*mixer_args)
    out_aug, saved, final_state, final_map = prepared[0], prepared[1:13], prepared[13], prepared[14]
    final_state, grad_mine = lax.optimization_barrier((final_state, grad_mine))
    grad_other = swapped(grad_mine, "head", 1)
    pair = jnp.stack([final_state, final_map])
    before = [shifted(pair, SEQ, r) for r in range(1, reach)] + [shifted(final_state[None], SEQ, reach)]
    later = [shifted(final_map, SEQ, -r) for r in range(1, reach)]
    mixed, branch, give, keep, state_in = attend(out_aug, outgate, o_gain, out_weight, before)
    hidden, normed_own = enter(block_in, *head_sum(give, keep), mlp_gain)
    near_mine = swapped(normed_own, SEQ, 1)
    normed_mlp, d_give, d_keep, part_give, part_keep, feed_give, feed_keep = feed(
        normed_own, swapped(normed_own, "head", 1), gate_weight.T, up_weight.T, down_weight, out_grad
    )
    line = Line()
    part_mine, part_other = head_sum(part_give, part_keep)
    line.last = part_mine
    d_give, near_mine = lax.optimization_barrier((d_give, near_mine))
    d_near = swapped(d_give, SEQ, 1)
    near_other = swapped(near_mine, "head", 1)
    d_hidden, attention_own, grad_mlp_gain = line.step(leave, part_mine, part_other, hidden, mlp_gain, out_grad)
    attention_gradient, grad_mixed, grad_outgate, grad_o_part, carry = line.step(
        attend_back, attention_own, swapped(attention_own, "head", 1), out_weight, mixed, outgate, o_gain, out_aug
    )
    after = [shifted(carry, SEQ, -r) for r in range(1, reach + 1)]
    feed_grads = line.step(
        feed_weights, d_keep, normed_mlp, out_grad, d_near, near_mine, near_other, grad_mine, grad_other
    )
    feed_sums = lax.psum(feed_grads, "far")
    feed_near = swapped(feed_sums, SEQ, 1)
    sum_out = Sum(line, X_FIRST, *line.step(gate_weights, normed, grad_outgate, branch, attention_gradient))
    feed_mine, feed_other = head_sum(feed_give, feed_keep)
    output = both_halves((hidden + feed_mine.astype(F32) + feed_other.astype(F32)).astype(BF))
    d_kq, d_v, tail, d_halo, grad_small, grad_taps, grad_scalars = line.step(
        lambda d_mixed: mixer_back(*mixer_args, saved, state_in, d_mixed, after, later), grad_mixed
    )
    following = shifted(d_halo, SEQ, -1)
    cut_q, cut_k, cut_v = slice(0, width_q), slice(width_q, width_q + width_k), slice(width_q + width_k, width)
    halo_kq = jnp.concatenate([d_halo[:, cut_k], d_halo[:, cut_q]], axis=1)
    sum_kq = Sum(
        line, X_FIRST, *line.step(functools.partial(mix_weights, X_FIRST[0]), normed, normed_halo, d_kq, halo_kq)
    )
    sum_v = Sum(
        line, X_FIRST,
        *line.step(functools.partial(mix_weights, X_FIRST[0]), normed, normed_halo, d_v, d_halo[:, cut_v], grad_small),
        back=V_BACK,
    )
    taps = conv_q.shape[0]

    def padded(*rows):
        joined = jnp.concatenate(rows, axis=1)
        return jnp.pad(joined, ((0, 0), (0, width - joined.shape[1])))

    for part in (sum_kq, sum_out, sum_v):
        part.next()
    mine, other = head_sum(
        *line.step(
            unproject, d_kq, d_v, tail, following, grad_outgate, grad_small,
            q_weight, k_weight, v_weight, outgate_weight, beta_rows, decay_rows,
        )
    )
    line.last = feed_sums
    for part in (sum_kq, sum_out, sum_v):
        part.next()
    line.last = feed_sums
    input_own, grad_attn_gain = line.step(finish, mine, other, block_in, attn_gain, d_hidden)
    grad_input = both_halves(input_own)
    small_sums = jnp.concatenate(
        [
            grad_taps[:taps], padded(grad_scalars[0:1], grad_scalars[1:2]),
            padded(grad_attn_gain), padded(grad_mlp_gain), padded(grad_o_part),
        ],
        axis=0,
    )
    bits = [1 << k for k in range(1, seq_size().bit_length() - 1)] + [1]
    small_got = swapped(small_sums, SEQ, bits[0])
    rounds = 0
    while rounds < max(3, len(bits)):
        if rounds == 2:
            line.last = feed_near
        for part in (sum_kq, sum_out, sum_v) if rounds < 3 else ():
            part.next()
        rounds += 1
        if rounds <= len(bits):
            small_sums = line.step(jnp.add, small_sums, small_got)
        if rounds < len(bits):
            small_got = swapped(small_sums, SEQ, bits[rounds])
    gains = small_sums[taps + 1 : taps + 4]
    gains = gains + swapped(gains, "head", 1)
    grad_o_gain = gains[2:3, :LANES]
    bit = 2
    while bit < lax.axis_size("head"):
        grad_o_gain = grad_o_gain + swapped(grad_o_gain, "head", bit)
        bit *= 2
    grad_outgate_w, grad_out_w = sum_out.finish(
        gate_out_kernel, "gate_out", [shaped((wide, width_q), F32), shaped((width_q, wide), F32)]
    )
    grad_v_w, grad_beta_w, grad_decay_w = sum_v.finish(
        functools.partial(mix_out_kernel, True), "mix_out",
        [shaped((wide, width_k), F32), shaped((betas, wide), F32), shaped((heads, wide), F32)],
    )
    grad_k_w, grad_q_w = sum_kq.finish(
        functools.partial(mix_out_kernel, False), "mix_out",
        [shaped((wide, width_k), F32), shaped((wide, width_q), F32)],
    )
    grad_gate_w, grad_up_w, grad_down_w = call(
        feed_out_kernel, "feed_out", [shaped((units, wide), F32)] * 3, [feed_sums, feed_near]
    )
    rate, shift = small_sums[taps, betas : betas + heads], small_sums[taps, LANES + betas : LANES + betas + heads]
    return (
        output, grad_input, gains[0, :wide], grad_q_w, grad_k_w, grad_v_w,
        small_sums[:taps, cut_q], small_sums[:taps, cut_k], small_sums[:taps, cut_v],
        grad_beta_w.T, grad_decay_w.T, rate, shift, grad_outgate_w, grad_o_gain[0], grad_out_w, gains[1, :wide],
        grad_gate_w.T, grad_up_w.T, grad_down_w,
    )


def solution(mesh):
    placed = (
        P(SEQ, None), P(), P(), P(None, "head"), P(None, "head"), P(None, "head"), P(None, "head"),
        P(None, "head"), P(None, "head"), P(None, "head"), P(None, "head"), P("head"), P("head"),
        P(None, "head"), P(), P("head", None), P(), P(None, "head"), P(None, "head"), P("head", None),
        P(SEQ, None),
    )
    given = (
        P(SEQ, None), P(SEQ, None), P(), P(None, "head"), P(None, "head"), P(None, "head"),
        P(None, "head"), P(None, "head"), P(None, "head"), P(None, "head"), P(None, "head"), P("head"),
        P("head"), P(None, "head"), P(), P("head", None), P(), P(None, "head"), P(None, "head"),
        P("head", None),
    )
    seq, head = mesh.devices.shape
    mesh = jax.sharding.Mesh(mesh.devices.reshape(seq // 2, 2, head), ("far", "near", "head"))
    return jax.shard_map(local, mesh=mesh, in_specs=placed, out_specs=given, check_vma=False)
```

```python
import functools
import math
import jax
import jax.numpy as jnp
from jax import lax
from jax.experimental import pallas as pl
from jax.experimental.pallas import tpu as pltpu
from jax.sharding import PartitionSpec as P

NH = 2
GROUP = 64
LANES = 128
EPSILON = 1e-06
BF = jnp.bfloat16
F32 = jnp.float32
VMEM = pltpu.VMEM
HBM = pltpu.HBM
VMEM_LIMIT = 60 * 1024 * 1024
SMALL_LIMIT = 24 * 1024 * 1024
EARLY = 64
SEQ = ("far", "near")


def seq_index():
    return lax.axis_index("far") * 2 + lax.axis_index("near")


def seq_size():
    return lax.axis_size("far") * lax.axis_size("near")


def mm(left, right):
    return jnp.dot(left.astype(BF), right.astype(BF), preferred_element_type=F32)


def mm_nt(left, right):
    return lax.dot_general(
        left.astype(BF), right.astype(BF), (((1,), (1,)), ((), ())), preferred_element_type=F32
    )


def mm_tn(left, right):
    return lax.dot_general(
        left.astype(BF), right.astype(BF), (((0,), (0,)), ((), ())), preferred_element_type=F32
    )


def mm_exact(left, right):
    return jnp.dot(left, right, preferred_element_type=F32, precision=lax.Precision.HIGHEST)


def sigmoid(values):
    return 1.0 / (1.0 + jnp.exp(-values))


def softplus(values):
    return jnp.maximum(values, 0.0) + jnp.log1p(jnp.exp(-jnp.abs(values)))


def documents_at(starts, positions):
    total = jnp.zeros(positions.shape, jnp.int32)
    for k in range(starts.shape[0]):
        total = total + (starts[k] <= positions).astype(jnp.int32)
    return total


def sub_order(index):
    return NH * (index % GROUP) + index // GROUP


def order_pair():
    rows = sub_order(lax.broadcasted_iota(jnp.int32, (LANES, LANES), 0))
    cols = sub_order(lax.broadcasted_iota(jnp.int32, (LANES, LANES), 1))
    return rows, cols


def gate_columns(small, log_rate, bias, heads):
    lane = lax.broadcasted_iota(jnp.int32, (1, LANES), 1)
    rate = jnp.zeros((1, LANES), F32)
    shift = jnp.zeros((1, LANES), F32)
    for h in range(heads):
        at = lane == NH * heads + h
        rate = jnp.where(at, -jnp.exp(jnp.full((1, LANES), log_rate[h], F32)), rate)
        shift = jnp.where(at, bias[h], shift)
    return sigmoid(small), rate * softplus(small + shift), small + shift, rate


def chunk_decays(rows, cols_ref, row_ref, doc_ref, c, h, heads, doc_before):
    cum_col = cols_ref[rows, NH * heads + h : NH * heads + h + 1]
    doc_col = doc_ref[rows, 0:1]
    packed = row_ref[c]
    cum_row = packed[NH * heads + h : NH * heads + h + 1, :]
    doc_row = packed[NH * heads + heads : NH * heads + heads + 1, :]
    token_row = lax.broadcasted_iota(jnp.int32, (GROUP, LANES), 1) % GROUP
    token_col = lax.broadcasted_iota(jnp.int32, (GROUP, LANES), 0)
    seen = (token_col >= token_row) & (doc_col == doc_row)
    pair = jnp.where(seen, jnp.exp(jnp.where(seen, cum_col - cum_row, 0.0)), 0.0)
    start = jnp.where(doc_col == doc_before, jnp.exp(cum_col), 0.0)
    cum_last = cum_col[GROUP - 1 :, :]
    doc_last = doc_col[GROUP - 1 :, :]
    to_end = jnp.where(doc_col == doc_last, jnp.exp(cum_last - cum_col), 0.0)
    return pair, start, to_end


def two(array):
    return jnp.concatenate([array, array], axis=0)


def beta_pair(rows, cols_ref, row_ref, c, h):
    lane = lax.broadcasted_iota(jnp.int32, (1, LANES), 1)
    packed = row_ref[c]
    row = jnp.where(lane < GROUP, packed[NH * h : NH * h + 1, :], packed[NH * h + 1 : NH * h + 2, :])
    col = jnp.concatenate(
        [cols_ref[rows, NH * h : NH * h + 1], cols_ref[rows, NH * h + 1 : NH * h + 2]], axis=0
    )
    return row, col


def copies(pairs, sems, first=0):
    return [
        pltpu.make_async_copy(source, target, sems.at[first + k]) for k, (source, target) in enumerate(pairs)
    ]


def begin(waiting):
    for copy in waiting:
        copy.start()
    return waiting


def end(waiting):
    for copy in waiting:
        copy.wait()


def prep_kernel(
    heads, starts, log_rate, bias, far_proj, halo, conv_q, conv_k, conv_v, far_small,
    out_aug, far_state_aug, far_wy_k, far_wy_v, far_inverse, far_step_p, far_query_map, far_keys, far_queries,
    far_conv_total, far_cols, far_doc, far_row,
    final_state, final_map,
    proj, small, state_aug, wy_k, wy_v, inverse, step_p, query_map, keys, queries, conv_total, cols, doc, row,
    ext, vals, score_map, step_b, masks, sems,
):
    arriving = begin(copies([(far_small, small), (far_proj, proj)], sems))
    tokens = proj.shape[0]
    chunks = tokens // GROUP
    first = seq_index() * tokens
    lead = 8
    lower_r = lax.broadcasted_iota(jnp.int32, (LANES, LANES), 0)
    lower_c = lax.broadcasted_iota(jnp.int32, (LANES, LANES), 1)
    lower = ((lower_r >= lower_c) & (lower_r // GROUP == lower_c // GROUP)).astype(F32)
    lane = lax.broadcasted_iota(jnp.int32, (LANES, LANES), 1)
    per = LANES // GROUP
    end(arriving[:1])
    for block in range(tokens // LANES):
        at = pl.ds(block * LANES, LANES)
        betas, logdec, _, _ = gate_columns(small[at, :], log_rate, bias, heads)
        cum = mm_exact(lower, logdec)
        where = lax.broadcasted_iota(jnp.int32, (LANES, LANES), 0) + (first + block * LANES)
        document = documents_at(starts, where).astype(F32)
        packed = jnp.where(lane < NH * heads, betas, jnp.where(lane < NH * heads + heads, cum, document))
        cols[at, :] = packed
        doc[at, :] = document
        turned = packed.T
        for part in range(per):
            piece = turned[0:8, part * GROUP : (part + 1) * GROUP]
            row[block * per + part] = jnp.concatenate([piece] * NH, axis=1)
    order_r, order_c = order_pair()
    level = 0
    width = 1
    while width < LANES:
        inside = (order_r // (2 * width) == order_c // (2 * width)) & (order_r // width > order_c // width)
        masks[level] = inside.astype(F32)
        level += 1
        width *= 2
    end(arriving[1:])
    ext[0:lead, :] = halo[16 - lead : 16, :].astype(F32)
    ext[lead:, :] = proj[...].astype(F32)
    width_q = heads * LANES
    width_k = NH * heads * LANES
    taps = conv_q.shape[0]

    def conv_chunk(c, _):
        base = pl.multiple_of(c * GROUP, GROUP)
        rows = pl.ds(base, GROUP)
        position = lax.broadcasted_iota(jnp.int32, (GROUP, LANES), 0) + (first + base)
        document = doc[rows, :]
        kept = [
            (documents_at(starts, position - lag).astype(F32) == document).astype(F32) for lag in range(1, taps)
        ]
        for group in range((width_q + 2 * width_k) // LANES):
            at = slice(group * LANES, (group + 1) * LANES)
            if group * LANES < width_q:
                kernel, shift = conv_q, 0
            elif group * LANES < width_q + width_k:
                kernel, shift = conv_k, width_q
            else:
                kernel, shift = conv_v, width_q + width_k
            cut = slice(at.start - shift, at.stop - shift)
            window = ext[pl.ds(base, GROUP + lead), at]
            total = kernel[taps - 1 : taps, cut] * window[lead:, :]
            for lag in range(1, taps):
                total += kernel[taps - 1 - lag : taps - lag, cut] * window[lead - lag : lead - lag + GROUP, :] * kept[lag - 1]
            conv_total[rows, at] = total
            active = total * sigmoid(total)
            if group * LANES < width_q:
                unit = active * lax.rsqrt(jnp.sum(active * active, axis=1, keepdims=True) + EPSILON)
                queries[group, c] = (unit * LANES ** (-0.5)).astype(BF)
            elif group * LANES < width_q + width_k:
                piece = group - width_q // LANES
                unit = active * lax.rsqrt(jnp.sum(active * active, axis=1, keepdims=True) + EPSILON)
                keys[piece // NH, c, (piece % NH) * GROUP : (piece % NH + 1) * GROUP] = unit.astype(BF)
            else:
                piece = group - (width_q + width_k) // LANES
                vals[piece // NH, c, (piece % NH) * GROUP : (piece % NH + 1) * GROUP] = active.astype(BF)
        return 0

    lax.fori_loop(0, chunks, conv_chunk, 0)
    leaving = begin(
        copies(
            [
                (conv_total, far_conv_total), (keys, far_keys), (queries, far_queries),
                (cols, far_cols), (doc, far_doc), (row, far_row),
            ],
            sems, 2,
        )
    )

    strict = order_r > order_c
    eye = (lower_r == lower_c).astype(F32)
    together = 4

    def part_chunks(step, _):
        jobs = []
        for k in range(together):
            c = step * together + k
            rows = pl.ds(pl.multiple_of(c * GROUP, GROUP), GROUP)
            before = documents_at(starts, jnp.full((1, 1), first + c * GROUP - 1, jnp.int32)).astype(F32)
            for h in range(heads):
                pair, start, to_end = chunk_decays(rows, cols, row, doc, c, h, heads, before)
                beta_row, beta_col = beta_pair(rows, cols, row, c, h)
                key = keys[h, c]
                query = queries[h, c]
                grams = mm_nt(jnp.concatenate([key, query], axis=0), key)
                system = jnp.where(strict, grams[:LANES] * two(pair), 0.0) * beta_row
                scores = grams[LANES:] * pair * beta_row
                jobs.append((c, h, start, to_end, beta_col, key, query, system, scores))
        inverses = [eye - job[7] * masks[0] for job in jobs]
        for n in range(1, level):
            halves = [mm(job[7] * masks[n], inv) for job, inv in zip(jobs, inverses)]
            inverses = [inv - mm(inv, half) for inv, half in zip(inverses, halves)]
        for job, inv in zip(jobs, inverses):
            c, h, start, to_end, beta_col, key, query, system, scores = job
            low_inv = inv.astype(BF)
            inverse[h, c] = low_inv
            key_f = key.astype(F32)
            both = mm(low_inv, jnp.concatenate([(two(start) * key_f).astype(BF), vals[h, c]], axis=1)).astype(BF)
            wy_k[h, c] = both[:, :LANES]
            wy_v[h, c] = both[:, LANES:]
            carried = (beta_col * two(to_end) * key_f).astype(BF)
            ahead = mm_tn(carried, both)
            step_p[h, c] = ahead[:, :LANES].astype(BF)
            step_b[h, c] = ahead[:, LANES:]
            scored = mm(scores, both)
            query_map[h, c] = (start * query.astype(F32) - scored[:, :LANES]).astype(BF)
            score_map[h, c] = scored[:, LANES:]
        return 0

    lax.fori_loop(0, chunks // together, part_chunks, 0)
    leaving += begin(
        copies(
            [
                (wy_k, far_wy_k), (wy_v, far_wy_v), (inverse, far_inverse), (step_p, far_step_p),
                (query_map, far_query_map),
            ],
            sems, 8,
        )
    )

    zero = jnp.zeros((LANES, LANES), F32)

    def advance(c, carry):
        rows = pl.ds(pl.multiple_of(c * GROUP, GROUP), GROUP)
        before = documents_at(starts, jnp.full((1, 1), first + c * GROUP - 1, jnp.int32)).astype(F32)
        new = []
        for h in range(heads):
            state = carry[h]
            low_state = state.astype(BF)
            state_aug[h, c] = low_state
            last = cols[rows, NH * heads + h : NH * heads + h + 1][GROUP - 1 :, :]
            whole = jnp.where(doc[rows, 0:1][GROUP - 1 :, :] == before, jnp.exp(last), 0.0)
            new.append(
                whole * state - mm(step_p[h, c], low_state) + jnp.concatenate([step_b[h, c], zero], axis=1)
            )
            mapped = mm(query_map[h, c], low_state)
            out_aug[h, rows, :] = jnp.concatenate([mapped[:, :LANES] + score_map[h, c], mapped[:, LANES:]], axis=1)
        return tuple(new)

    initial = jnp.concatenate([zero, eye], axis=1)
    last = lax.fori_loop(0, chunks, advance, (initial,) * heads)
    leaving += begin(copies([(state_aug, far_state_aug)], sems, 13))
    for h in range(heads):
        final_state[h] = last[h][:, :LANES].astype(final_state.dtype)
        final_map[h] = last[h][:, LANES:].astype(final_map.dtype)
    end(leaving)


def specs(count, space=None):
    return [pl.BlockSpec(memory_space=space or pltpu.VMEM)] * count


def mixer_prep(starts, log_rate, bias, proj, halo, conv_q, conv_k, conv_v, small):
    tokens, width = proj.shape
    heads = log_rate.shape[0]
    chunks = tokens // GROUP
    square = (heads, chunks, LANES, LANES)
    shape = jax.ShapeDtypeStruct
    outs = [
        shape((heads, tokens, 2 * LANES), F32),
        shape((heads, chunks, LANES, 2 * LANES), BF),
        shape(square, BF),
        shape(square, BF),
        shape(square, BF),
        shape(square, BF),
        shape((heads, chunks, GROUP, LANES), BF),
        shape(square, BF),
        shape((heads, chunks, GROUP, LANES), BF),
        shape((tokens, width), F32),
        shape((tokens, LANES), F32),
        shape((tokens, LANES), F32),
        shape((chunks, 8, LANES), F32),
        shape((heads, LANES, LANES), BF),
        shape((heads, LANES, LANES), BF),
    ]
    return pl.pallas_call(
        functools.partial(prep_kernel, heads),
        out_shape=outs,
        in_specs=specs(3, pltpu.SMEM) + specs(1, HBM) + specs(4) + specs(1, HBM),
        out_specs=specs(1) + specs(12, HBM) + specs(2),
        scratch_shapes=[VMEM(proj.shape, BF), VMEM(small.shape, F32)]
        + [VMEM(out.shape, out.dtype) for out in outs[1:13]]
        + [
            VMEM((tokens + 8, width), F32),
            VMEM(square, BF),
            VMEM((heads, chunks, GROUP, LANES), F32),
            VMEM(square, F32),
            VMEM((8, LANES, LANES), F32),
            pltpu.SemaphoreType.DMA((14,)),
        ],
        compiler_params=pltpu.CompilerParams(vmem_limit_bytes=VMEM_LIMIT),
        cost_estimate=pl.CostEstimate(flops=24_000_000_000, bytes_accessed=4_000_000, transcendentals=0),
        name="mixer_prep",
    )(starts, log_rate, bias, proj, halo, conv_q, conv_k, conv_v, small)


def back_kernel(
    heads, reach, starts, log_rate, bias, far_proj, halo, conv_q, conv_k, conv_v, far_small,
    far_state_aug, far_wy_k, far_wy_v, far_inverse, far_step_p, far_query_map, far_keys, far_queries,
    far_conv_total, far_cols, far_doc, far_row, state_in, d_mixed, *rest,
):
    after = rest[:reach]
    later = rest[reach : 2 * reach - 1]
    (
        d_kq, d_v, tail, d_halo, d_small, d_taps, d_scalars,
        proj, small, state_aug, wy_k, wy_v, inverse, step_p, query_map, keys, queries, conv_total, cols, doc, row,
        ext, state_grads, d_query, d_key, d_value, col_grads, row_grads, d_total, sems,
    ) = rest[2 * reach - 1 :]
    arriving = begin(
        copies(
            [
                (far_step_p, step_p), (far_query_map, query_map), (far_cols, cols), (far_doc, doc), (far_row, row),
                (far_state_aug, state_aug), (far_wy_k, wy_k), (far_wy_v, wy_v), (far_inverse, inverse),
                (far_keys, keys), (far_queries, queries),
                (far_small, small), (far_conv_total, conv_total), (far_proj, proj),
            ],
            sems,
        )
    )
    tokens = proj.shape[0]
    chunks = tokens // GROUP
    first = seq_index() * tokens
    lead = 8
    lane = lax.broadcasted_iota(jnp.int32, (GROUP, LANES), 1)

    def document_before(c):
        return documents_at(starts, jnp.full((1, 1), first + c * GROUP - 1, jnp.int32)).astype(F32)

    def whole_decay(c, h):
        at = pl.ds(pl.multiple_of(c * GROUP, GROUP) + GROUP - 8, 8)
        last = cols[at, NH * heads + h : NH * heads + h + 1][7:8, :]
        return jnp.where(doc[at, 0:1][7:8, :] == document_before(c), jnp.exp(last), 0.0)

    at_end = []
    for h in range(heads):
        state = after[reach - 1][h].astype(F32)
        for r in range(reach - 2, -1, -1):
            state = mm_tn(later[r][h], state) + after[r][h].astype(F32)
        at_end.append(state)
    end(arriving[:5])

    def retreat(step, carry):
        c = chunks - 1 - step
        rows = pl.ds(pl.multiple_of(c * GROUP, GROUP), GROUP)
        new = []
        for h in range(heads):
            low_state = carry[h].astype(BF)
            state_grads[h, c] = low_state
            new.append(
                whole_decay(c, h) * carry[h]
                - mm_tn(step_p[h, c], low_state)
                + mm_tn(query_map[h, c], d_mixed[rows, h * LANES : (h + 1) * LANES])
            )
        return tuple(new)

    lax.fori_loop(0, chunks, retreat, tuple(at_end))
    end(arriving[5:11])

    order_r, order_c = order_pair()
    strict = order_r > order_c
    together = 2
    last_token = lax.broadcasted_iota(jnp.int32, (GROUP, 1), 0) == GROUP - 1

    def chunk_back(step, _):
        for k in range(together):
            c = step * together + k
            rows = pl.ds(pl.multiple_of(c * GROUP, GROUP), GROUP)
            before = document_before(c)
            col_acc = jnp.zeros((GROUP, LANES), F32)
            row_acc = []
            row_beta = []
            for h in range(heads):
                pair, start, to_end = chunk_decays(rows, cols, row, doc, c, h, heads, before)
                beta_row, beta_col = beta_pair(rows, cols, row, c, h)
                key = keys[h, c]
                query = queries[h, c]
                key_f = key.astype(F32)
                query_f = query.astype(F32)
                d_out = d_mixed[rows, h * LANES : (h + 1) * LANES]
                d_state = state_grads[h, c]
                both = state_aug[h, c]
                state = both[:, :LANES].astype(F32) + mm(both[:, LANES:], state_in[h])
                low_state = state.astype(BF)
                fresh = wy_v[h, c].astype(F32) - mm(wy_k[h, c], low_state)
                grams = mm_nt(jnp.concatenate([key, query], axis=0), key)
                pair2 = two(pair)
                system = jnp.where(strict, grams[:LANES] * pair2, 0.0)
                scores = grams[LANES:] * pair
                key_end = two(to_end) * key_f
                key_start = two(start) * key_f
                d_wide = mm_tn(scores, d_out) + mm(key_end, d_state)
                solved = mm_tn(inverse[h, c], beta_col * d_wide)
                d_value[h, c] = solved
                low_fresh = fresh.astype(BF)
                crossed = mm_nt(
                    jnp.concatenate([solved.astype(BF), d_out], axis=0),
                    jnp.concatenate([low_fresh, low_state], axis=0),
                )
                pairs = jnp.where(strict, crossed[:LANES, :LANES], 0.0)
                solved_state = crossed[:LANES, LANES:]
                out_state = crossed[LANES:, LANES:]
                fresh_grad = mm_nt(beta_col * fresh, d_state)
                system_pairs = system * pairs
                decayed = -(system_pairs * beta_row)
                gram_grad = -(pairs * pair2 * beta_row)
                score_grad = crossed[LANES:, :LANES] * beta_row
                query_key = score_grad * pair
                score_decay = score_grad * scores
                stacked = jnp.concatenate([gram_grad, query_key], axis=0).astype(BF)
                direct = mm(stacked, key)
                turned = mm_tn(stacked, jnp.concatenate([key, query], axis=0))
                d_key[h, c] = direct[:LANES] + turned - two(start) * solved_state + two(to_end) * fresh_grad
                d_query[h, c] = direct[LANES:] + start * out_state
                ending = key_end * fresh_grad
                parts = decayed - key_start * solved_state - ending
                parts = parts[:GROUP] + parts[GROUP:] + score_decay + (start * query_f) * out_state
                last_grad = jnp.sum(ending, keepdims=True) + whole_decay(c, h) * jnp.sum(
                    state * d_state.astype(F32), keepdims=True
                )
                decay_col = jnp.sum(parts, axis=1, keepdims=True) + jnp.where(last_token, last_grad, 0.0)
                beta_sum = jnp.sum(d_wide * fresh, axis=1, keepdims=True)
                col_acc = jnp.where(lane == NH * heads + h, decay_col, col_acc)
                for s in range(NH):
                    col_acc = jnp.where(lane == NH * h + s, beta_sum[s * GROUP : (s + 1) * GROUP], col_acc)
                beta_row_sum = jnp.sum(system_pairs, axis=0, keepdims=True)
                row_beta.append(-beta_row_sum)
                row_acc.append(beta_row * beta_row_sum - jnp.sum(score_decay, axis=0, keepdims=True))
            col_grads[rows, :] = col_acc
            row_grads[c] = jnp.concatenate(
                row_acc + row_beta + [jnp.zeros((8 - 2 * heads, LANES), F32)], axis=0
            )
        return 0

    lax.fori_loop(0, chunks // together, chunk_back, 0)

    end(arriving[11:])

    lower_r = lax.broadcasted_iota(jnp.int32, (LANES, LANES), 0)
    lower_c = lax.broadcasted_iota(jnp.int32, (LANES, LANES), 1)
    upper = ((lower_r <= lower_c) & (lower_r // GROUP == lower_c // GROUP)).astype(F32)
    per = LANES // GROUP
    scalar_decay = jnp.zeros((1, LANES), F32)
    scalar_rate = jnp.zeros((1, LANES), F32)
    wide = lax.broadcasted_iota(jnp.int32, (LANES, LANES), 1)
    for block in range(tokens // LANES):
        at = pl.ds(block * LANES, LANES)
        pieces = []
        for part in range(per):
            c = block * per + part
            turned = jnp.concatenate([row_grads[c], jnp.zeros((LANES - 8, LANES), F32)], axis=0).T
            piece = jnp.zeros((GROUP, LANES), F32)
            for h in range(heads):
                decay_col = turned[:GROUP, h : h + 1] + turned[GROUP:, h : h + 1]
                piece = jnp.where(lane == NH * heads + h, decay_col, piece)
                for s in range(NH):
                    beta_col = turned[s * GROUP : (s + 1) * GROUP, heads + h : heads + h + 1]
                    piece = jnp.where(lane == NH * h + s, beta_col, piece)
            pieces.append(piece)
        grads = col_grads[at, :] + jnp.concatenate(pieces, axis=0)
        d_logdec = mm_exact(upper, grads)
        betas, logdec, argument, rate = gate_columns(small[at, :], log_rate, bias, heads)
        d_argument = d_logdec * rate * sigmoid(argument)
        scalar_rate += jnp.sum(d_logdec * logdec, axis=0, keepdims=True)
        scalar_decay += jnp.sum(d_argument, axis=0, keepdims=True)
        d_small[at, :] = jnp.where(
            wide < NH * heads,
            grads * betas * (1.0 - betas),
            jnp.where(wide < NH * heads + heads, d_argument, 0.0),
        ).astype(BF)
    d_scalars[...] = jnp.concatenate([scalar_rate, scalar_decay, jnp.zeros((6, LANES), F32)], axis=0)

    ext[0:lead, :] = halo[16 - lead : 16, :].astype(F32)
    ext[lead:, :] = proj[...].astype(F32)
    width_q = heads * LANES
    width_k = NH * heads * LANES
    width = width_q + 2 * width_k
    taps = conv_q.shape[0]
    d_taps[...] = jnp.zeros(d_taps.shape, F32)
    d_total[tokens:, :] = jnp.zeros((8, width), F32)

    def kernel_of(group):
        if group * LANES < width_q:
            return conv_q, slice(group * LANES, (group + 1) * LANES)
        if group * LANES < width_q + width_k:
            return conv_k, slice(group * LANES - width_q, (group + 1) * LANES - width_q)
        return conv_v, slice(group * LANES - width_q - width_k, (group + 1) * LANES - width_q - width_k)

    def active_back(c, _):
        base = pl.multiple_of(c * GROUP, GROUP)
        rows = pl.ds(base, GROUP)
        position = lax.broadcasted_iota(jnp.int32, (GROUP, LANES), 0) + (first + base)
        document = doc[rows, :]
        kept = [
            (documents_at(starts, position - lag).astype(F32) == document).astype(F32) for lag in range(1, taps)
        ]
        for group in range(width // LANES):
            at = slice(group * LANES, (group + 1) * LANES)
            total = conv_total[rows, at]
            sg = sigmoid(total)
            if group * LANES < width_q + width_k:
                active = total * sg
                scale = lax.rsqrt(jnp.sum(active * active, axis=1, keepdims=True) + EPSILON)
                unit = active * scale
                if group * LANES < width_q:
                    grad = d_query[group, c] * LANES ** (-0.5)
                else:
                    piece = group - width_q // LANES
                    grad = d_key[piece // NH, c, (piece % NH) * GROUP : (piece % NH + 1) * GROUP]
                grad = scale * (grad - unit * jnp.sum(unit * grad, axis=1, keepdims=True))
            else:
                piece = group - (width_q + width_k) // LANES
                grad = d_value[piece // NH, c, (piece % NH) * GROUP : (piece % NH + 1) * GROUP]
            grad = grad * (sg * (1.0 + total * (1.0 - sg)))
            d_total[rows, at] = grad
            window = ext[pl.ds(base, GROUP + lead), at]
            sums = []
            for j in range(taps):
                lag = taps - 1 - j
                term = grad * window[lead - lag : lead - lag + GROUP, :]
                if lag > 0:
                    term = term * kept[lag - 1]
                sums.append(jnp.sum(term, axis=0, keepdims=True))
            d_taps[0:taps, at] += jnp.concatenate(sums, axis=0)
        return 0

    lax.fori_loop(0, chunks, active_back, 0)

    def conv_back(c, _):
        base = pl.multiple_of(c * GROUP, GROUP)
        rows = pl.ds(base, GROUP)
        position = lax.broadcasted_iota(jnp.int32, (GROUP, LANES), 0) + (first + base)
        document = doc[rows, :]
        kept = [
            (documents_at(starts, position + lag).astype(F32) == document).astype(F32) for lag in range(1, taps)
        ]
        for group in range(width // LANES):
            at = slice(group * LANES, (group + 1) * LANES)
            kernel, cut = kernel_of(group)
            window = d_total[pl.ds(base, GROUP + lead), at]
            grad = kernel[taps - 1 : taps, cut] * window[:GROUP]
            for lag in range(1, taps):
                grad += kernel[taps - 1 - lag : taps - lag, cut] * kept[lag - 1] * window[lag : lag + GROUP]
            target = d_v if kernel is conv_v else d_kq
            shift = width_k if kernel is conv_q else 0
            target[rows, cut.start + shift : cut.stop + shift] = grad.astype(BF)
            tail[:, at] = grad[GROUP - 16 :]
        return 0

    lax.fori_loop(0, chunks, conv_back, 0)
    position = lax.broadcasted_iota(jnp.int32, (8, LANES), 0) + (first - 8)
    document = documents_at(starts, position)
    for group in range(width // LANES):
        at = slice(group * LANES, (group + 1) * LANES)
        kernel, cut = kernel_of(group)
        window = jnp.concatenate([jnp.zeros((8, LANES), F32), d_total[0:8, at]], axis=0)
        grad = jnp.zeros((8, LANES), F32)
        for lag in range(1, taps):
            kept = (documents_at(starts, position + lag) == document).astype(F32)
            grad += kernel[taps - 1 - lag : taps - lag, cut] * kept * window[lag : lag + 8]
        d_halo[:, at] = grad


def mixer_back(starts, log_rate, bias, proj, halo, conv_q, conv_k, conv_v, small, saved, state_in, d_mixed, after, later):
    tokens, width = proj.shape
    heads = log_rate.shape[0]
    chunks = tokens // GROUP
    reach = len(after)
    square = (heads, chunks, LANES, LANES)
    shape = jax.ShapeDtypeStruct
    outs = [
        shape((tokens, conv_k.shape[1] + conv_q.shape[1]), BF),
        shape((tokens, conv_v.shape[1]), BF),
        shape((16, width), F32),
        shape((8, width), F32),
        shape((tokens, LANES), BF),
        shape((8, width), F32),
        shape((8, LANES), F32),
    ]
    operands = [starts, log_rate, bias, proj, halo, conv_q, conv_k, conv_v, small, *saved, state_in, d_mixed, *after, *later]
    return pl.pallas_call(
        functools.partial(back_kernel, heads, reach),
        out_shape=outs,
        in_specs=specs(3, pltpu.SMEM) + specs(1, HBM) + specs(4) + specs(13, HBM) + specs(len(operands) - 21),
        out_specs=specs(len(outs)),
        scratch_shapes=[VMEM(a.shape, a.dtype) for a in (proj, small, *saved)]
        + [
            VMEM((tokens + 8, width), F32),
            VMEM(square, BF),
            VMEM((heads, chunks, GROUP, LANES), F32),
            VMEM(square, F32),
            VMEM(square, F32),
            VMEM((tokens, LANES), F32),
            VMEM((chunks, 8, LANES), F32),
            VMEM((tokens + 8, width), F32),
            pltpu.SemaphoreType.DMA((14,)),
        ],
        compiler_params=pltpu.CompilerParams(vmem_limit_bytes=VMEM_LIMIT),
        cost_estimate=pl.CostEstimate(flops=2_000_000_000, bytes_accessed=4_000_000, transcendentals=0),
        name="mixer_back",
    )(*operands)


def call(kernel, name, outs, operands, smem=0, scratch=(), flops=0, limit=SMALL_LIMIT):
    moved = sum(a.size * a.dtype.itemsize for a in operands) + sum(
        math.prod(o.shape) * jnp.dtype(o.dtype).itemsize for o in outs
    )
    return pl.pallas_call(
        kernel,
        out_shape=outs,
        in_specs=specs(smem, pltpu.SMEM) + specs(len(operands) - smem),
        out_specs=specs(len(outs)),
        scratch_shapes=list(scratch),
        compiler_params=pltpu.CompilerParams(vmem_limit_bytes=limit),
        cost_estimate=pl.CostEstimate(flops=flops // EARLY, bytes_accessed=moved // EARLY, transcendentals=0),
        name=name,
    )(*operands)


def shaped(dims, kind):
    return jax.ShapeDtypeStruct(dims, kind)


def half_rows(ref, own):
    half = ref.shape[0] // 2
    low = lax.axis_index("head") % 2
    return pl.ds(pl.multiple_of((low if own else 1 - low) * half, half), half)


def seq_bits():
    at = seq_index()
    z = at // 2 % 4
    low, high = z % 2, z // 2
    return {"x": at % 2, "pair": low ^ high, "cross": high}


PARTNER = {"x": 1, "pair": 2, "cross": 6}
X_FIRST = ("x", "pair", "cross")
V_BACK = ("x", "cross", "pair")
Z_FIRST = ("pair", "cross", "x")


def half_width(ref, own, stage="x"):
    half = ref.shape[1] // 2
    low = seq_bits()[stage]
    return pl.ds(pl.multiple_of((low if own else 1 - low) * half, half), half)


def project_kernel(
    far_x, gain, far_q, far_k, far_v, far_gate, beta_w, decay_w, far_normed, far_projected, far_outgate, far_small, edge,
    x, q_w, k_w, v_w, gate_w, normed, projected, outgate, small, side_w, sems,
):
    arriving = begin(
        copies([(far_x, x), (far_q, q_w), (far_k, k_w), (far_v, v_w), (far_gate, gate_w)], sems)
    )
    gather_side(side_w, beta_w, decay_w)
    end(arriving[:1])
    x_float = x[...].astype(F32)
    low = (x_float * lax.rsqrt(jnp.mean(x_float * x_float, axis=1, keepdims=True) + EPSILON) * gain[...]).astype(BF)
    normed[...] = low
    leaving = begin(copies([(normed, far_normed)], sems, 5))
    last = x.shape[0] - edge.shape[0]
    small[...] = mm_nt(low, side_w[...])
    leaving += begin(copies([(small, far_small)], sems, 6))
    at = 0
    for k, weight in enumerate((q_w, k_w, v_w)):
        end(arriving[1 + k : 2 + k])
        piece = mm(low, weight[...]).astype(BF)
        projected[:, at : at + weight.shape[1]] = piece
        edge[:, at : at + weight.shape[1]] = piece[last:, :]
        at += weight.shape[1]
    edge[:, at:] = low[last:, :]
    leaving += begin(copies([(projected, far_projected)], sems, 7))
    end(arriving[4:])
    outgate[...] = mm(low, gate_w[...])
    leaving += begin(copies([(outgate, far_outgate)], sems, 8))
    end(leaving)


def gather_side(side_w, beta_w, decay_w):
    betas = beta_w.shape[0]
    side_w[...] = jnp.zeros(side_w.shape, F32)
    side_w[0:betas, :] = beta_w[...].astype(F32)
    side_w[betas : betas + decay_w.shape[0], :] = decay_w[...].astype(F32)


def project(x, gain, q_w, k_w, v_w, gate_w, beta_w, decay_w):
    tokens, wide = x.shape
    width = q_w.shape[1] + k_w.shape[1] + v_w.shape[1]
    outs = [
        shaped((tokens, wide), BF), shaped((tokens, width), BF),
        shaped((tokens, gate_w.shape[1]), F32), shaped((tokens, LANES), F32), shaped((16, width + wide), BF),
    ]
    operands = [x, gain.reshape(1, -1), q_w, k_w, v_w, gate_w, beta_w, decay_w]
    moved = 8 * x.size
    return pl.pallas_call(
        project_kernel,
        out_shape=outs,
        in_specs=specs(1, HBM) + specs(1) + specs(4, HBM) + specs(2),
        out_specs=specs(4, HBM) + specs(1),
        scratch_shapes=[VMEM(a.shape, a.dtype) for a in (x, q_w, k_w, v_w, gate_w)]
        + [VMEM(out.shape, out.dtype) for out in outs[:4]]
        + [VMEM((LANES, wide), F32), pltpu.SemaphoreType.DMA((9,))],
        compiler_params=pltpu.CompilerParams(vmem_limit_bytes=VMEM_LIMIT),
        cost_estimate=pl.CostEstimate(flops=8 * tokens * wide * width, bytes_accessed=moved, transcendentals=0),
        name="project",
    )(*operands)


def attend_kernel(heads, reach, out_aug, outgate, o_gain, out_weight, *rest):
    before = rest[:reach]
    mixed, branch, give, keep, state_in = rest[reach:]
    gain = o_gain[...]
    for h in range(heads):
        at = slice(h * LANES, (h + 1) * LANES)
        state = before[reach - 1][0, h].astype(F32)
        for r in range(reach - 2, -1, -1):
            state = mm(before[r][1, h], state) + before[r][0, h].astype(F32)
        state_in[h] = state
        mix = out_aug[h, :, :LANES] + mm(out_aug[h, :, LANES:], state)
        mixed[:, at] = mix
        gate = outgate[:, at]
        normed = mix * lax.rsqrt(jnp.mean(mix * mix, axis=1, keepdims=True) + EPSILON)
        branch[:, at] = (normed * gain * (gate * sigmoid(gate))).astype(BF)
    give[...] = mm(branch[half_rows(branch, False), :], out_weight[...]).astype(BF)
    keep[...] = mm(branch[half_rows(branch, True), :], out_weight[...])


def attend(out_aug, outgate, o_gain, out_weight, before):
    heads, tokens, _ = out_aug.shape
    wide = out_weight.shape[1]
    outs = [
        shaped((tokens, heads * LANES), F32), shaped((tokens, heads * LANES), BF),
        shaped((tokens // 2, wide), BF), shaped((tokens // 2, wide), F32), shaped((heads, LANES, LANES), F32),
    ]
    operands = [out_aug, outgate, o_gain.reshape(1, -1), out_weight, *before]
    return call(
        functools.partial(attend_kernel, heads, len(before)), "attend", outs, operands,
        flops=2 * tokens * wide * heads * LANES,
    )


def enter_kernel(x, mine, other, gain, hidden, normed):
    value = x[half_rows(x, True), :].astype(F32) + mine[...].astype(F32) + other[...].astype(F32)
    hidden[...] = value
    normed[...] = (
        value * lax.rsqrt(jnp.mean(value * value, axis=1, keepdims=True) + EPSILON) * gain[...]
    ).astype(BF)


def enter(x, mine, other, gain):
    outs = [shaped(mine.shape, F32), shaped(mine.shape, BF)]
    return call(enter_kernel, "enter", outs, [x, mine, other, gain.reshape(1, -1)])


def near_units(units, own):
    near = lax.axis_index("near")
    return pl.ds(pl.multiple_of((near if own else 1 - near) * (units // 2), 16), units // 2)


def half_lanes(ref, own):
    half = ref.shape[1] // 2
    low = lax.axis_index("head") % 2
    return pl.ds(pl.multiple_of((low if own else 1 - low) * half, half), half)


def feed_kernel(
    own, other, gate_w, up_w, down_w, out_grad,
    normed, d_give, d_keep, part_give, part_keep, feed_give, feed_keep,
):
    units = gate_w.shape[0]
    half = units // 2
    for mine, source, part, fed in ((False, other, part_give, feed_give), (True, own, part_keep, feed_keep)):
        rows = half_rows(normed, mine)
        lanes = half_lanes(d_give, mine)
        low = source[...]
        normed[rows, :] = low
        part_sum = jnp.zeros(part.shape, F32)
        feed_sum = jnp.zeros(fed.shape, F32)
        for near, out in ((False, d_give), (True, d_keep)):
            cut = near_units(units, near)
            gate = mm_nt(gate_w[cut, :], low)
            up = mm_nt(up_w[cut, :], low)
            d_inner = mm_nt(down_w[cut, :], out_grad[rows, :])
            sg = sigmoid(gate)
            active = gate * sg
            low_inner = (active * up).astype(BF)
            low_gate = (d_inner * up * (sg * (1.0 + gate * (1.0 - sg)))).astype(BF)
            low_up = (d_inner * active).astype(BF)
            out[0:half, lanes] = low_gate
            out[half : 2 * half, lanes] = low_up
            out[2 * half : 3 * half, lanes] = low_inner
            part_sum += mm_tn(low_gate, gate_w[cut, :]) + mm_tn(low_up, up_w[cut, :])
            feed_sum += mm_tn(low_inner, down_w[cut, :])
        part[...] = part_sum.astype(part.dtype)
        fed[...] = feed_sum.astype(fed.dtype)


def feed(own, other, gate_w, up_w, down_w, out_grad):
    tokens, wide = out_grad.shape
    units = gate_w.shape[0]
    half = (tokens // 2, wide)
    outs = [shaped((tokens, wide), BF)] + [shaped((3 * units // 2, tokens), BF)] * 2 + [
        shaped(half, BF), shaped(half, F32), shaped(half, BF), shaped(half, F32),
    ]
    operands = [own, other, gate_w, up_w, down_w, out_grad]
    return call(feed_kernel, "feed", outs, operands, flops=12 * tokens * wide * units)


def leave_kernel(mine, other, hidden, gain, out_grad, d_hidden, low, d_gain):
    grad = mine[...].astype(F32) + other[...].astype(F32)
    value = hidden[...]
    scale = lax.rsqrt(jnp.mean(value * value, axis=1, keepdims=True) + EPSILON)
    unit = value * scale
    d_gain[...] = jnp.sum(grad * unit, axis=0, keepdims=True)
    d_unit = grad * gain[...]
    total = out_grad[half_rows(out_grad, True), :].astype(F32) + scale * (
        d_unit - unit * jnp.mean(d_unit * unit, axis=1, keepdims=True)
    )
    d_hidden[...] = total
    low[...] = total.astype(BF)


def leave(mine, other, hidden, gain, out_grad):
    outs = [shaped(mine.shape, F32), shaped(mine.shape, BF), shaped((1, mine.shape[1]), F32)]
    return call(leave_kernel, "leave", outs, [mine, other, hidden, gain.reshape(1, -1), out_grad])


def finish_kernel(mine, other, x, gain, d_hidden, low, d_gain):
    grad = mine[...].astype(F32) + other[...].astype(F32)
    value = x[half_rows(x, True), :].astype(F32)
    scale = lax.rsqrt(jnp.mean(value * value, axis=1, keepdims=True) + EPSILON)
    unit = value * scale
    d_gain[...] = jnp.sum(grad * unit, axis=0, keepdims=True)
    d_unit = grad * gain[...]
    low[...] = (
        d_hidden[...] + scale * (d_unit - unit * jnp.mean(d_unit * unit, axis=1, keepdims=True))
    ).astype(BF)


def finish(mine, other, x, gain, d_hidden):
    outs = [shaped(mine.shape, BF), shaped((1, mine.shape[1]), F32)]
    return call(finish_kernel, "finish", outs, [mine, other, x, gain.reshape(1, -1), d_hidden])


def attend_back_kernel(
    heads, own, other, out_weight, mixed, outgate, o_gain, out_aug,
    grad, d_mixed, d_outgate, d_gain, carry,
):
    gain = o_gain[...]
    gain_sum = jnp.zeros((1, LANES), F32)
    carries = [jnp.zeros((LANES, LANES), F32)] * heads
    for mine, source in ((True, own), (False, other)):
        rows = half_rows(grad, mine)
        low = source[...]
        grad[rows, :] = low
        d_branch = mm_nt(low, out_weight[...])
        for h in range(heads):
            at = slice(h * LANES, (h + 1) * LANES)
            mix = mixed[rows, at]
            gate = outgate[rows, at]
            grad_h = d_branch[:, at]
            scale = lax.rsqrt(jnp.mean(mix * mix, axis=1, keepdims=True) + EPSILON)
            normed = mix * scale
            sg = sigmoid(gate)
            through = grad_h * (gate * sg)
            gain_sum += jnp.sum(through * normed, axis=0, keepdims=True)
            d_normed = through * gain
            d_mix = (scale * (d_normed - normed * jnp.mean(d_normed * normed, axis=1, keepdims=True))).astype(BF)
            d_mixed[rows, at] = d_mix
            d_outgate[rows, at] = (grad_h * normed * gain * (sg * (1.0 + gate * (1.0 - sg)))).astype(BF)
            carries[h] += mm_tn(out_aug[h, rows, LANES:], d_mix)
    for h in range(heads):
        carry[h] = carries[h].astype(carry.dtype)
    d_gain[...] = gain_sum


def attend_back(own, other, out_weight, mixed, outgate, o_gain, out_aug):
    heads, tokens, _ = out_aug.shape
    wide = out_weight.shape[1]
    outs = [
        shaped((tokens, wide), BF), shaped((tokens, heads * LANES), BF), shaped((tokens, heads * LANES), BF),
        shaped((1, LANES), F32), shaped((heads, LANES, LANES), BF),
    ]
    operands = [own, other, out_weight, mixed, outgate, o_gain.reshape(1, -1), out_aug]
    return call(
        functools.partial(attend_back_kernel, heads), "attend_back", outs, operands,
        flops=2 * tokens * wide * heads * LANES,
    )


def store_rows_cut(part, at, piece):
    quarters = part.shape[0]
    rows = piece.shape[0] // quarters
    for q in range(quarters):
        for i in range(piece.shape[1] // LANES):
            part[q, at + i * rows : at + (i + 1) * rows, :] = piece[
                q * rows : (q + 1) * rows, i * LANES : (i + 1) * LANES
            ].astype(BF)


def store_cols_cut(part, at, piece):
    for q in range(part.shape[0]):
        part[q, at : at + piece.shape[0], :] = piece[:, q * LANES : (q + 1) * LANES].astype(BF)


def feed_weights_kernel(
    d_own, normed, out_grad, d_near, normed_mine, normed_other, grad_mine, grad_other, grads
):
    half = d_own.shape[0] // 3
    for k in range(3):
        right, mine, other = (out_grad, grad_mine, grad_other) if k == 2 else (normed, normed_mine, normed_other)
        rows = slice(k * half, (k + 1) * half)
        total = mm(d_own[rows, :], right[...])
        total += mm(d_near[rows, half_lanes(d_near, True)], mine[...])
        total += mm(d_near[rows, half_lanes(d_near, False)], other[...])
        grads[rows, :] = total.astype(BF)


def feed_weights(d_own, normed, out_grad, d_near, normed_mine, normed_other, grad_mine, grad_other):
    tokens, wide = normed.shape
    rows = d_own.shape[0]
    operands = [d_own, normed, out_grad, d_near, normed_mine, normed_other, grad_mine, grad_other]
    (grads,) = call(
        feed_weights_kernel, "feed_weights", [shaped((rows, wide), BF)], operands, flops=4 * tokens * wide * rows
    )
    return grads


def feed_out_kernel(mine, other, *outs):
    units = outs[0].shape[0]
    half = units // 2
    for own, ref in ((True, mine), (False, other)):
        for k, out in enumerate(outs):
            out[near_units(units, own), :] = ref[k * half : (k + 1) * half, :].astype(F32)


def gate_weights_kernel(normed, d_outgate, branch, grad, give, keep):
    for own, part in ((False, give), (True, keep)):
        store_rows_cut(part, 0, mm_tn(normed[:, half_width(normed, own)], d_outgate[...]))
        store_cols_cut(part, d_outgate.shape[1], mm_tn(branch[...], grad[:, half_width(grad, own)]))


def gate_weights(normed, d_outgate, branch, grad):
    rows = d_outgate.shape[1] + branch.shape[1]
    outs = [shaped((4, rows, LANES), BF)] * 2
    operands = [normed, d_outgate, branch, grad]
    return call(
        gate_weights_kernel, "gate_weights", outs, operands, flops=2 * normed.shape[0] * normed.shape[1] * rows
    )


def mix_weights_kernel(first, normed, halo, d_cols, d_halo, *rest):
    *side, give, keep = rest
    low_halo = d_halo[...].astype(BF)
    for own, part in ((False, give), (True, keep)):
        at = half_width(normed, own, first)
        left = normed[:, at]
        total = mm_tn(left, d_cols[...]) + mm_tn(halo[halo.shape[0] - d_halo.shape[0] :, at], low_halo)
        store_rows_cut(part, 0, total)
        if side:
            store_cols_cut(part, d_cols.shape[1], mm_tn(side[0][...], left)[:16])


def mix_weights(first, normed, halo, d_cols, d_halo, *side):
    tokens, wide = normed.shape
    rows = d_cols.shape[1] + 16 * len(side)
    operands = [normed, halo, d_cols, d_halo, *side]
    return call(
        functools.partial(mix_weights_kernel, first), "mix_weights", [shaped((4, rows, LANES), BF)] * 2,
        operands, flops=2 * tokens * wide * rows,
    )


def unproject_kernel(
    d_kq, d_v, tail, following, d_outgate, d_small, q_w, k_w, v_w, gate_w, beta_w, decay_w, give, keep,
    joined, side_w,
):
    tokens, width = joined.shape
    wide_q, wide_k = q_w.shape[1], k_w.shape[1]
    joined[:, 0:wide_q] = d_kq[:, wide_k:]
    joined[:, wide_q : wide_q + wide_k] = d_kq[:, :wide_k]
    joined[:, wide_q + wide_k :] = d_v[...]
    joined[tokens - 16 :, :] = jnp.concatenate([tail[0:8, :], tail[8:16, :] + following[...]], axis=0).astype(BF)
    gather_side(side_w, beta_w, decay_w)
    for own, part in ((False, give), (True, keep)):
        rows = half_rows(joined, own)
        total = mm_nt(d_outgate[rows, :], gate_w[...]) + mm(d_small[rows, :], side_w[...])
        at = 0
        for weight in (q_w, k_w, v_w):
            total += mm_nt(joined[rows, at : at + weight.shape[1]], weight[...])
            at += weight.shape[1]
        part[...] = total.astype(part.dtype)


def unproject(d_kq, d_v, tail, following, d_outgate, d_small, q_w, k_w, v_w, gate_w, beta_w, decay_w):
    tokens = d_v.shape[0]
    wide, width = q_w.shape[0], tail.shape[1]
    half = (tokens // 2, wide)
    operands = [d_kq, d_v, tail, following, d_outgate, d_small, q_w, k_w, v_w, gate_w, beta_w, decay_w]
    return call(
        unproject_kernel, "unproject", [shaped(half, BF), shaped(half, F32)], operands,
        scratch=[VMEM((tokens, width), BF), VMEM((LANES, wide), F32)],
        flops=2 * tokens * (width + 384) * wide,
    )


def fold_kernel(stage, keep, got, *outs):
    if len(outs) == 1:
        outs[0][...] = (keep[...].astype(F32) + got[...].astype(F32)).astype(BF)
        return
    mine = seq_bits()[stage]
    half = keep.shape[0] // 2
    for own, out in ((False, outs[0]), (True, outs[1])):
        at = (mine if own else 1 - mine) * half
        for k in range(half):
            out[k] = (keep[at + k].astype(F32) + got[at + k].astype(F32)).astype(BF)


def fold(stage, keep, got):
    count, rows, lanes = keep.shape
    outs = [shaped((count // 2, rows, lanes), BF)] * 2 if stage else [shaped(keep.shape, BF)]
    return call(functools.partial(fold_kernel, stage), "fold", outs, [keep, got])


class Line:
    def __init__(self):
        self.last = None

    def after(self, *arrays):
        if self.last is None:
            return arrays
        return lax.optimization_barrier((*arrays, self.last))[:-1]

    def step(self, function, *arrays):
        result = function(*self.after(*arrays))
        self.last = jax.tree.leaves(result)[0]
        return result


class Sum:
    def __init__(self, line, order, give, keep, back=None):
        self.line, self.order, self.keep, self.at = line, order, keep, 0
        self.back = order[::-1] if back is None else back
        self.got = swapped(give, SEQ, PARTNER[order[0]])

    def next(self):
        stages = len(self.order)
        self.at += 1
        if self.at < stages:
            give, self.keep = self.line.step(
                functools.partial(fold, self.order[self.at]), self.keep, self.got
            )
            self.got = swapped(give, SEQ, PARTNER[self.order[self.at]])
            return
        if self.at == stages:
            (mine,) = self.line.step(functools.partial(fold, None), self.keep, self.got)
            bit = 8
            while bit < seq_size():
                mine = (mine.astype(F32) + swapped(mine, SEQ, bit).astype(F32)).astype(BF)
                bit *= 2
        else:
            mine = self.line.step(lambda *parts: jnp.concatenate(parts, axis=0), self.keep, self.got)
        self.keep = mine
        self.got = swapped(mine, SEQ, PARTNER[self.back[self.at - stages]])

    def finish(self, kernel, name, outs):
        return self.line.step(
            lambda *parts: call(functools.partial(kernel, (self.order, self.back)), name, outs, list(parts)), self.keep, self.got
        )


def blocks_of(orders, mine, other):
    order, back = orders
    bits = seq_bits()
    for last, ref in ((0, mine), (1, other)):
        for slot in range(4):
            flips = dict(zip(back, (slot % 2, slot // 2, last)))
            first, second, third = (bits[stage] ^ flips[stage] for stage in order)
            yield 4 * first + 2 * second + third, ref, slot


def at_block(index):
    return pl.ds(pl.multiple_of(index * LANES, LANES), LANES)


def load_rows_cut(ref, slot, at, count):
    return [ref[slot, at + i * LANES : at + (i + 1) * LANES, :].astype(F32) for i in range(count)]


def gate_out_kernel(order, mine, other, outgate, out):
    for index, ref, slot in blocks_of(order, mine, other):
        width = outgate.shape[1]
        for i, piece in enumerate(load_rows_cut(ref, slot, 0, width // LANES)):
            outgate[at_block(index), i * LANES : (i + 1) * LANES] = piece
        out[:, at_block(index)] = ref[slot, width : width + out.shape[0], :].astype(F32)


def mix_out_kernel(side, order, mine, other, *outs):
    wide = outs if not side else outs[:-2]
    for index, ref, slot in blocks_of(order, mine, other):
        at = 0
        for out in wide:
            for i, piece in enumerate(load_rows_cut(ref, slot, at, out.shape[1] // LANES)):
                out[at_block(index), i * LANES : (i + 1) * LANES] = piece
            at += out.shape[1]
        if side:
            pieces = ref[slot, at : at + 16, :].astype(F32)
            at = 0
            for part in outs[-2:]:
                part[:, at_block(index)] = pieces[at : at + part.shape[0], :]
                at += part.shape[0]


def shifted(value, axis, steps):
    count = seq_size()
    leading, last = max(0, -steps), min(count, count - steps)
    return lax.ppermute(value, axis, [(source, source + steps) for source in range(leading, last)])


def swapped(value, axis, bit):
    return lax.ppermute(value, axis, [(s, s ^ bit) for s in range(seq_size() if axis == SEQ else lax.axis_size(axis))])


def head_sum(give, keep):
    total = keep + swapped(give, "head", 1).astype(F32)
    mine = total.astype(BF)
    other = swapped(mine, "head", 2)
    bit = 4
    while bit < lax.axis_size("head"):
        mine = (mine.astype(F32) + other.astype(F32)).astype(BF)
        other = swapped(mine, "head", bit)
        bit *= 2
    return mine, other


def both_halves(mine):
    low = lax.axis_index("head") % 2
    other = swapped(mine, "head", 1)
    return jnp.concatenate([jnp.where(low == 0, mine, other), jnp.where(low == 0, other, mine)], axis=0)


def reach_of(tokens, count):
    whole = tokens * count
    longest = whole // 4 + 2 * (whole // 64 - 1)
    return max(1, min(count - 1, -(-(longest - 1) // tokens)))


def local(
    block_in, seq_start, attn_gain, q_weight, k_weight, v_weight, conv_q, conv_k, conv_v,
    beta_weight, decay_weight, a_log, dt_bias, outgate_weight, o_gain, out_weight,
    mlp_gain, gate_weight, up_weight, down_weight, out_grad,
):
    tokens = block_in.shape[0]
    heads = a_log.shape[0]
    width_q = q_weight.shape[1]
    width_k = k_weight.shape[1]
    width = width_q + 2 * width_k
    betas = beta_weight.shape[1]
    reach = reach_of(tokens, seq_size())
    wide = block_in.shape[1]
    units = gate_weight.shape[1]
    beta_rows, decay_rows = beta_weight.T, decay_weight.T
    core = lax.axis_index("head") % 2
    grad_mine = swapped(lax.dynamic_slice_in_dim(out_grad, core * (tokens // 2), tokens // 2, 0), SEQ, 1)
    normed, projected, outgate, small, edge = project(
        block_in, attn_gain, q_weight, k_weight, v_weight, outgate_weight, beta_rows, decay_rows
    )
    halo = shifted(edge, SEQ, 1)
    halo, normed_halo = halo[:, :width], halo[:, width:]
    mixer_args = (seq_start, a_log, dt_bias, projected, halo, conv_q, conv_k, conv_v, small)
    prepared = mixer_prep(*mixer_args)
    out_aug, saved, final_state, final_map = prepared[0], prepared[1:13], prepared[13], prepared[14]
    final_state, grad_mine = lax.optimization_barrier((final_state, grad_mine))
    grad_other = swapped(grad_mine, "head", 1)
    pair = jnp.stack([final_state, final_map])
    before = [shifted(pair, SEQ, r) for r in range(1, reach)] + [shifted(final_state[None], SEQ, reach)]
    later = [shifted(final_map, SEQ, -r) for r in range(1, reach)]
    mixed, branch, give, keep, state_in = attend(out_aug, outgate, o_gain, out_weight, before)
    hidden, normed_own = enter(block_in, *head_sum(give, keep), mlp_gain)
    near_mine = swapped(normed_own, SEQ, 1)
    normed_mlp, d_give, d_keep, part_give, part_keep, feed_give, feed_keep = feed(
        normed_own, swapped(normed_own, "head", 1), gate_weight.T, up_weight.T, down_weight, out_grad
    )
    line = Line()
    part_mine, part_other = head_sum(part_give, part_keep)
    line.last = part_mine
    d_give, near_mine = lax.optimization_barrier((d_give, near_mine))
    d_near = swapped(d_give, SEQ, 1)
    near_other = swapped(near_mine, "head", 1)
    d_hidden, attention_own, grad_mlp_gain = line.step(leave, part_mine, part_other, hidden, mlp_gain, out_grad)
    attention_gradient, grad_mixed, grad_outgate, grad_o_part, carry = line.step(
        attend_back, attention_own, swapped(attention_own, "head", 1), out_weight, mixed, outgate, o_gain, out_aug
    )
    after = [shifted(carry, SEQ, -r) for r in range(1, reach + 1)]
    feed_grads = line.step(
        feed_weights, d_keep, normed_mlp, out_grad, d_near, near_mine, near_other, grad_mine, grad_other
    )
    feed_sums = lax.psum(feed_grads, "far")
    feed_near = swapped(feed_sums, SEQ, 1)
    sum_out = Sum(line, X_FIRST, *line.step(gate_weights, normed, grad_outgate, branch, attention_gradient))
    feed_mine, feed_other = head_sum(feed_give, feed_keep)
    output = both_halves((hidden + feed_mine.astype(F32) + feed_other.astype(F32)).astype(BF))
    d_kq, d_v, tail, d_halo, grad_small, grad_taps, grad_scalars = line.step(
        lambda d_mixed: mixer_back(*mixer_args, saved, state_in, d_mixed, after, later), grad_mixed
    )
    following = shifted(d_halo, SEQ, -1)
    cut_q, cut_k, cut_v = slice(0, width_q), slice(width_q, width_q + width_k), slice(width_q + width_k, width)
    halo_kq = jnp.concatenate([d_halo[:, cut_k], d_halo[:, cut_q]], axis=1)
    sum_kq = Sum(
        line, X_FIRST, *line.step(functools.partial(mix_weights, X_FIRST[0]), normed, normed_halo, d_kq, halo_kq)
    )
    sum_v = Sum(
        line, X_FIRST,
        *line.step(functools.partial(mix_weights, X_FIRST[0]), normed, normed_halo, d_v, d_halo[:, cut_v], grad_small),
        back=V_BACK,
    )
    taps = conv_q.shape[0]

    def padded(*rows):
        joined = jnp.concatenate(rows, axis=1)
        return jnp.pad(joined, ((0, 0), (0, width - joined.shape[1])))

    for part in (sum_kq, sum_out, sum_v):
        part.next()
    mine, other = head_sum(
        *line.step(
            unproject, d_kq, d_v, tail, following, grad_outgate, grad_small,
            q_weight, k_weight, v_weight, outgate_weight, beta_rows, decay_rows,
        )
    )
    for part in (sum_kq, sum_out, sum_v):
        part.next()
    line.last = feed_sums
    input_own, grad_attn_gain = line.step(finish, mine, other, block_in, attn_gain, d_hidden)
    grad_input = both_halves(input_own)
    small_sums = jnp.concatenate(
        [
            grad_taps[:taps], padded(grad_scalars[0:1], grad_scalars[1:2]),
            padded(grad_attn_gain), padded(grad_mlp_gain), padded(grad_o_part),
        ],
        axis=0,
    )
    bits = [1 << k for k in range(1, seq_size().bit_length() - 1)] + [1]
    small_got = swapped(small_sums, SEQ, bits[0])
    rounds = 0
    while rounds < max(3, len(bits)):
        if rounds == 2:
            line.last = feed_near
        for part in (sum_kq, sum_out, sum_v) if rounds < 3 else ():
            part.next()
        rounds += 1
        if rounds <= len(bits):
            small_sums = line.step(jnp.add, small_sums, small_got)
        if rounds < len(bits):
            small_got = swapped(small_sums, SEQ, bits[rounds])
    gains = small_sums[taps + 1 : taps + 4]
    gains = gains + swapped(gains, "head", 1)
    grad_o_gain = gains[2:3, :LANES]
    bit = 2
    while bit < lax.axis_size("head"):
        grad_o_gain = grad_o_gain + swapped(grad_o_gain, "head", bit)
        bit *= 2
    grad_outgate_w, grad_out_w = sum_out.finish(
        gate_out_kernel, "gate_out", [shaped((wide, width_q), F32), shaped((width_q, wide), F32)]
    )
    grad_v_w, grad_beta_w, grad_decay_w = sum_v.finish(
        functools.partial(mix_out_kernel, True), "mix_out",
        [shaped((wide, width_k), F32), shaped((betas, wide), F32), shaped((heads, wide), F32)],
    )
    grad_k_w, grad_q_w = sum_kq.finish(
        functools.partial(mix_out_kernel, False), "mix_out",
        [shaped((wide, width_k), F32), shaped((wide, width_q), F32)],
    )
    grad_gate_w, grad_up_w, grad_down_w = call(
        feed_out_kernel, "feed_out", [shaped((units, wide), F32)] * 3, [feed_sums, feed_near]
    )
    rate, shift = small_sums[taps, betas : betas + heads], small_sums[taps, LANES + betas : LANES + betas + heads]
    return (
        output, grad_input, gains[0, :wide], grad_q_w, grad_k_w, grad_v_w,
        small_sums[:taps, cut_q], small_sums[:taps, cut_k], small_sums[:taps, cut_v],
        grad_beta_w.T, grad_decay_w.T, rate, shift, grad_outgate_w, grad_o_gain[0], grad_out_w, gains[1, :wide],
        grad_gate_w.T, grad_up_w.T, grad_down_w,
    )


def solution(mesh):
    placed = (
        P(SEQ, None), P(), P(), P(None, "head"), P(None, "head"), P(None, "head"), P(None, "head"),
        P(None, "head"), P(None, "head"), P(None, "head"), P(None, "head"), P("head"), P("head"),
        P(None, "head"), P(), P("head", None), P(), P(None, "head"), P(None, "head"), P("head", None),
        P(SEQ, None),
    )
    given = (
        P(SEQ, None), P(SEQ, None), P(), P(None, "head"), P(None, "head"), P(None, "head"),
        P(None, "head"), P(None, "head"), P(None, "head"), P(None, "head"), P(None, "head"), P("head"),
        P("head"), P(None, "head"), P(), P("head", None), P(), P(None, "head"), P(None, "head"),
        P("head", None),
    )
    seq, head = mesh.devices.shape
    mesh = jax.sharding.Mesh(mesh.devices.reshape(seq // 2, 2, head), ("far", "near", "head"))
    return jax.shard_map(local, mesh=mesh, in_specs=placed, out_specs=given, check_vma=False)
```
